32 devices in a mesh: ctx: 8 (over z, y), tp: 4 (over x, core).
Axes of the slice: x: 2, y: 2, z: 4, core: 2. Of those that a mesh axis runs over, the one named last changes fastest.
Arguments:
- values_in: bfloat16 [2048, 8192], P('ctx', 'tp'), may hold values from -6 to 6
- gate_in: bfloat16 [2048, 8192], P('ctx', 'tp'), may hold values from -6 to 6
- keys_in: bfloat16 [2048, 1024], P('ctx', 'tp'), may hold values from -3 to 3
- queries_in: bfloat16 [2048, 1024], P('ctx', 'tp'), may hold values from -3 to 3
- step_in: bfloat16 [2048, 128], P('ctx', 'tp'), may hold values from -4 to 4
- block_order: int32 [32], replicated, may hold values from 0 to 31, as said below
- doc_lengths: int32 [16], replicated, may hold values from 1 to 1024, 2048 in all
- conv_values: float32 [4, 8192], P(None, 'tp'), may hold values from -3 to 3
- conv_keys: float32 [4, 1024], P(None, 'tp'), may hold values from -3 to 3
- conv_queries: float32 [4, 1024], P(None, 'tp'), may hold values from -3 to 3
- decay_log: float32 [128], P('tp'), may hold values from -7 to 0, as said below
- step_bias: float32 [128], P('tp'), may hold values from -9 to -2, as said below
- skip_gain: float32 [128], P('tp'), may hold values from 0.5 to 2
- norm_gain: float32 [8192], P('tp'), may hold values from 0.25 to 1.75
- out_weight: bfloat16 [8192, 4096], P('tp'), may hold values from -0.0625 to 0.0625
Outputs:
- layer_out: bfloat16 [2048, 4096], P(('ctx', 'tp'))
The draws below stay inside these ranges and needn't reach their ends.
Inputs may be any that keep to these rules, and one draw needn't show every extreme that they name: `block_order`: loaded block j sits on loader j // 4; sequence block q belongs to owner q // 4; every block appears once; the 4 blocks of each loader belong to 4 different owners. `doc_lengths`: document lengths in sequence order; they sum to 2048 and the longest is exactly 1024. `decay_log`: logarithm of each head's decay coefficient. `step_bias`: bias added to each head's time-step pre-activation.
All inputs are finite; a program needn't handle non-finite values.
Results may differ from the reference program's by a relative error of at most 0.02.
Values may be sent and summed in bfloat16 or wider, within the bound.
No kernel may reach another device: no remote copies, remote signals or barrier semaphores. Data moves between devices by JAX's collectives and lax.ppermute only.
A program may use at most 128 MiB of HBM per device.

```python
import math
import jax
import jax.numpy as jnp
import numpy as np
from jax import lax

HEADS = 128
HEAD_DIM = 64
STATE = 128
GROUPS = 8
CONV = 4
OUTW = 4096
SPAN = 256
BLK = 64
DOCS = 16
TOKENS = 2048
NBLK = 32
BLK_DEV = 4
CAP = 1
N_CTX = 8
N_TP = 4


def draw_block_order(key, part):
    loaders = N_CTX
    per_dev = BLK_DEV
    capacity = CAP
    subkeys = jax.random.split(jax.random.fold_in(key, 3), 5)
    spare = jax.random.permutation(subkeys[0], (loaders - 1) * capacity).astype(jnp.int32)
    distances = jnp.concatenate([jnp.zeros((capacity,), jnp.int32), 1 + spare[:per_dev - capacity] % (loaders - 1)])
    loader_ids = jnp.arange(loaders, dtype=jnp.int32)
    owner_linear = (loader_ids[:, None] + distances[None, :]) % loaders
    loader_shuffle = jax.random.permutation(subkeys[1], loaders).astype(jnp.int32)
    owner_shuffle = jax.random.permutation(subkeys[2], loaders).astype(jnp.int32)
    owners = owner_shuffle[owner_linear].reshape(-1)
    scores = jax.random.permutation(subkeys[3], loaders * per_dev).astype(jnp.int32)
    ranked_ahead = (owners[None, :] == owners[:, None]) & (scores[None, :] < scores[:, None])
    slot_rank = jnp.sum(ranked_ahead.astype(jnp.int32), axis=1, dtype=jnp.int32)
    sequence_block = (owners * per_dev + slot_rank).reshape(loaders, per_dev)
    shuffle_scores = jax.random.permutation(subkeys[4], loaders * per_dev).astype(jnp.int32).reshape(loaders, per_dev)
    local_order = jnp.argsort(shuffle_scores, axis=1, stable=True)
    arranged = jnp.take_along_axis(sequence_block, local_order, axis=1)
    placed = jnp.zeros((loaders, per_dev), jnp.int32).at[loader_shuffle].set(arranged)
    return placed.reshape(-1)


def head_table(key):
    base = jax.random.fold_in(key, 11)
    pick_key, fast_key, slow_key, jitter_key = jax.random.split(base, 4)
    fast_heads = jax.random.randint(pick_key, (HEADS,), 0, 8) < 4
    fast_log = jax.random.uniform(fast_key, (HEADS,), jnp.float32, math.log(30.0), math.log(50.0))
    slow_log = jax.random.uniform(slow_key, (HEADS,), jnp.float32, math.log(TOKENS / 2.0), math.log(TOKENS * 4.0))
    memory_log = jnp.where(fast_heads, fast_log, slow_log)
    jitter = jax.random.uniform(jitter_key, (HEADS,), jnp.float32, -0.7, 0.7)
    step_log = math.log(0.5) - 0.5 * memory_log + jitter
    return (memory_log, step_log)


def draw_decay_log(key, part):
    memory_log, step_log = head_table(key)
    return (-memory_log - step_log).astype(jnp.float32)


def draw_step_bias(key, part):
    memory_log, step_log = head_table(key)
    return (step_log - 0.5).astype(jnp.float32)


def block_scale(own_key, shape, cuts, low, top_value):
    def one(dim, blocks):
        draws = jax.random.uniform(jax.random.fold_in(jax.random.fold_in(own_key, 6), dim), (blocks,), jnp.float32, low / len(cuts), top_value / len(cuts))
        return jnp.repeat(jnp.exp(draws), shape[dim] // blocks).reshape((-1,) + (1,) * (len(shape) - dim - 1))

    level = one(*cuts[0])
    for cut in cuts[1:]:
        level = level * one(*cut)
    return level


def profile(number_of, total, reach, lean):
    loads = [(1 << 20) // math.isqrt(rank ** lean) + 1 for rank in range(2, number_of + 1)]
    surplus, given = total - reach - (number_of - 1), [1] * (number_of - 1)
    while surplus > 0:
        movable = [i for i in range(number_of - 1) if given[i] < reach]
        pool, budget = sum([loads[i] for i in movable]), surplus
        for i in movable:
            addition = min(reach - given[i], max(1, budget * loads[i] // pool), surplus)
            given[i] = given[i] + addition
            surplus = surplus - addition
    return np.array([reach] + given)


def ragged(rng, number_of, total, limit, lean):
    if number_of == 2:
        one = jax.random.randint(rng, (), max(1, total - limit), min(limit, total - 1) + 1)
        return jnp.stack([one, total - one])
    tallies = jnp.asarray(profile(number_of, total, limit, lean), jnp.int32)
    twos = (number_of - 1) // 2
    giver, receiver = tallies[1:1 + 2 * twos:2], tallies[2:2 + 2 * twos:2]
    slack = jnp.minimum(giver - 1, limit - receiver)
    passed = jax.random.randint(jax.random.fold_in(rng, 1), (twos,), 0, 1 << 20) % (slack + 1)
    tallies = tallies.at[1:1 + 2 * twos:2].set(giver - passed).at[2:2 + 2 * twos:2].set(receiver + passed)
    return tallies[jax.random.permutation(jax.random.fold_in(rng, 2), number_of)]


def noise(rng, dims, deviation, limit, cuts=(), kind=jnp.bfloat16):
    entries = jax.random.normal(rng, dims, jnp.float32) * deviation
    if len(cuts) > 0:
        entries = block_scale(rng, dims, cuts, -0.22, 0.18) * entries
    return jnp.clip(entries, min=-limit, max=limit).astype(kind)


def setup_inputs(seed: int = 0) -> dict:
    splits = jax.random.split(jax.random.key(seed), 16)
    values_in = noise(splits[0], (TOKENS, HEADS * HEAD_DIM), 1.0, 6.0, ((0, 8), (1, 4)))
    gate_in = noise(splits[1], (TOKENS, HEADS * HEAD_DIM), 1.0, 6.0, ((0, 8), (1, 4)))
    keys_in = noise(splits[2], (TOKENS, GROUPS * STATE), 0.5, 3.0, ((0, 8), (1, 4)))
    queries_in = noise(splits[3], (TOKENS, GROUPS * STATE), 0.5, 3.0, ((0, 8), (1, 4)))
    step_in = noise(splits[4], (TOKENS, HEADS), 1.0, 4.0, ((0, 8), (1, 4)))
    block_order = draw_block_order(jax.random.fold_in(splits[15], 71), 0)
    doc_lengths = ragged(splits[6], DOCS, TOKENS, TOKENS // 2, 2).astype(jnp.int32)
    conv_values = noise(splits[7], (CONV, HEADS * HEAD_DIM), 0.5, 3.0, ((1, 4),), jnp.float32)
    conv_keys = noise(splits[8], (CONV, GROUPS * STATE), 0.5, 3.0, ((1, 4),), jnp.float32)
    conv_queries = noise(splits[9], (CONV, GROUPS * STATE), 0.5, 3.0, ((1, 4),), jnp.float32)
    decay_log = draw_decay_log(jax.random.fold_in(splits[15], 71), 0)
    step_bias = draw_step_bias(jax.random.fold_in(splits[15], 71), 0)
    skip_gain = jnp.clip(jnp.exp(math.log(2.0) - 1.3862944 * jax.random.uniform(splits[12], (HEADS,), jnp.float32) ** block_scale(splits[12], (HEADS,), ((0, 4),), -0.2, 0.2)), 0.5, 2.0)
    norm_gain = jnp.clip(1.0 + 0.15 * jax.random.normal(splits[13], (HEADS * HEAD_DIM,), jnp.float32), 0.25, 1.75)
    out_weight = noise(splits[14], (HEADS * HEAD_DIM, OUTW), (HEADS * HEAD_DIM) ** -0.5, 0.0625, ((0, 4),))
    return {"values_in": values_in, "gate_in": gate_in, "keys_in": keys_in, "queries_in": queries_in, "step_in": step_in, "block_order": block_order, "doc_lengths": doc_lengths, "conv_values": conv_values, "conv_keys": conv_keys, "conv_queries": conv_queries, "decay_log": decay_log, "step_bias": step_bias, "skip_gain": skip_gain, "norm_gain": norm_gain, "out_weight": out_weight}


def document_index(positions, doc_lengths):
    offsets = jnp.cumsum(doc_lengths) - doc_lengths
    below_start = offsets[None, :] <= positions[:, None]
    documents = lax.optimization_barrier(jnp.sum(below_start.astype(jnp.int32), axis=1, dtype=jnp.int32)) - 1
    openings = jnp.any(offsets[None, :] == positions[:, None], axis=1).astype(jnp.int32)
    return (documents, openings)

def causal_conv(extended, weight, doc_ext):
    tap_count = weight.shape[0]
    row_count = extended.shape[0] - tap_count + 1
    current = doc_ext[tap_count - 1:]
    accumulated = jnp.zeros((row_count, extended.shape[1]), jnp.float32)
    for tap_index in range(tap_count):
        keep_rows = (doc_ext[tap_index:tap_index + row_count] == current)[:, None]
        shifted = extended[tap_index:tap_index + row_count].astype(jnp.float32) * weight[tap_index]
        accumulated = accumulated + jnp.where(keep_rows, shifted, 0.0)
    return lax.optimization_barrier(jax.nn.silu(accumulated).astype(jnp.bfloat16))

def span_outputs(value_rows, step_rows, key_rows, query_rows, decay_sums, documents):
    row_count = value_rows.shape[0]
    per_group = value_rows.shape[1] // key_rows.shape[1]
    row_ids = jnp.arange(row_count, dtype=jnp.int32)
    keep_mask = (documents[:, None] == documents[None, :]) & (row_ids[None, :] <= row_ids[:, None])
    differences = decay_sums[:, :, None] - decay_sums[:, None, :]
    decays = jnp.where(keep_mask[None], jnp.exp(jnp.minimum(differences, 0.0)), 0.0)
    inner_products = jnp.einsum('ign,jgn->gij', query_rows.astype(jnp.float32), key_rows.astype(jnp.float32), precision=lax.Precision.HIGHEST)
    weighted = (decays * jnp.repeat(inner_products, per_group, axis=0) * step_rows.T[:, None, :]).astype(jnp.bfloat16)
    return jnp.einsum('hij,jhp->ihp', weighted.astype(jnp.float32), value_rows.astype(jnp.float32), precision=lax.Precision.HIGHEST)

def span_states(value_rows, step_rows, key_rows, decay_sums, documents, openings):
    per_group = value_rows.shape[1] // key_rows.shape[1]
    tail_decay = jnp.where((documents == documents[-1])[None, :], jnp.exp(decay_sums[:, -1:] - decay_sums), 0.0)
    tail_weight = tail_decay.T * step_rows
    head_keys = jnp.repeat(key_rows.astype(jnp.float32), per_group, axis=1)
    tail_keys = (tail_weight[:, :, None] * head_keys).astype(jnp.bfloat16)
    local_state = jnp.einsum('jhp,jhn->hpn', value_rows.astype(jnp.float32), tail_keys.astype(jnp.float32), precision=lax.Precision.HIGHEST)
    opened = jnp.cumsum(openings)
    span_gate = jnp.where(opened[-1] == 0, jnp.exp(decay_sums[:, -1]), 0.0)
    inflow = jnp.where((opened == 0)[None, :], jnp.exp(decay_sums), 0.0)
    return (local_state, span_gate, inflow)

def span_inflow(query_rows, entering, inflow):
    per_group = entering.shape[0] // query_rows.shape[1]
    head_queries = jnp.repeat(query_rows.astype(jnp.float32), per_group, axis=1)
    carried = jnp.einsum('ihn,hpn->ihp', head_queries, entering, precision=lax.Precision.HIGHEST)
    return carried * inflow.T[:, :, None]

def gated_norm(mixed_rows, gate_rows, norm_gain, groups_local):
    gated_rows = mixed_rows * jax.nn.silu(gate_rows.astype(jnp.float32))
    grouped = gated_rows.reshape(gated_rows.shape[0], groups_local, -1)
    inverse_rms = lax.rsqrt(lax.optimization_barrier(jnp.mean(grouped * grouped, axis=2, keepdims=True)) + 1e-05)
    return ((grouped * inverse_rms).reshape(gated_rows.shape) * norm_gain).astype(jnp.bfloat16)

def reference(values_in, gate_in, keys_in, queries_in, step_in, block_order, doc_lengths, conv_values, conv_keys, conv_queries, decay_log, step_bias, skip_gain, norm_gain, out_weight):

    def to_sequence(loaded):
        blocks = loaded.reshape(NBLK, BLK, loaded.shape[1])
        placed = jnp.zeros_like(blocks).at[block_order].set(blocks)
        return placed.reshape(TOKENS, loaded.shape[1])
    value_seq = to_sequence(values_in)
    gate_seq = to_sequence(gate_in)
    key_seq = to_sequence(keys_in)
    query_seq = to_sequence(queries_in)
    step_seq = to_sequence(step_in)
    rim_rows = CONV - 1
    positions = jnp.arange(TOKENS + rim_rows, dtype=jnp.int32) - rim_rows
    doc_ext, open_ext = document_index(positions, doc_lengths)
    documents = doc_ext[rim_rows:]
    openings = open_ext[rim_rows:]
    width_local = HEADS * HEAD_DIM // N_TP
    state_local = GROUPS * STATE // N_TP
    heads_local = HEADS // N_TP
    groups_local = GROUPS // N_TP
    span_count = TOKENS // SPAN

    def padded(rows):
        return jnp.concatenate([jnp.zeros((rim_rows, rows.shape[1]), rows.dtype), rows], axis=0)

    def advance(carried, inputs):
        value_rows, key_rows, query_rows, step_rows, rate_rows, span_docs, span_openings = inputs
        decay_sums = jnp.cumsum(rate_rows.T, axis=1)
        intra = span_outputs(value_rows, step_rows, key_rows, query_rows, decay_sums, span_docs)
        local_state, span_gate, inflow = span_states(value_rows, step_rows, key_rows, decay_sums, span_docs, span_openings)
        inter = span_inflow(query_rows, carried, inflow)
        return (span_gate[:, None, None] * carried + local_state, intra + inter)
    accumulated = jnp.zeros((TOKENS, OUTW), jnp.float32)
    for group_index in range(N_TP):
        channel_lo = group_index * width_local
        state_lo = group_index * state_local
        head_lo = group_index * heads_local
        conv_value = causal_conv(padded(value_seq[:, channel_lo:channel_lo + width_local]), conv_values[:, channel_lo:channel_lo + width_local], doc_ext)
        conv_key = causal_conv(padded(key_seq[:, state_lo:state_lo + state_local]), conv_keys[:, state_lo:state_lo + state_local], doc_ext)
        conv_query = causal_conv(padded(query_seq[:, state_lo:state_lo + state_local]), conv_queries[:, state_lo:state_lo + state_local], doc_ext)
        step_size = jax.nn.softplus(step_seq[:, head_lo:head_lo + heads_local].astype(jnp.float32) + step_bias[head_lo:head_lo + heads_local])
        rates = -jnp.exp(decay_log[head_lo:head_lo + heads_local]) * step_size
        value_rows = conv_value.reshape(span_count, SPAN, heads_local, HEAD_DIM)
        key_rows = conv_key.reshape(span_count, SPAN, groups_local, STATE)
        query_rows = conv_query.reshape(span_count, SPAN, groups_local, STATE)
        start_state = jnp.zeros((heads_local, HEAD_DIM, STATE), jnp.float32)
        inputs = (value_rows, key_rows, query_rows, step_size.reshape(span_count, SPAN, heads_local), rates.reshape(span_count, SPAN, heads_local), documents.reshape(span_count, SPAN), openings.reshape(span_count, SPAN))
        final_state, outputs = lax.scan(advance, start_state, inputs)
        mixed_rows = outputs + skip_gain[head_lo:head_lo + heads_local][None, None, :, None] * value_rows.astype(jnp.float32)
        mixed_rows = mixed_rows.reshape(TOKENS, width_local)
        normed = gated_norm(mixed_rows, gate_seq[:, channel_lo:channel_lo + width_local], norm_gain[channel_lo:channel_lo + width_local], groups_local)
        partial_value = jnp.dot(normed, out_weight[channel_lo:channel_lo + width_local], preferred_element_type=jnp.float32).astype(jnp.bfloat16)
        partial_value = lax.optimization_barrier(partial_value)
        accumulated = accumulated + partial_value.astype(jnp.float32)
    return accumulated.astype(jnp.bfloat16)
```

```python
import functools

import jax
import jax.numpy as jnp
from jax import lax
from jax.experimental import pallas as pl
from jax.experimental.pallas import tpu as pltpu
from jax.sharding import PartitionSpec as P

HEAD_DIM = 64
STATE = 128
CONV = 4
SPAN = 256
BLK = 64


def shifted_2(value, axis, steps):
    count = lax.axis_size(axis)
    leading, last = (max(0, -steps), min(count, count - steps))
    return lax.ppermute(value, axis, [(source, source + steps) for source in range(leading, last)])


def carried_in(shard, axis, join, neutral):
    place = lax.axis_index(axis)
    gathered = jax.tree.map(
        lambda a, kind: lax.all_gather(a.astype(kind), axis),
        shard,
        jax.tree.map(lambda a: jnp.bfloat16 if a.dtype == jnp.float32 else a.dtype, shard),
    )
    state = jax.tree.map(lambda a, e: jnp.zeros_like(a) + jnp.asarray(e, a.dtype), shard, neutral)

    def one(turn, state):
        return join(
            state,
            jax.tree.map(
                lambda a, own: lax.dynamic_index_in_dim(a, turn, 0, False).astype(own.dtype),
                gathered,
                shard,
            ),
        )

    return lax.fori_loop(0, place, one, state)


def document_index(positions, doc_lengths):
    offsets = jnp.cumsum(doc_lengths) - doc_lengths
    below_start = offsets[None, :] <= positions[:, None]
    documents = jnp.sum(below_start.astype(jnp.int32), axis=1, dtype=jnp.int32) - 1
    openings = jnp.any(offsets[None, :] == positions[:, None], axis=1).astype(jnp.int32)
    return (documents, openings)


def causal_conv(extended, weight, doc_ext):
    tap_count = weight.shape[0]
    row_count = extended.shape[0] - tap_count + 1
    current = doc_ext[tap_count - 1 :]
    accumulated = jnp.zeros((row_count, extended.shape[1]), jnp.float32)
    for tap_index in range(tap_count):
        keep_rows = (doc_ext[tap_index : tap_index + row_count] == current)[:, None]
        shifted = (
            extended[tap_index : tap_index + row_count].astype(jnp.float32) * weight[tap_index]
        )
        accumulated = accumulated + jnp.where(keep_rows, shifted, 0.0)
    return lax.optimization_barrier(jax.nn.silu(accumulated).astype(jnp.bfloat16))


def span_outputs(value_rows, step_rows, key_rows, query_rows, decay_sums, documents):
    row_count = value_rows.shape[0]
    per_group = value_rows.shape[1] // key_rows.shape[1]
    row_ids = jnp.arange(row_count, dtype=jnp.int32)
    keep_mask = (documents[:, None] == documents[None, :]) & (row_ids[None, :] <= row_ids[:, None])
    differences = decay_sums[:, :, None] - decay_sums[:, None, :]
    decays = jnp.where(keep_mask[None], jnp.exp(jnp.minimum(differences, 0.0)), 0.0)
    inner_products = jnp.einsum(
        "ign,jgn->gij", query_rows, key_rows, preferred_element_type=jnp.float32
    )
    weighted = (
        decays * jnp.repeat(inner_products, per_group, axis=0) * step_rows.T[:, None, :]
    ).astype(jnp.bfloat16)
    return jnp.einsum("hij,jhp->ihp", weighted, value_rows, preferred_element_type=jnp.float32)


def span_states(value_rows, step_rows, key_rows, decay_sums, documents, openings):
    per_group = value_rows.shape[1] // key_rows.shape[1]
    tail_decay = jnp.where(
        (documents == documents[-1])[None, :], jnp.exp(decay_sums[:, -1:] - decay_sums), 0.0
    )
    tail_weight = tail_decay.T * step_rows
    head_keys = jnp.repeat(key_rows, per_group, axis=1)
    tail_keys = (tail_weight[:, :, None] * head_keys.astype(jnp.float32)).astype(jnp.bfloat16)
    local_state = jnp.einsum(
        "jhp,jhn->hpn", value_rows, tail_keys, preferred_element_type=jnp.float32
    )
    opened = jnp.cumsum(openings)
    span_gate = jnp.where(opened[-1] == 0, jnp.exp(decay_sums[:, -1]), 0.0)
    inflow = jnp.where((opened == 0)[None, :], jnp.exp(decay_sums), 0.0)
    return (local_state, span_gate, inflow)


def span_inflow(query_rows, entering, inflow):
    per_group = entering.shape[0] // query_rows.shape[1]
    head_queries = jnp.repeat(query_rows.astype(jnp.float32), per_group, axis=1)
    carried = jnp.einsum("ihn,hpn->ihp", head_queries, entering, precision=lax.Precision.HIGHEST)
    return carried * inflow.T[:, :, None]


def gated_norm(mixed_rows, gate_rows, norm_gain, groups_local):
    gated_rows = mixed_rows * jax.nn.silu(gate_rows.astype(jnp.float32))
    grouped = gated_rows.reshape(gated_rows.shape[0], groups_local, -1)
    inverse_rms = lax.rsqrt(jnp.mean(grouped * grouped, axis=2, keepdims=True) + 1e-05)
    return ((grouped * inverse_rms).reshape(gated_rows.shape) * norm_gain).astype(jnp.bfloat16)


def on_device(
    values_in,
    gate_in,
    keys_in,
    queries_in,
    step_in,
    block_order,
    doc_lengths,
    conv_values,
    conv_keys,
    conv_queries,
    decay_log,
    step_bias,
    skip_gain,
    norm_gain,
    out_weight,
):
    ctx_count = lax.axis_size("ctx")
    ctx_index = lax.axis_index("ctx")
    token_count = values_in.shape[0]
    per_dev = token_count // BLK
    capacity = (per_dev + ctx_count - 1) // ctx_count
    rim_rows = CONV - 1
    pos_table = block_order.reshape(ctx_count, per_dev)
    owner_of = pos_table // per_dev
    local_ids = jnp.arange(per_dev, dtype=jnp.int32)
    earlier = local_ids[None, :] < local_ids[:, None]
    same_owner = owner_of[:, :, None] == owner_of[:, None, :]
    slot_rank = jnp.sum((same_owner & earlier[None]).astype(jnp.int32), axis=2, dtype=jnp.int32)
    my_owner = lax.dynamic_index_in_dim(owner_of, ctx_index, 0, keepdims=False)
    my_rank = lax.dynamic_index_in_dim(slot_rank, ctx_index, 0, keepdims=False)
    slot_ids = jnp.arange(ctx_count * capacity, dtype=jnp.int32)
    slot_hit = (my_owner * capacity + my_rank)[None, :] == slot_ids[:, None]
    source = jnp.sum(jnp.where(slot_hit, local_ids[None, :], 0), axis=1, dtype=jnp.int32)
    filled = jnp.any(slot_hit, axis=1)

    def pack_slots(local_rows):
        blocks = local_rows.reshape(per_dev, BLK, local_rows.shape[1])
        picked = jnp.where(filled[:, None, None], blocks[source], jnp.zeros((), local_rows.dtype))
        return picked

    all_slots = (jnp.arange(ctx_count, dtype=jnp.int32)[:, None] * capacity + slot_rank).reshape(-1)
    wanted = ctx_index * per_dev + local_ids
    owner_hit = block_order[None, :] == wanted[:, None]
    pick_slot = jnp.sum(jnp.where(owner_hit, all_slots[None, :], 0), axis=1, dtype=jnp.int32)

    def unpack_slots(received):
        return received[pick_slot].reshape(token_count, received.shape[2])

    packed_values = pack_slots(values_in)
    packed_gates = pack_slots(gate_in)
    packed_keys = pack_slots(keys_in)
    packed_queries = pack_slots(queries_in)
    packed_steps = pack_slots(step_in)
    received = (
        lax.all_to_all(packed_values, "ctx", split_axis=0, concat_axis=0, tiled=True),
        lax.all_to_all(packed_gates, "ctx", split_axis=0, concat_axis=0, tiled=True),
        lax.all_to_all(packed_keys, "ctx", split_axis=0, concat_axis=0, tiled=True),
        lax.all_to_all(packed_queries, "ctx", split_axis=0, concat_axis=0, tiled=True),
        lax.all_to_all(packed_steps, "ctx", split_axis=0, concat_axis=0, tiled=True),
    )
    own_values = unpack_slots(received[0])
    own_gates = unpack_slots(received[1])
    own_keys = unpack_slots(received[2])
    own_queries = unpack_slots(received[3])
    own_steps = unpack_slots(received[4])
    rim_values, rim_keys, rim_queries = shifted_2(
        (
            own_values[token_count - rim_rows :],
            own_keys[token_count - rim_rows :],
            own_queries[token_count - rim_rows :],
        ),
        "ctx",
        1,
    )
    positions = (
        ctx_index * token_count - rim_rows + jnp.arange(token_count + rim_rows, dtype=jnp.int32)
    )
    doc_ext, open_ext = document_index(positions, doc_lengths)
    documents = doc_ext[rim_rows:]
    openings = open_ext[rim_rows:]
    conv_value = causal_conv(
        jnp.concatenate([rim_values, own_values], axis=0), conv_values, doc_ext
    )
    conv_key = causal_conv(jnp.concatenate([rim_keys, own_keys], axis=0), conv_keys, doc_ext)
    conv_query = causal_conv(
        jnp.concatenate([rim_queries, own_queries], axis=0), conv_queries, doc_ext
    )
    heads_local = own_steps.shape[1]
    groups_local = own_keys.shape[1] // STATE
    span_count = token_count // SPAN
    step_size = jax.nn.softplus(own_steps.astype(jnp.float32) + step_bias)
    rates = -jnp.exp(decay_log) * step_size
    value_rows = conv_value.reshape(span_count, SPAN, heads_local, HEAD_DIM)
    key_rows = conv_key.reshape(span_count, SPAN, groups_local, STATE)
    query_rows = conv_query.reshape(span_count, SPAN, groups_local, STATE)
    step_spans = step_size.reshape(span_count, SPAN, heads_local)
    decay_sums = jnp.cumsum(rates.reshape(span_count, SPAN, heads_local).transpose(0, 2, 1), axis=2)
    span_docs = documents.reshape(span_count, SPAN)
    span_openings = openings.reshape(span_count, SPAN)
    intra = jax.vmap(span_outputs)(
        value_rows, step_spans, key_rows, query_rows, decay_sums, span_docs
    )
    local_states, span_gates, inflows = jax.vmap(span_states)(
        value_rows, step_spans, key_rows, decay_sums, span_docs, span_openings
    )

    def advance(running, inputs):
        decay_product, accumulated = running
        span_state, span_gate = inputs
        advanced = (span_gate * decay_product, span_gate[:, None, None] * accumulated + span_state)
        return (advanced, running)

    start_carry = (
        jnp.ones((heads_local,), jnp.float32),
        jnp.zeros((heads_local, HEAD_DIM, STATE), jnp.float32),
    )
    summary, prefixes = lax.scan(advance, start_carry, (local_states, span_gates))

    def combine(earlier_part, later_part):
        return (
            earlier_part[0] * later_part[0],
            later_part[0][:, None, None] * earlier_part[1] + later_part[1],
        )

    incoming = carried_in(summary, "ctx", combine, start_carry)
    entering = prefixes[0][:, :, None, None] * incoming[1][None] + prefixes[1]
    entering, inflows = (entering, inflows)
    inter = jax.vmap(span_inflow)(query_rows, entering, inflows)
    mixed_rows = intra + inter + skip_gain[None, None, :, None] * value_rows.astype(jnp.float32)
    mixed_rows = mixed_rows.reshape(token_count, heads_local * HEAD_DIM)
    normed = gated_norm(mixed_rows, own_gates, norm_gain, groups_local)
    return lax.psum_scatter(
        jnp.dot(normed, out_weight, preferred_element_type=jnp.float32).astype(jnp.bfloat16),
        "tp",
        scatter_dimension=0,
        tiled=True,
    )


CHUNK = 128
LANES = 128


def shift_rows(extended, steps, row_count):
    return pltpu.roll(extended, steps, 0)[8 : 8 + row_count]


def tapped(current, previous, taps, since):
    row_count, width = current.shape
    extended = jnp.concatenate([previous, current], axis=0)
    total = None
    for tap_index in range(CONV):
        steps = CONV - 1 - tap_index
        weight = taps[tap_index : tap_index + 1, :]
        if steps == 0:
            term = current * weight
        else:
            keep = since >= steps
            term = jnp.where(keep, shift_rows(extended, steps, row_count) * weight, 0.0)
        total = term if total is None else total + term
    return total / (1.0 + jnp.exp(-total))


def loaded_block(inverse, sequence_block, me, per_dev):
    loaded = inverse[sequence_block]
    slot = jnp.bitwise_xor(lax.div(loaded, per_dev), me)
    return slot, pl.multiple_of(lax.rem(loaded, per_dev) * BLK, BLK)


def invert_order(order, inverse, count):
    def one(j, carry):
        inverse[order[j]] = j
        return carry

    lax.fori_loop(0, count, one, 0)


def mixing_kernel(
    heads,
    group_heads,
    per_dev,
    chunks_step,
    me_ref,
    order_ref,
    lengths_ref,
    rows_ref,
    key_taps_ref,
    query_taps_ref,
    bias_ref,
    log_ref,
    mix_ref,
    query_ref,
    key_ref,
    tail_ref,
    inflow_ref,
    gate_ref,
    since_ref,
    inverse,
    previous,
):
    me = me_ref[0]
    step_id = pl.program_id(0)
    token_rows = per_dev * BLK

    @pl.when(step_id == 0)
    def _():
        invert_order(order_ref, inverse, order_ref.shape[0])
        previous[...] = jnp.zeros_like(previous)

    lane = lax.broadcasted_iota(jnp.int32, (8, LANES), 1)
    row8 = lax.broadcasted_iota(jnp.int32, (8, LANES), 0)
    own = lax.rem(me * heads, group_heads)
    bias = jnp.zeros((8, LANES), jnp.float32)
    decay = jnp.zeros((8, LANES), jnp.float32)
    for h in range(heads):
        bias = jnp.where(row8 == h, bias_ref[me * heads + h], bias)
        decay = jnp.where(row8 == h, log_ref[me * heads + h], decay)
    decay = -jnp.exp(decay)
    causal = lax.broadcasted_iota(jnp.int32, (CHUNK, CHUNK), 0) >= lax.broadcasted_iota(
        jnp.int32, (CHUNK, CHUNK), 1
    )
    column = lax.broadcasted_iota(jnp.int32, (CHUNK, CHUNK), 1).astype(jnp.float32)
    row_of = lax.broadcasted_iota(jnp.int32, (CHUNK, CHUNK), 0).astype(jnp.float32)
    low_half = lax.broadcasted_iota(jnp.int32, (CHUNK, LANES), 1) < HEAD_DIM
    taps = jnp.concatenate([key_taps_ref[...], query_taps_ref[...]], axis=1)

    def one_chunk(local, carry):
        chunk = step_id * chunks_step + local
        first = chunk * CHUNK
        pieces, raw = [], None
        for half in range(CHUNK // BLK):
            loaded = inverse[chunk * (CHUNK // BLK) + half]
            slot = jnp.bitwise_xor(lax.div(loaded, per_dev), me)
            inner = lax.rem(loaded, per_dev)
            start = pl.multiple_of(inner * BLK, BLK)
            pieces.append(rows_ref[slot, pl.ds(start, BLK), :].astype(jnp.float32))
            lanes_at = pl.multiple_of(lax.div(inner, 2) * LANES, LANES)
            steps_in = rows_ref[
                slot, pl.ds(token_rows, group_heads), pl.ds(lanes_at, LANES)
            ].astype(jnp.float32)
            turn = BLK * jnp.bitwise_xor(lax.rem(inner, 2), half)
            steps_in = pltpu.roll(steps_in, turn, 1)
            raw = steps_in if raw is None else jnp.where(lane[:1] < BLK, raw, steps_in)
        raw = pltpu.roll(raw, lax.rem(group_heads - own, group_heads), 0)[:8] + bias
        step = jnp.maximum(raw, 0.0) + jnp.log(1.0 + jnp.exp(-jnp.abs(raw)))
        sums = decay * step
        width = 1
        while width < CHUNK:
            sums = sums + jnp.where(lane >= width, pltpu.roll(sums, width, 1), 0.0)
            width *= 2
        position = first + lane
        begun = jnp.zeros_like(lane)
        offset = jnp.int32(0)
        for k in range(lengths_ref.shape[0]):
            begun = jnp.where(position >= offset, offset, begun)
            offset = offset + lengths_ref[k]
        last_sum = jnp.sum(jnp.where(lane == CHUNK - 1, sums, 0.0), axis=1, keepdims=True)
        last_begun = jnp.max(begun, axis=1, keepdims=True)
        tail = jnp.where(position >= last_begun, jnp.exp(last_sum - sums) * step, 0.0)
        inflow = jnp.where(begun < first, jnp.exp(sums), 0.0)
        gate = jnp.where(last_begun < first, jnp.exp(last_sum), 0.0)
        since = (position - begun).astype(jnp.float32)
        stacked = jnp.concatenate(
            [sums, tail, inflow, since, jnp.zeros((CHUNK - 32, LANES), jnp.float32)], axis=0
        )
        turned = stacked.T

        def spread(at):
            return jnp.broadcast_to(turned[:, at : at + 1], (CHUNK, LANES))

        since_rows = spread(24)
        since_ref[local] = since_rows
        current = jnp.concatenate(pieces, axis=0)
        wide_since = jnp.concatenate([since_rows, since_rows], axis=1)
        conv = tapped(current, previous[...], taps, wide_since).astype(jnp.bfloat16)
        previous[...] = current[CHUNK - 8 :]
        keys, queries = conv[:, :STATE], conv[:, STATE:]
        query_ref[local] = queries
        key_ref[local] = keys.astype(jnp.float32).T.astype(jnp.bfloat16)
        inner_products = lax.dot_general(
            queries, keys, (((1,), (1,)), ((), ())), preferred_element_type=jnp.float32
        )
        allowed = jnp.where(causal & (column >= row_of - since_rows), 0.0, -1e30)
        for h in range(heads):
            exponent = (spread(h) + allowed) - sums[h : h + 1, :]
            weights = jnp.exp(exponent) * (inner_products * step[h : h + 1, :])
            mix_ref[local, :, h * CHUNK : (h + 1) * CHUNK] = weights.astype(jnp.bfloat16)
        for pair in range(heads // 2):
            at = slice(pair * LANES, (pair + 1) * LANES)
            tail_ref[local, :, at] = jnp.where(
                low_half, spread(8 + 2 * pair), spread(9 + 2 * pair)
            )
            inflow_ref[local, :, at] = jnp.where(
                low_half, spread(16 + 2 * pair), spread(17 + 2 * pair)
            )
            gate_ref[local, :, at] = jnp.where(
                low_half[:8],
                jnp.broadcast_to(gate[2 * pair : 2 * pair + 1], (8, LANES)),
                jnp.broadcast_to(gate[2 * pair + 1 : 2 * pair + 2], (8, LANES)),
            )
        return carry

    lax.fori_loop(0, chunks_step, one_chunk, 0)


def scan_kernel(
    heads,
    per_dev,
    chunks_step,
    me_ref,
    order_ref,
    skip_ref,
    rows_ref,
    taps_ref,
    mix_ref,
    query_ref,
    key_ref,
    tail_ref,
    inflow_ref,
    gate_ref,
    since_ref,
    out_ref,
    inverse,
    previous,
    state,
):
    me = me_ref[0]
    step_id = pl.program_id(0)

    @pl.when(step_id == 0)
    def _():
        invert_order(order_ref, inverse, order_ref.shape[0])
        previous[...] = jnp.zeros_like(previous)
        state[...] = jnp.zeros_like(state)

    width = heads * HEAD_DIM
    lane = lax.broadcasted_iota(jnp.int32, (1, width), 1)
    skip = jnp.zeros((1, width), jnp.float32)
    for h in range(heads):
        skip = jnp.where(lane >= h * HEAD_DIM, skip_ref[me * heads + h], skip)
    low_half = lax.broadcasted_iota(jnp.int32, (CHUNK, LANES), 1) < HEAD_DIM
    taps = taps_ref[...]

    def one_chunk(local, carry):
        chunk = step_id * chunks_step + local
        pieces = []
        for half in range(CHUNK // BLK):
            slot, start = loaded_block(
                inverse, chunk * (CHUNK // BLK) + half, me, per_dev
            )
            pieces.append(rows_ref[slot, pl.ds(start, BLK), :].astype(jnp.float32))
        current = jnp.concatenate(pieces, axis=0)
        since = since_ref[local]
        wide_since = jnp.concatenate([since] * (width // LANES), axis=1)
        values = tapped(current, previous[...], taps, wide_since).astype(jnp.bfloat16)
        previous[...] = current[CHUNK - 8 :]
        values_wide = values.astype(jnp.float32)
        entering = state[...]
        carried = jnp.dot(
            query_ref[local], entering.astype(jnp.bfloat16), preferred_element_type=jnp.float32
        )
        total = carried * inflow_ref[local] + skip * values_wide
        tail_values = (values_wide * tail_ref[local]).astype(jnp.bfloat16)
        state[...] = gate_ref[local][:1] * entering + jnp.dot(
            key_ref[local], tail_values, preferred_element_type=jnp.float32
        )
        zero = jnp.zeros((CHUNK, LANES), jnp.bfloat16)
        for pair in range(heads // 2):
            at = slice(pair * LANES, (pair + 1) * LANES)
            both = values[:, at]
            block = jnp.concatenate(
                [jnp.where(low_half, both, zero), jnp.where(low_half, zero, both)], axis=0
            )
            intra = jnp.dot(
                mix_ref[local, :, 2 * pair * CHUNK : 2 * (pair + 1) * CHUNK],
                block,
                preferred_element_type=jnp.float32,
            )
            out_ref[local, :, at] = total[:, at] + intra
        return carry

    lax.fori_loop(0, chunks_step, one_chunk, 0)


def gating_kernel(per_dev, me_ref, order_ref, mixed_ref, rows_ref, *refs):
    out_refs, inverse = refs[:-1], refs[-1]
    me = me_ref[0]
    invert_order(order_ref, inverse, order_ref.shape[0])
    for turn, out_ref in enumerate(out_refs):
        owner = jnp.bitwise_xor(me, turn)

        def one_block(b, carry, owner=owner, out_ref=out_ref):
            slot, start = loaded_block(inverse, owner * per_dev + b, me, per_dev)
            gates = rows_ref[slot, pl.ds(start, BLK), :].astype(jnp.float32)
            at = pl.multiple_of((owner * per_dev + b) * BLK, BLK)
            mixed = mixed_ref[pl.ds(at, BLK), :]
            gated = mixed * (gates / (1.0 + jnp.exp(-gates)))
            out_ref[pl.ds(pl.multiple_of(b * BLK, BLK), BLK), :] = gated.astype(jnp.bfloat16)
            return carry

        lax.fori_loop(0, per_dev, one_block, 0)


def projection_kernel(
    groups, place_ref, gated_ref, gain_ref, weight_ref, away_ref, stay_ref, normed
):
    turns, rows, width = gated_ref.shape
    per_group = turns // groups
    me, mine = place_ref[0], place_ref[1]
    piece = rows // 4

    @pl.when(pl.program_id(0) == 0)
    def _():
        for group in range(groups):
            members = range(group * per_group, (group + 1) * per_group)
            squares = jnp.zeros((rows, 1), jnp.float32)
            for turn in members:
                gated = gated_ref[turn].astype(jnp.float32)
                squares = squares + jnp.sum(gated * gated, axis=1, keepdims=True)
            inverse_rms = lax.rsqrt(squares * (1.0 / (per_group * width)) + 1e-05)
            for turn in members:
                source = jnp.bitwise_xor(me, turn)
                gain = gain_ref[pl.ds(source, 1), :]
                result = (gated_ref[turn].astype(jnp.float32) * inverse_rms * gain).astype(
                    jnp.bfloat16
                )
                at = pl.multiple_of(source * width, width)
                for block in range(4):
                    away = jnp.bitwise_xor(block, mine)
                    kept = 1 - lax.rem(away, 2)
                    slot = 2 * kept + (1 - lax.div(away, 2))
                    target = pl.multiple_of(slot * piece, piece)
                    normed[pl.ds(target, piece), pl.ds(at, width)] = result[
                        block * piece : (block + 1) * piece
                    ]

    partial = jnp.dot(normed[...], weight_ref[...], preferred_element_type=jnp.float32)
    partial = partial.astype(jnp.bfloat16)
    away_ref[...] = partial[: 2 * piece]
    stay_ref[...] = partial[2 * piece :]


def head_split(
    values_in,
    gate_in,
    keys_in,
    queries_in,
    step_in,
    block_order,
    doc_lengths,
    conv_values,
    conv_keys,
    conv_queries,
    decay_log,
    step_bias,
    skip_gain,
    norm_gain,
    out_weight,
):
    ctx_count = lax.axis_size("ctx")
    me = lax.axis_index("ctx")
    tp_index = lax.axis_index("tp")
    token_count, channels = values_in.shape
    per_dev = token_count // BLK
    blocks = block_order.shape[0]
    total_tokens = token_count * ctx_count
    heads_local = step_in.shape[1]
    heads = heads_local // ctx_count
    width = heads * HEAD_DIM
    groups = keys_in.shape[1] // STATE
    group_heads = heads_local // groups
    lanes_count = ctx_count // groups
    chunks = total_tokens // CHUNK
    my_group = me // lanes_count
    place = jnp.stack([me, tp_index]).astype(jnp.int32)
    me_only = place[:1]

    def turned(value, turn):
        return lax.ppermute(value, "ctx", [(i, i ^ turn) for i in range(ctx_count)])

    def for_group(group):
        keys = lax.dynamic_slice_in_dim(keys_in, group * STATE, STATE, 1)
        queries = lax.dynamic_slice_in_dim(queries_in, group * STATE, STATE, 1)
        steps = lax.dynamic_slice_in_dim(step_in, group * group_heads, group_heads, 1)
        return jnp.concatenate([jnp.concatenate([keys, queries], axis=1), steps.T], axis=0)

    held = [for_group(my_group)]
    for g in range(1, groups):
        held.append(turned(for_group(my_group ^ g), g * lanes_count))
    held = jnp.stack(held)
    gathered = [held]
    for turn in range(1, lanes_count):
        gathered.append(turned(held, turn))
    group_rows = jnp.stack(gathered, axis=1).reshape((ctx_count,) + held.shape[1:])

    def spread_heads(rows):
        own = lax.dynamic_slice_in_dim(rows, me * width, width, 1)
        result = [own]
        for turn in range(1, ctx_count):
            block = lax.dynamic_slice_in_dim(rows, (me ^ turn) * width, width, 1)
            result.append(turned(block, turn))
        return jnp.stack(result)

    value_rows = spread_heads(values_in)
    gate_rows = spread_heads(gate_in)

    key_taps = lax.dynamic_slice_in_dim(conv_keys, my_group * STATE, STATE, 1)
    query_taps = lax.dynamic_slice_in_dim(conv_queries, my_group * STATE, STATE, 1)
    value_taps = lax.dynamic_slice_in_dim(conv_values, me * width, width, 1)

    smem = pl.BlockSpec(memory_space=pltpu.SMEM)

    def whole(array):
        return pl.BlockSpec(array.shape, lambda *ids: (0,) * array.ndim)

    grid_steps = 4
    chunks_step = chunks // grid_steps

    def per_step(rows, columns):
        return pl.BlockSpec((chunks_step, rows, columns), lambda i: (i, 0, 0))

    mix_shapes = [
        ((CHUNK, heads * CHUNK), jnp.bfloat16),
        ((CHUNK, STATE), jnp.bfloat16),
        ((STATE, CHUNK), jnp.bfloat16),
        ((CHUNK, width), jnp.float32),
        ((CHUNK, width), jnp.float32),
        ((8, width), jnp.float32),
        ((CHUNK, LANES), jnp.float32),
    ]
    mixing = pl.pallas_call(
        functools.partial(mixing_kernel, heads, group_heads, per_dev, chunks_step),
        grid=(grid_steps,),
        in_specs=[smem, smem, smem, whole(group_rows), whole(key_taps), whole(query_taps), smem, smem],
        out_specs=[per_step(*shape) for shape, _ in mix_shapes],
        out_shape=[jax.ShapeDtypeStruct((chunks,) + shape, kind) for shape, kind in mix_shapes],
        scratch_shapes=[pltpu.SMEM((blocks,), jnp.int32), pltpu.VMEM((8, 2 * STATE), jnp.float32)],
        compiler_params=pltpu.CompilerParams(vmem_limit_bytes=24 * 1024 * 1024),
        cost_estimate=pl.CostEstimate(flops=20_000_000, bytes_accessed=12_000_000, transcendentals=2_000_000),
        name="mixing",
    )(me_only, block_order, doc_lengths, group_rows, key_taps, query_taps, step_bias, decay_log)

    mixed = pl.pallas_call(
        functools.partial(scan_kernel, heads, per_dev, chunks_step),
        grid=(grid_steps,),
        in_specs=[smem, smem, smem, whole(value_rows), whole(value_taps)]
        + [per_step(*shape) for shape, _ in mix_shapes],
        out_specs=per_step(CHUNK, width),
        out_shape=jax.ShapeDtypeStruct((chunks, CHUNK, width), jnp.float32),
        scratch_shapes=[
            pltpu.SMEM((blocks,), jnp.int32),
            pltpu.VMEM((8, width), jnp.float32),
            pltpu.VMEM((STATE, width), jnp.float32),
        ],
        compiler_params=pltpu.CompilerParams(vmem_limit_bytes=24 * 1024 * 1024),
        cost_estimate=pl.CostEstimate(flops=600_000_000, bytes_accessed=14_000_000, transcendentals=600_000),
        name="scan",
    )(me_only, block_order, skip_gain, value_rows, value_taps, *mixing)

    gated = pl.pallas_call(
        functools.partial(gating_kernel, per_dev),
        in_specs=[smem, smem, pl.BlockSpec(memory_space=pltpu.VMEM), pl.BlockSpec(memory_space=pltpu.VMEM)],
        out_specs=[pl.BlockSpec(memory_space=pltpu.VMEM)] * ctx_count,
        out_shape=[jax.ShapeDtypeStruct((token_count, width), jnp.bfloat16)] * ctx_count,
        scratch_shapes=[pltpu.SMEM((blocks,), jnp.int32)],
        compiler_params=pltpu.CompilerParams(vmem_limit_bytes=24 * 1024 * 1024),
        cost_estimate=pl.CostEstimate(flops=5_000_000, bytes_accessed=4_000_000, transcendentals=600_000),
        name="gating",
    )(me_only, block_order, mixed.reshape(total_tokens, width), gate_rows)

    received = jnp.stack([gated[0]] + [turned(gated[turn], turn) for turn in range(1, ctx_count)])

    columns = out_weight.shape[1]
    tile = 512
    half_shape = jax.ShapeDtypeStruct((token_count // 2, columns), jnp.bfloat16)
    gain = norm_gain.reshape(ctx_count, width)
    away, stay = pl.pallas_call(
        functools.partial(projection_kernel, groups),
        grid=(columns // tile,),
        in_specs=[
            smem,
            whole(received),
            whole(gain),
            pl.BlockSpec((channels, tile), lambda i: (0, i)),
        ],
        out_specs=[pl.BlockSpec((token_count // 2, tile), lambda i: (0, i))] * 2,
        out_shape=[half_shape] * 2,
        scratch_shapes=[pltpu.VMEM((token_count, channels), jnp.bfloat16)],
        compiler_params=pltpu.CompilerParams(vmem_limit_bytes=24 * 1024 * 1024),
        cost_estimate=pl.CostEstimate(
            flops=2 * token_count * channels * columns, bytes_accessed=20_000_000, transcendentals=0
        ),
        name="projection",
    )(place, received, gain, out_weight)

    def joined(kept, sent, turn):
        came = lax.ppermute(sent, "tp", [(i, i ^ turn) for i in range(4)])
        return (kept.astype(jnp.float32) + came.astype(jnp.float32)).astype(jnp.bfloat16)

    across = joined(stay, away, 1)
    piece = token_count // 4
    return joined(across[piece:], across[:piece], 2)


def solution(mesh):
    in_specs = (
        P("ctx", "tp"),
        P("ctx", "tp"),
        P("ctx", "tp"),
        P("ctx", "tp"),
        P("ctx", "tp"),
        P(),
        P(),
        P(None, "tp"),
        P(None, "tp"),
        P(None, "tp"),
        P("tp"),
        P("tp"),
        P("tp"),
        P("tp"),
        P("tp", None),
    )
    out_specs = P(("ctx", "tp"), None)
    ctx_count, tp_count = mesh.shape["ctx"], mesh.shape["tp"]
    plan = head_split if tp_count == 4 and ctx_count == 8 else on_device
    return jax.shard_map(
        plan, mesh=mesh, in_specs=in_specs, out_specs=out_specs, check_vma=False
    )
```

```python
import functools

import jax
import jax.numpy as jnp
from jax import lax
from jax.experimental import pallas as pl
from jax.experimental.pallas import tpu as pltpu
from jax.sharding import PartitionSpec as P

HEAD_DIM = 64
STATE = 128
CONV = 4
SPAN = 256
BLK = 64


def shifted_2(value, axis, steps):
    count = lax.axis_size(axis)
    leading, last = (max(0, -steps), min(count, count - steps))
    return lax.ppermute(value, axis, [(source, source + steps) for source in range(leading, last)])


def carried_in(shard, axis, join, neutral):
    place = lax.axis_index(axis)
    gathered = jax.tree.map(
        lambda a, kind: lax.all_gather(a.astype(kind), axis),
        shard,
        jax.tree.map(lambda a: jnp.bfloat16 if a.dtype == jnp.float32 else a.dtype, shard),
    )
    state = jax.tree.map(lambda a, e: jnp.zeros_like(a) + jnp.asarray(e, a.dtype), shard, neutral)

    def one(turn, state):
        return join(
            state,
            jax.tree.map(
                lambda a, own: lax.dynamic_index_in_dim(a, turn, 0, False).astype(own.dtype),
                gathered,
                shard,
            ),
        )

    return lax.fori_loop(0, place, one, state)


def document_index(positions, doc_lengths):
    offsets = jnp.cumsum(doc_lengths) - doc_lengths
    below_start = offsets[None, :] <= positions[:, None]
    documents = jnp.sum(below_start.astype(jnp.int32), axis=1, dtype=jnp.int32) - 1
    openings = jnp.any(offsets[None, :] == positions[:, None], axis=1).astype(jnp.int32)
    return (documents, openings)


def causal_conv(extended, weight, doc_ext):
    tap_count = weight.shape[0]
    row_count = extended.shape[0] - tap_count + 1
    current = doc_ext[tap_count - 1 :]
    accumulated = jnp.zeros((row_count, extended.shape[1]), jnp.float32)
    for tap_index in range(tap_count):
        keep_rows = (doc_ext[tap_index : tap_index + row_count] == current)[:, None]
        shifted = (
            extended[tap_index : tap_index + row_count].astype(jnp.float32) * weight[tap_index]
        )
        accumulated = accumulated + jnp.where(keep_rows, shifted, 0.0)
    return lax.optimization_barrier(jax.nn.silu(accumulated).astype(jnp.bfloat16))


def span_outputs(value_rows, step_rows, key_rows, query_rows, decay_sums, documents):
    row_count = value_rows.shape[0]
    per_group = value_rows.shape[1] // key_rows.shape[1]
    row_ids = jnp.arange(row_count, dtype=jnp.int32)
    keep_mask = (documents[:, None] == documents[None, :]) & (row_ids[None, :] <= row_ids[:, None])
    differences = decay_sums[:, :, None] - decay_sums[:, None, :]
    decays = jnp.where(keep_mask[None], jnp.exp(jnp.minimum(differences, 0.0)), 0.0)
    inner_products = jnp.einsum(
        "ign,jgn->gij", query_rows, key_rows, preferred_element_type=jnp.float32
    )
    weighted = (
        decays * jnp.repeat(inner_products, per_group, axis=0) * step_rows.T[:, None, :]
    ).astype(jnp.bfloat16)
    return jnp.einsum("hij,jhp->ihp", weighted, value_rows, preferred_element_type=jnp.float32)


def span_states(value_rows, step_rows, key_rows, decay_sums, documents, openings):
    per_group = value_rows.shape[1] // key_rows.shape[1]
    tail_decay = jnp.where(
        (documents == documents[-1])[None, :], jnp.exp(decay_sums[:, -1:] - decay_sums), 0.0
    )
    tail_weight = tail_decay.T * step_rows
    head_keys = jnp.repeat(key_rows, per_group, axis=1)
    tail_keys = (tail_weight[:, :, None] * head_keys.astype(jnp.float32)).astype(jnp.bfloat16)
    local_state = jnp.einsum(
        "jhp,jhn->hpn", value_rows, tail_keys, preferred_element_type=jnp.float32
    )
    opened = jnp.cumsum(openings)
    span_gate = jnp.where(opened[-1] == 0, jnp.exp(decay_sums[:, -1]), 0.0)
    inflow = jnp.where((opened == 0)[None, :], jnp.exp(decay_sums), 0.0)
    return (local_state, span_gate, inflow)


def span_inflow(query_rows, entering, inflow):
    per_group = entering.shape[0] // query_rows.shape[1]
    head_queries = jnp.repeat(query_rows.astype(jnp.float32), per_group, axis=1)
    carried = jnp.einsum("ihn,hpn->ihp", head_queries, entering, precision=lax.Precision.HIGHEST)
    return carried * inflow.T[:, :, None]


def gated_norm(mixed_rows, gate_rows, norm_gain, groups_local):
    gated_rows = mixed_rows * jax.nn.silu(gate_rows.astype(jnp.float32))
    grouped = gated_rows.reshape(gated_rows.shape[0], groups_local, -1)
    inverse_rms = lax.rsqrt(jnp.mean(grouped * grouped, axis=2, keepdims=True) + 1e-05)
    return ((grouped * inverse_rms).reshape(gated_rows.shape) * norm_gain).astype(jnp.bfloat16)


def on_device(
    values_in,
    gate_in,
    keys_in,
    queries_in,
    step_in,
    block_order,
    doc_lengths,
    conv_values,
    conv_keys,
    conv_queries,
    decay_log,
    step_bias,
    skip_gain,
    norm_gain,
    out_weight,
):
    ctx_count = lax.axis_size("ctx")
    ctx_index = lax.axis_index("ctx")
    token_count = values_in.shape[0]
    per_dev = token_count // BLK
    capacity = (per_dev + ctx_count - 1) // ctx_count
    rim_rows = CONV - 1
    pos_table = block_order.reshape(ctx_count, per_dev)
    owner_of = pos_table // per_dev
    local_ids = jnp.arange(per_dev, dtype=jnp.int32)
    earlier = local_ids[None, :] < local_ids[:, None]
    same_owner = owner_of[:, :, None] == owner_of[:, None, :]
    slot_rank = jnp.sum((same_owner & earlier[None]).astype(jnp.int32), axis=2, dtype=jnp.int32)
    my_owner = lax.dynamic_index_in_dim(owner_of, ctx_index, 0, keepdims=False)
    my_rank = lax.dynamic_index_in_dim(slot_rank, ctx_index, 0, keepdims=False)
    slot_ids = jnp.arange(ctx_count * capacity, dtype=jnp.int32)
    slot_hit = (my_owner * capacity + my_rank)[None, :] == slot_ids[:, None]
    source = jnp.sum(jnp.where(slot_hit, local_ids[None, :], 0), axis=1, dtype=jnp.int32)
    filled = jnp.any(slot_hit, axis=1)

    def pack_slots(local_rows):
        blocks = local_rows.reshape(per_dev, BLK, local_rows.shape[1])
        picked = jnp.where(filled[:, None, None], blocks[source], jnp.zeros((), local_rows.dtype))
        return picked

    all_slots = (jnp.arange(ctx_count, dtype=jnp.int32)[:, None] * capacity + slot_rank).reshape(-1)
    wanted = ctx_index * per_dev + local_ids
    owner_hit = block_order[None, :] == wanted[:, None]
    pick_slot = jnp.sum(jnp.where(owner_hit, all_slots[None, :], 0), axis=1, dtype=jnp.int32)

    def unpack_slots(received):
        return received[pick_slot].reshape(token_count, received.shape[2])

    packed_values = pack_slots(values_in)
    packed_gates = pack_slots(gate_in)
    packed_keys = pack_slots(keys_in)
    packed_queries = pack_slots(queries_in)
    packed_steps = pack_slots(step_in)
    received = (
        lax.all_to_all(packed_values, "ctx", split_axis=0, concat_axis=0, tiled=True),
        lax.all_to_all(packed_gates, "ctx", split_axis=0, concat_axis=0, tiled=True),
        lax.all_to_all(packed_keys, "ctx", split_axis=0, concat_axis=0, tiled=True),
        lax.all_to_all(packed_queries, "ctx", split_axis=0, concat_axis=0, tiled=True),
        lax.all_to_all(packed_steps, "ctx", split_axis=0, concat_axis=0, tiled=True),
    )
    own_values = unpack_slots(received[0])
    own_gates = unpack_slots(received[1])
    own_keys = unpack_slots(received[2])
    own_queries = unpack_slots(received[3])
    own_steps = unpack_slots(received[4])
    rim_values, rim_keys, rim_queries = shifted_2(
        (
            own_values[token_count - rim_rows :],
            own_keys[token_count - rim_rows :],
            own_queries[token_count - rim_rows :],
        ),
        "ctx",
        1,
    )
    positions = (
        ctx_index * token_count - rim_rows + jnp.arange(token_count + rim_rows, dtype=jnp.int32)
    )
    doc_ext, open_ext = document_index(positions, doc_lengths)
    documents = doc_ext[rim_rows:]
    openings = open_ext[rim_rows:]
    conv_value = causal_conv(
        jnp.concatenate([rim_values, own_values], axis=0), conv_values, doc_ext
    )
    conv_key = causal_conv(jnp.concatenate([rim_keys, own_keys], axis=0), conv_keys, doc_ext)
    conv_query = causal_conv(
        jnp.concatenate([rim_queries, own_queries], axis=0), conv_queries, doc_ext
    )
    heads_local = own_steps.shape[1]
    groups_local = own_keys.shape[1] // STATE
    span_count = token_count // SPAN
    step_size = jax.nn.softplus(own_steps.astype(jnp.float32) + step_bias)
    rates = -jnp.exp(decay_log) * step_size
    value_rows = conv_value.reshape(span_count, SPAN, heads_local, HEAD_DIM)
    key_rows = conv_key.reshape(span_count, SPAN, groups_local, STATE)
    query_rows = conv_query.reshape(span_count, SPAN, groups_local, STATE)
    step_spans = step_size.reshape(span_count, SPAN, heads_local)
    decay_sums = jnp.cumsum(rates.reshape(span_count, SPAN, heads_local).transpose(0, 2, 1), axis=2)
    span_docs = documents.reshape(span_count, SPAN)
    span_openings = openings.reshape(span_count, SPAN)
    intra = jax.vmap(span_outputs)(
        value_rows, step_spans, key_rows, query_rows, decay_sums, span_docs
    )
    local_states, span_gates, inflows = jax.vmap(span_states)(
        value_rows, step_spans, key_rows, decay_sums, span_docs, span_openings
    )

    def advance(running, inputs):
        decay_product, accumulated = running
        span_state, span_gate = inputs
        advanced = (span_gate * decay_product, span_gate[:, None, None] * accumulated + span_state)
        return (advanced, running)

    start_carry = (
        jnp.ones((heads_local,), jnp.float32),
        jnp.zeros((heads_local, HEAD_DIM, STATE), jnp.float32),
    )
    summary, prefixes = lax.scan(advance, start_carry, (local_states, span_gates))

    def combine(earlier_part, later_part):
        return (
            earlier_part[0] * later_part[0],
            later_part[0][:, None, None] * earlier_part[1] + later_part[1],
        )

    incoming = carried_in(summary, "ctx", combine, start_carry)
    entering = prefixes[0][:, :, None, None] * incoming[1][None] + prefixes[1]
    entering, inflows = (entering, inflows)
    inter = jax.vmap(span_inflow)(query_rows, entering, inflows)
    mixed_rows = intra + inter + skip_gain[None, None, :, None] * value_rows.astype(jnp.float32)
    mixed_rows = mixed_rows.reshape(token_count, heads_local * HEAD_DIM)
    normed = gated_norm(mixed_rows, own_gates, norm_gain, groups_local)
    return lax.psum_scatter(
        jnp.dot(normed, out_weight, preferred_element_type=jnp.float32).astype(jnp.bfloat16),
        "tp",
        scatter_dimension=0,
        tiled=True,
    )


CHUNK = 128
LANES = 128


def tapped(current, previous, taps, since):
    row_count = current.shape[0]
    extended = jnp.concatenate([previous, current], axis=0)
    total = None
    for tap_index in range(CONV):
        steps = CONV - 1 - tap_index
        weight = taps[tap_index : tap_index + 1, :]
        if steps == 0:
            term = current * weight
        else:
            shifted = pltpu.roll(extended, steps, 0)[8 : 8 + row_count]
            term = jnp.where(since >= steps, shifted * weight, 0.0)
        total = term if total is None else total + term
    return silu(total)


def silu(x):
    half = 0.5 * x
    return half + half * jnp.tanh(half)


def mixing_kernel(
    heads,
    group_heads,
    per_dev,
    chunks_step,
    piece_count,
    me_ref,
    order_ref,
    lengths_ref,
    bias_ref,
    log_ref,
    key_taps_ref,
    query_taps_ref,
    *refs,
):
    piece_refs, refs = refs[:piece_count], refs[piece_count:]
    mix_ref, query_ref, key_ref, tail_ref, inflow_ref, gate_ref, since_ref = refs[:7]
    sequence, previous, raw_steps, step_rows, row_stack = refs[7:]
    groups = piece_refs[0].shape[0]
    me = me_ref[0]
    step_id = pl.program_id(0)
    token_rows = per_dev * BLK
    chunks = raw_steps.shape[0]

    @pl.when(step_id == 0)
    def _():
        previous[...] = jnp.zeros_like(previous)
        lane = lax.broadcasted_iota(jnp.int32, (8, LANES), 1)
        row8 = lax.broadcasted_iota(jnp.int32, (8, LANES), 0)
        own = lax.rem(me * heads, group_heads)
        for g in range(groups):
            for turn, piece_ref in enumerate(piece_refs):
                loader = jnp.bitwise_xor(me, g * piece_count + turn)
                for b in range(per_dev):
                    place = order_ref[loader * per_dev + b]
                    rows = pl.ds(pl.multiple_of(place * BLK, BLK), BLK)
                    sequence[rows, :] = piece_ref[g, b * BLK : (b + 1) * BLK, :]
                    at = (b // 2) * LANES
                    steps_in = piece_ref[
                        g, token_rows : token_rows + group_heads, at : at + LANES
                    ].astype(jnp.float32)
                    parity = lax.rem(place, 2)
                    steps_in = pltpu.roll(
                        steps_in, lax.rem(group_heads - own, group_heads), 0
                    )[:8]
                    steps_in = pltpu.roll(steps_in, BLK * jnp.bitwise_xor(parity, b % 2), 1)
                    chunk = lax.div(place, 2)
                    raw_steps[chunk] = jnp.where(
                        lane // BLK == parity, steps_in, raw_steps[chunk]
                    )
        bias = jnp.zeros((8, LANES), jnp.float32)
        decay = jnp.zeros((8, LANES), jnp.float32)
        for h in range(heads):
            bias = jnp.where(row8 == h, bias_ref[me * heads + h], bias)
            decay = jnp.where(row8 == h, log_ref[me * heads + h], decay)
        decay = -jnp.exp(decay)
        raw = jnp.where(row8[None] < heads, raw_steps[...] + bias[None], 0.0)
        step = jnp.maximum(raw, 0.0) + jnp.log(1.0 + jnp.exp(-jnp.abs(raw)))
        step_rows[...] = step
        sums = decay[None] * step
        lanes = lax.broadcasted_iota(jnp.int32, (chunks, 8, LANES), 2)
        width = 1
        while width < CHUNK:
            sums = sums + jnp.where(lanes >= width, pltpu.roll(sums, width, 2), 0.0)
            width *= 2
        first = lax.broadcasted_iota(jnp.int32, (chunks, 8, LANES), 0) * CHUNK
        position = first + lanes
        begun = jnp.zeros_like(position)
        offset = jnp.int32(0)
        for k in range(lengths_ref.shape[0]):
            begun = jnp.where(position >= offset, offset, begun)
            offset = offset + lengths_ref[k]
        last_sum = jnp.sum(jnp.where(lanes == CHUNK - 1, sums, 0.0), axis=2, keepdims=True)
        last_begun = jnp.max(begun, axis=2, keepdims=True)
        row_stack[:, 0:8] = sums
        row_stack[:, 8:16] = jnp.where(
            position >= last_begun, jnp.exp(last_sum - sums) * step, 0.0
        )
        row_stack[:, 16:24] = jnp.where(begun < first, jnp.exp(sums), 0.0)
        row_stack[:, 24:32] = (position - begun).astype(jnp.float32)
        row_stack[:, 32:40] = jnp.where(
            last_begun < first, jnp.exp(last_sum), jnp.zeros_like(sums)
        )

    causal = lax.broadcasted_iota(jnp.int32, (CHUNK, CHUNK), 0) >= lax.broadcasted_iota(
        jnp.int32, (CHUNK, CHUNK), 1
    )
    column = lax.broadcasted_iota(jnp.int32, (CHUNK, CHUNK), 1).astype(jnp.float32)
    row_of = lax.broadcasted_iota(jnp.int32, (CHUNK, CHUNK), 0).astype(jnp.float32)
    low_half = lax.broadcasted_iota(jnp.int32, (CHUNK, LANES), 1) < HEAD_DIM
    taps = jnp.concatenate([key_taps_ref[...], query_taps_ref[...]], axis=1)

    def one_chunk(local, carry):
        chunk = step_id * chunks_step + local
        turned = jnp.concatenate(
            [row_stack[chunk, :32], jnp.zeros((CHUNK - 32, LANES), jnp.float32)], axis=0
        ).T

        def spread(at):
            return jnp.broadcast_to(turned[:, at : at + 1], (CHUNK, LANES))

        since_rows = spread(24)
        since_ref[local] = since_rows
        rows = pl.ds(pl.multiple_of(chunk * CHUNK, CHUNK), CHUNK)
        current = sequence[rows, :].astype(jnp.float32)
        wide_since = jnp.concatenate([since_rows, since_rows], axis=1)
        conv = tapped(current, previous[...], taps, wide_since)
        previous[...] = current[CHUNK - 8 :]
        keys, queries = conv[:, :STATE].astype(jnp.bfloat16), conv[:, STATE:].astype(jnp.bfloat16)
        query_ref[local] = queries
        key_ref[local] = conv[:, :STATE].T.astype(jnp.bfloat16)
        inner_products = lax.dot_general(
            queries, keys, (((1,), (1,)), ((), ())), preferred_element_type=jnp.float32
        )
        allowed = jnp.where(causal & (column >= row_of - since_rows), 0.0, -1e30)
        for h in range(heads):
            exponent = (spread(h) + allowed) - row_stack[chunk, h : h + 1, :]
            weights = jnp.exp(exponent) * (inner_products * step_rows[chunk, h : h + 1, :])
            mix_ref[local, :, h * CHUNK : (h + 1) * CHUNK] = weights.astype(jnp.bfloat16)
        gate = row_stack[chunk, 32:40]
        for pair in range(heads // 2):
            at = slice(pair * LANES, (pair + 1) * LANES)
            tail_ref[local, :, at] = jnp.where(
                low_half, spread(8 + 2 * pair), spread(9 + 2 * pair)
            )
            inflow_ref[local, :, at] = jnp.where(
                low_half, spread(16 + 2 * pair), spread(17 + 2 * pair)
            )
            gate_ref[local, :, at] = jnp.where(
                low_half[:8],
                jnp.broadcast_to(gate[2 * pair : 2 * pair + 1], (8, LANES)),
                jnp.broadcast_to(gate[2 * pair + 1 : 2 * pair + 2], (8, LANES)),
            )
        return carry

    lax.fori_loop(0, chunks_step, one_chunk, 0, unroll=2)


def scan_kernel(
    heads, per_dev, chunks_step, piece_count, me_ref, order_ref, skip_ref, taps_ref, *refs
):
    piece_refs, refs = refs[:piece_count], refs[piece_count:]
    mix_ref, query_ref, key_ref, tail_ref, inflow_ref, gate_ref, since_ref, out_ref = refs[:8]
    sequence, previous, state = refs[8:]
    me = me_ref[0]
    step_id = pl.program_id(0)

    @pl.when(step_id == 0)
    def _():
        previous[...] = jnp.zeros_like(previous)
        state[...] = jnp.zeros_like(state)
        for turn, piece_ref in enumerate(piece_refs):
            loader = jnp.bitwise_xor(me, turn)
            for b in range(per_dev):
                place = order_ref[loader * per_dev + b]
                rows = pl.ds(pl.multiple_of(place * BLK, BLK), BLK)
                sequence[rows, :] = piece_ref[b * BLK : (b + 1) * BLK, :]

    width = heads * HEAD_DIM
    lane = lax.broadcasted_iota(jnp.int32, (1, width), 1)
    skip = jnp.zeros((1, width), jnp.float32)
    for h in range(heads):
        skip = jnp.where(lane >= h * HEAD_DIM, skip_ref[me * heads + h], skip)
    low_half = lax.broadcasted_iota(jnp.int32, (CHUNK, LANES), 1) < HEAD_DIM
    taps = taps_ref[...]

    def one_chunk(local, carry):
        chunk = step_id * chunks_step + local
        rows = pl.ds(pl.multiple_of(chunk * CHUNK, CHUNK), CHUNK)
        current = sequence[rows, :].astype(jnp.float32)
        wide_since = jnp.concatenate([since_ref[local]] * (width // LANES), axis=1)
        values = tapped(current, previous[...], taps, wide_since).astype(jnp.bfloat16)
        previous[...] = current[CHUNK - 8 :]
        values_wide = values.astype(jnp.float32)
        entering = state[...]
        carried = jnp.dot(
            query_ref[local], entering.astype(jnp.bfloat16), preferred_element_type=jnp.float32
        )
        total = carried * inflow_ref[local] + skip * values_wide
        tail_values = (values_wide * tail_ref[local]).astype(jnp.bfloat16)
        state[...] = gate_ref[local, :1, :] * entering + jnp.dot(
            key_ref[local], tail_values, preferred_element_type=jnp.float32
        )
        zero = jnp.zeros((CHUNK, LANES), jnp.bfloat16)
        for pair in range(heads // 2):
            at = slice(pair * LANES, (pair + 1) * LANES)
            both = values[:, at]
            block = jnp.concatenate(
                [jnp.where(low_half, both, zero), jnp.where(low_half, zero, both)], axis=0
            )
            intra = jnp.dot(
                mix_ref[local, :, 2 * pair * CHUNK : 2 * (pair + 1) * CHUNK],
                block,
                preferred_element_type=jnp.float32,
            )
            out_ref[local, :, at] = total[:, at] + intra
        return carry

    lax.fori_loop(0, chunks_step, one_chunk, 0, unroll=2)


def gating_kernel(per_dev, piece_count, place_ref, order_ref, mixed_ref, *refs):
    piece_refs, out_refs, laid = refs[:piece_count], refs[piece_count:-1], refs[-1]
    me, mine = place_ref[0], place_ref[1]
    for turn, piece_ref in enumerate(piece_refs):
        loader = jnp.bitwise_xor(me, turn)
        for b in range(per_dev):
            place = order_ref[loader * per_dev + b]
            gates = piece_ref[b * BLK : (b + 1) * BLK, :].astype(jnp.float32)
            mixed = mixed_ref[pl.ds(pl.multiple_of(place * BLK, BLK), BLK), :]
            gated = (mixed * silu(gates)).astype(jnp.bfloat16)
            owner_turn = jnp.bitwise_xor(lax.div(place, per_dev), me)
            away = jnp.bitwise_xor(lax.rem(place, per_dev), mine)
            slot = 2 * (1 - lax.rem(away, 2)) + (1 - lax.div(away, 2))
            laid[owner_turn, pl.ds(pl.multiple_of(slot * BLK, BLK), BLK), :] = gated
    for turn, out_ref in enumerate(out_refs):
        out_ref[...] = laid[turn]


def normed_into(normed, gated_refs, gain_ref, me, first_turn):
    count = len(gated_refs)
    rows, width = gated_refs[0].shape
    wide = [ref[...].astype(jnp.float32) for ref in gated_refs]
    squares = wide[0] * wide[0]
    for piece in wide[1:]:
        squares = squares + piece * piece
    mean = jnp.sum(squares, axis=1, keepdims=True) * (1.0 / (count * width))
    inverse_rms = lax.rsqrt(mean + 1e-05)
    for turn, piece in enumerate(wide):
        source = jnp.bitwise_xor(me, first_turn + turn)
        at = pl.multiple_of(lax.rem(source, count) * width, width)
        gain = gain_ref[pl.ds(source, 1), :]
        normed[:, pl.ds(at, width)] = (piece * inverse_rms * gain).astype(jnp.bfloat16)


def near_kernel(place_ref, gain_ref, weight_ref, *refs):
    gated_refs, partial_ref, normed = refs[:-2], refs[-2], refs[-1]

    @pl.when(pl.program_id(0) == 0)
    def _():
        normed_into(normed, gated_refs, gain_ref, place_ref[0], 0)

    partial_ref[...] = jnp.dot(
        normed[...], weight_ref[...], preferred_element_type=jnp.float32
    )


def far_kernel(place_ref, gain_ref, weight_ref, near_ref, *refs):
    gated_refs, away_ref, stay_ref, normed = refs[:-3], refs[-3], refs[-2], refs[-1]

    @pl.when(pl.program_id(0) == 0)
    def _():
        normed_into(normed, gated_refs, gain_ref, place_ref[0], len(gated_refs))

    partial = near_ref[...] + jnp.dot(
        normed[...], weight_ref[...], preferred_element_type=jnp.float32
    )
    partial = partial.astype(jnp.bfloat16)
    rows = partial.shape[0] // 2
    away_ref[...] = partial[:rows]
    stay_ref[...] = partial[rows:]


def head_split(
    values_in,
    gate_in,
    keys_in,
    queries_in,
    step_in,
    block_order,
    doc_lengths,
    conv_values,
    conv_keys,
    conv_queries,
    decay_log,
    step_bias,
    skip_gain,
    norm_gain,
    out_weight,
):
    ctx_count = lax.axis_size("ctx")
    tp_count = lax.axis_size("tp")
    me = lax.axis_index("ctx")
    tp_index = lax.axis_index("tp")
    token_count, channels = values_in.shape
    per_dev = token_count // BLK
    total_tokens = token_count * ctx_count
    heads_local = step_in.shape[1]
    heads = heads_local // ctx_count
    width = heads * HEAD_DIM
    groups = keys_in.shape[1] // STATE
    group_heads = heads_local // groups
    near = ctx_count // groups
    chunks = total_tokens // CHUNK
    my_group = me // near
    place = jnp.stack([me, tp_index]).astype(jnp.int32)

    def turned(value, turn):
        return lax.ppermute(value, "ctx", [(i, i ^ turn) for i in range(ctx_count)])

    def for_group(group):
        keys = lax.dynamic_slice_in_dim(keys_in, group * STATE, STATE, 1)
        queries = lax.dynamic_slice_in_dim(queries_in, group * STATE, STATE, 1)
        steps = lax.dynamic_slice_in_dim(step_in, group * group_heads, group_heads, 1)
        return jnp.concatenate([jnp.concatenate([keys, queries], axis=1), steps.T], axis=0)

    def for_heads(turn):
        at = (me ^ turn) * width
        return jnp.stack(
            [lax.dynamic_slice_in_dim(rows, at, width, 1) for rows in (values_in, gate_in)]
        )

    held = jnp.stack([for_group(my_group), turned(for_group(my_group ^ 1), near)])
    group_rows = [held] + [turned(held, turn) for turn in range(1, near)]
    head_rows = [for_heads(0)] + [turned(for_heads(turn), turn) for turn in range(1, ctx_count)]

    key_taps = lax.dynamic_slice_in_dim(conv_keys, my_group * STATE, STATE, 1)
    query_taps = lax.dynamic_slice_in_dim(conv_queries, my_group * STATE, STATE, 1)
    value_taps = lax.dynamic_slice_in_dim(conv_values, me * width, width, 1)

    smem = pl.BlockSpec(memory_space=pltpu.SMEM)
    vmem = pl.BlockSpec(memory_space=pltpu.VMEM)
    params = pltpu.CompilerParams(vmem_limit_bytes=28 * 1024 * 1024)

    def whole(array):
        return pl.BlockSpec(array.shape, lambda *ids: (0,) * array.ndim)

    grid_steps = 4
    chunks_step = chunks // grid_steps

    def per_step(rows, columns):
        return pl.BlockSpec((chunks_step, rows, columns), lambda i: (i, 0, 0))

    mix_shapes = [
        ((CHUNK, heads * CHUNK), jnp.bfloat16),
        ((CHUNK, STATE), jnp.bfloat16),
        ((STATE, CHUNK), jnp.bfloat16),
        ((CHUNK, width), jnp.float32),
        ((CHUNK, width), jnp.float32),
        ((8, width), jnp.float32),
        ((CHUNK, LANES), jnp.float32),
    ]
    mixing = pl.pallas_call(
        functools.partial(mixing_kernel, heads, group_heads, per_dev, chunks_step, near),
        grid=(grid_steps,),
        in_specs=[smem] * 5 + [whole(key_taps), whole(query_taps)] + [whole(held)] * near,
        out_specs=[per_step(*shape) for shape, _ in mix_shapes],
        out_shape=[jax.ShapeDtypeStruct((chunks,) + shape, kind) for shape, kind in mix_shapes],
        scratch_shapes=[
            pltpu.VMEM((total_tokens, 2 * STATE), jnp.bfloat16),
            pltpu.VMEM((8, 2 * STATE), jnp.float32),
            pltpu.VMEM((chunks, 8, LANES), jnp.float32),
            pltpu.VMEM((chunks, 8, LANES), jnp.float32),
            pltpu.VMEM((chunks, 40, LANES), jnp.float32),
        ],
        compiler_params=params,
        cost_estimate=pl.CostEstimate(
            flops=20_000_000, bytes_accessed=20_000_000, transcendentals=2_000_000
        ),
        name="mixing",
    )(place, block_order, doc_lengths, step_bias, decay_log, key_taps, query_taps, *group_rows)

    mixed = pl.pallas_call(
        functools.partial(scan_kernel, heads, per_dev, chunks_step, ctx_count),
        grid=(grid_steps,),
        in_specs=[smem] * 3
        + [whole(value_taps)]
        + [pl.BlockSpec((None, token_count, width), lambda i: (0, 0, 0))] * ctx_count
        + [per_step(*shape) for shape, _ in mix_shapes],
        out_specs=per_step(CHUNK, width),
        out_shape=jax.ShapeDtypeStruct((chunks, CHUNK, width), jnp.float32),
        scratch_shapes=[
            pltpu.VMEM((total_tokens, width), jnp.bfloat16),
            pltpu.VMEM((8, width), jnp.float32),
            pltpu.VMEM((STATE, width), jnp.float32),
        ],
        compiler_params=params,
        cost_estimate=pl.CostEstimate(
            flops=600_000_000, bytes_accessed=14_000_000, transcendentals=600_000
        ),
        name="scan",
    )(place, block_order, skip_gain, value_taps, *head_rows, *mixing)

    gated = pl.pallas_call(
        functools.partial(gating_kernel, per_dev, ctx_count),
        grid=(1,),
        in_specs=[smem, smem, pl.BlockSpec((total_tokens, width), lambda i: (0, 0))]
        + [pl.BlockSpec((None, token_count, width), lambda i: (1, 0, 0))] * ctx_count,
        out_specs=[pl.BlockSpec((token_count, width), lambda i: (0, 0))] * ctx_count,
        out_shape=[jax.ShapeDtypeStruct((token_count, width), jnp.bfloat16)] * ctx_count,
        scratch_shapes=[pltpu.VMEM((ctx_count, token_count, width), jnp.bfloat16)],
        compiler_params=params,
        cost_estimate=pl.CostEstimate(
            flops=5_000_000, bytes_accessed=4_000_000, transcendentals=600_000
        ),
        name="gating",
    )(place, block_order, mixed.reshape(total_tokens, width), *head_rows)

    pieces = [gated[0]] + [turned(gated[turn], turn) for turn in range(1, ctx_count)]

    columns = out_weight.shape[1]
    tile = 2048
    tiles = columns // tile
    group_width = near * width
    gain = norm_gain.reshape(ctx_count, width)
    weight = out_weight.reshape(groups, group_width, columns)

    def project(kernel, gated_pieces, own, first, count, extra, extra_specs, out_specs, out_shape):
        spec = pltpu.PrefetchScalarGridSpec(
            num_scalar_prefetch=1,
            grid=(count,),
            in_specs=[
                pl.BlockSpec(gain.shape, lambda i, at: (0, 0)),
                pl.BlockSpec(
                    (None, group_width, tile),
                    lambda i, at: (
                        lax.div(at[0], near) if own else 1 - lax.div(at[0], near),
                        0,
                        first + i,
                    ),
                ),
            ]
            + extra_specs
            + [pl.BlockSpec((token_count, width), lambda i, at: (0, 0))] * len(gated_pieces),
            out_specs=out_specs,
            scratch_shapes=[pltpu.VMEM((token_count, group_width), jnp.bfloat16)],
        )
        return pl.pallas_call(
            kernel,
            grid_spec=spec,
            out_shape=out_shape,
            compiler_params=pltpu.CompilerParams(vmem_limit_bytes=44 * 1024 * 1024),
            cost_estimate=pl.CostEstimate(
                flops=2 * token_count * group_width * tile * count,
                bytes_accessed=2 * group_width * tile * count,
                transcendentals=0,
            ),
            name="near_projection" if own else "far_projection",
        )(place, gain, weight, *extra, *gated_pieces)

    near_partial = project(
        near_kernel,
        pieces[:near],
        True,
        0,
        tiles,
        [],
        [],
        pl.BlockSpec((token_count, tile), lambda i, at: (0, i)),
        jax.ShapeDtypeStruct((token_count, columns), jnp.float32),
    )

    def joined(kept, sent, turn):
        came = lax.ppermute(sent, "tp", [(i, i ^ turn) for i in range(tp_count)])
        return (kept.astype(jnp.float32) + came.astype(jnp.float32)).astype(jnp.bfloat16)

    results = []
    rows = token_count // 2
    parts = 2
    part_tiles = tiles // parts
    for part in range(parts):
        first = part * part_tiles
        away, stay = project(
            far_kernel,
            pieces[near:],
            False,
            first,
            part_tiles,
            [near_partial],
            [pl.BlockSpec((token_count, tile), lambda i, at, first=first: (0, first + i))],
            [pl.BlockSpec((rows, tile), lambda i, at: (0, i))] * 2,
            [jax.ShapeDtypeStruct((rows, columns // parts), jnp.bfloat16)] * 2,
        )
        across = joined(stay, away, 1)
        results.append(joined(across[rows // 2 :], across[: rows // 2], 2))
    return jnp.concatenate(results, axis=1)


def on_mesh(*arrays):
    ctx_count, tp_count = lax.axis_size("ctx"), lax.axis_size("tp")
    groups = arrays[2].shape[1] // STATE
    heads_local = arrays[4].shape[1]
    fits = (
        groups == 2
        and tp_count == 4
        and ctx_count & (ctx_count - 1) == 0
        and heads_local % (2 * ctx_count) == 0
        and heads_local // ctx_count <= 8
        and arrays[0].shape[0] == 2 * STATE
    )
    return (head_split if fits else on_device)(*arrays)


def solution(mesh):
    in_specs = (
        P("ctx", "tp"),
        P("ctx", "tp"),
        P("ctx", "tp"),
        P("ctx", "tp"),
        P("ctx", "tp"),
        P(),
        P(),
        P(None, "tp"),
        P(None, "tp"),
        P(None, "tp"),
        P("tp"),
        P("tp"),
        P("tp"),
        P("tp"),
        P("tp", None),
    )
    out_specs = P(("ctx", "tp"), None)
    return jax.shard_map(
        on_mesh, mesh=mesh, in_specs=in_specs, out_specs=out_specs, check_vma=False
    )
```

```python
import functools

import jax
import jax.numpy as jnp
from jax import lax
from jax.experimental import pallas as pl
from jax.experimental.pallas import tpu as pltpu
from jax.sharding import PartitionSpec as P

HEAD_DIM = 64
STATE = 128
CONV = 4
SPAN = 256
BLK = 64


def shifted_2(value, axis, steps):
    count = lax.axis_size(axis)
    leading, last = (max(0, -steps), min(count, count - steps))
    return lax.ppermute(value, axis, [(source, source + steps) for source in range(leading, last)])


def carried_in(shard, axis, join, neutral):
    place = lax.axis_index(axis)
    gathered = jax.tree.map(
        lambda a, kind: lax.all_gather(a.astype(kind), axis),
        shard,
        jax.tree.map(lambda a: jnp.bfloat16 if a.dtype == jnp.float32 else a.dtype, shard),
    )
    state = jax.tree.map(lambda a, e: jnp.zeros_like(a) + jnp.asarray(e, a.dtype), shard, neutral)

    def one(turn, state):
        return join(
            state,
            jax.tree.map(
                lambda a, own: lax.dynamic_index_in_dim(a, turn, 0, False).astype(own.dtype),
                gathered,
                shard,
            ),
        )

    return lax.fori_loop(0, place, one, state)


def document_index(positions, doc_lengths):
    offsets = jnp.cumsum(doc_lengths) - doc_lengths
    below_start = offsets[None, :] <= positions[:, None]
    documents = jnp.sum(below_start.astype(jnp.int32), axis=1, dtype=jnp.int32) - 1
    openings = jnp.any(offsets[None, :] == positions[:, None], axis=1).astype(jnp.int32)
    return (documents, openings)


def causal_conv(extended, weight, doc_ext):
    tap_count = weight.shape[0]
    row_count = extended.shape[0] - tap_count + 1
    current = doc_ext[tap_count - 1 :]
    accumulated = jnp.zeros((row_count, extended.shape[1]), jnp.float32)
    for tap_index in range(tap_count):
        keep_rows = (doc_ext[tap_index : tap_index + row_count] == current)[:, None]
        shifted = (
            extended[tap_index : tap_index + row_count].astype(jnp.float32) * weight[tap_index]
        )
        accumulated = accumulated + jnp.where(keep_rows, shifted, 0.0)
    return lax.optimization_barrier(jax.nn.silu(accumulated).astype(jnp.bfloat16))


def span_outputs(value_rows, step_rows, key_rows, query_rows, decay_sums, documents):
    row_count = value_rows.shape[0]
    per_group = value_rows.shape[1] // key_rows.shape[1]
    row_ids = jnp.arange(row_count, dtype=jnp.int32)
    keep_mask = (documents[:, None] == documents[None, :]) & (row_ids[None, :] <= row_ids[:, None])
    differences = decay_sums[:, :, None] - decay_sums[:, None, :]
    decays = jnp.where(keep_mask[None], jnp.exp(jnp.minimum(differences, 0.0)), 0.0)
    inner_products = jnp.einsum(
        "ign,jgn->gij", query_rows, key_rows, preferred_element_type=jnp.float32
    )
    weighted = (
        decays * jnp.repeat(inner_products, per_group, axis=0) * step_rows.T[:, None, :]
    ).astype(jnp.bfloat16)
    return jnp.einsum("hij,jhp->ihp", weighted, value_rows, preferred_element_type=jnp.float32)


def span_states(value_rows, step_rows, key_rows, decay_sums, documents, openings):
    per_group = value_rows.shape[1] // key_rows.shape[1]
    tail_decay = jnp.where(
        (documents == documents[-1])[None, :], jnp.exp(decay_sums[:, -1:] - decay_sums), 0.0
    )
    tail_weight = tail_decay.T * step_rows
    head_keys = jnp.repeat(key_rows, per_group, axis=1)
    tail_keys = (tail_weight[:, :, None] * head_keys.astype(jnp.float32)).astype(jnp.bfloat16)
    local_state = jnp.einsum(
        "jhp,jhn->hpn", value_rows, tail_keys, preferred_element_type=jnp.float32
    )
    opened = jnp.cumsum(openings)
    span_gate = jnp.where(opened[-1] == 0, jnp.exp(decay_sums[:, -1]), 0.0)
    inflow = jnp.where((opened == 0)[None, :], jnp.exp(decay_sums), 0.0)
    return (local_state, span_gate, inflow)


def span_inflow(query_rows, entering, inflow):
    per_group = entering.shape[0] // query_rows.shape[1]
    head_queries = jnp.repeat(query_rows.astype(jnp.float32), per_group, axis=1)
    carried = jnp.einsum("ihn,hpn->ihp", head_queries, entering, precision=lax.Precision.HIGHEST)
    return carried * inflow.T[:, :, None]


def gated_norm(mixed_rows, gate_rows, norm_gain, groups_local):
    gated_rows = mixed_rows * jax.nn.silu(gate_rows.astype(jnp.float32))
    grouped = gated_rows.reshape(gated_rows.shape[0], groups_local, -1)
    inverse_rms = lax.rsqrt(jnp.mean(grouped * grouped, axis=2, keepdims=True) + 1e-05)
    return ((grouped * inverse_rms).reshape(gated_rows.shape) * norm_gain).astype(jnp.bfloat16)


def on_device(
    values_in,
    gate_in,
    keys_in,
    queries_in,
    step_in,
    block_order,
    doc_lengths,
    conv_values,
    conv_keys,
    conv_queries,
    decay_log,
    step_bias,
    skip_gain,
    norm_gain,
    out_weight,
):
    ctx_count = lax.axis_size("ctx")
    ctx_index = lax.axis_index("ctx")
    token_count = values_in.shape[0]
    per_dev = token_count // BLK
    capacity = (per_dev + ctx_count - 1) // ctx_count
    rim_rows = CONV - 1
    pos_table = block_order.reshape(ctx_count, per_dev)
    owner_of = pos_table // per_dev
    local_ids = jnp.arange(per_dev, dtype=jnp.int32)
    earlier = local_ids[None, :] < local_ids[:, None]
    same_owner = owner_of[:, :, None] == owner_of[:, None, :]
    slot_rank = jnp.sum((same_owner & earlier[None]).astype(jnp.int32), axis=2, dtype=jnp.int32)
    my_owner = lax.dynamic_index_in_dim(owner_of, ctx_index, 0, keepdims=False)
    my_rank = lax.dynamic_index_in_dim(slot_rank, ctx_index, 0, keepdims=False)
    slot_ids = jnp.arange(ctx_count * capacity, dtype=jnp.int32)
    slot_hit = (my_owner * capacity + my_rank)[None, :] == slot_ids[:, None]
    source = jnp.sum(jnp.where(slot_hit, local_ids[None, :], 0), axis=1, dtype=jnp.int32)
    filled = jnp.any(slot_hit, axis=1)

    def pack_slots(local_rows):
        blocks = local_rows.reshape(per_dev, BLK, local_rows.shape[1])
        picked = jnp.where(filled[:, None, None], blocks[source], jnp.zeros((), local_rows.dtype))
        return picked

    all_slots = (jnp.arange(ctx_count, dtype=jnp.int32)[:, None] * capacity + slot_rank).reshape(-1)
    wanted = ctx_index * per_dev + local_ids
    owner_hit = block_order[None, :] == wanted[:, None]
    pick_slot = jnp.sum(jnp.where(owner_hit, all_slots[None, :], 0), axis=1, dtype=jnp.int32)

    def unpack_slots(received):
        return received[pick_slot].reshape(token_count, received.shape[2])

    packed_values = pack_slots(values_in)
    packed_gates = pack_slots(gate_in)
    packed_keys = pack_slots(keys_in)
    packed_queries = pack_slots(queries_in)
    packed_steps = pack_slots(step_in)
    received = (
        lax.all_to_all(packed_values, "ctx", split_axis=0, concat_axis=0, tiled=True),
        lax.all_to_all(packed_gates, "ctx", split_axis=0, concat_axis=0, tiled=True),
        lax.all_to_all(packed_keys, "ctx", split_axis=0, concat_axis=0, tiled=True),
        lax.all_to_all(packed_queries, "ctx", split_axis=0, concat_axis=0, tiled=True),
        lax.all_to_all(packed_steps, "ctx", split_axis=0, concat_axis=0, tiled=True),
    )
    own_values = unpack_slots(received[0])
    own_gates = unpack_slots(received[1])
    own_keys = unpack_slots(received[2])
    own_queries = unpack_slots(received[3])
    own_steps = unpack_slots(received[4])
    rim_values, rim_keys, rim_queries = shifted_2(
        (
            own_values[token_count - rim_rows :],
            own_keys[token_count - rim_rows :],
            own_queries[token_count - rim_rows :],
        ),
        "ctx",
        1,
    )
    positions = (
        ctx_index * token_count - rim_rows + jnp.arange(token_count + rim_rows, dtype=jnp.int32)
    )
    doc_ext, open_ext = document_index(positions, doc_lengths)
    documents = doc_ext[rim_rows:]
    openings = open_ext[rim_rows:]
    conv_value = causal_conv(
        jnp.concatenate([rim_values, own_values], axis=0), conv_values, doc_ext
    )
    conv_key = causal_conv(jnp.concatenate([rim_keys, own_keys], axis=0), conv_keys, doc_ext)
    conv_query = causal_conv(
        jnp.concatenate([rim_queries, own_queries], axis=0), conv_queries, doc_ext
    )
    heads_local = own_steps.shape[1]
    groups_local = own_keys.shape[1] // STATE
    span_count = token_count // SPAN
    step_size = jax.nn.softplus(own_steps.astype(jnp.float32) + step_bias)
    rates = -jnp.exp(decay_log) * step_size
    value_rows = conv_value.reshape(span_count, SPAN, heads_local, HEAD_DIM)
    key_rows = conv_key.reshape(span_count, SPAN, groups_local, STATE)
    query_rows = conv_query.reshape(span_count, SPAN, groups_local, STATE)
    step_spans = step_size.reshape(span_count, SPAN, heads_local)
    decay_sums = jnp.cumsum(rates.reshape(span_count, SPAN, heads_local).transpose(0, 2, 1), axis=2)
    span_docs = documents.reshape(span_count, SPAN)
    span_openings = openings.reshape(span_count, SPAN)
    intra = jax.vmap(span_outputs)(
        value_rows, step_spans, key_rows, query_rows, decay_sums, span_docs
    )
    local_states, span_gates, inflows = jax.vmap(span_states)(
        value_rows, step_spans, key_rows, decay_sums, span_docs, span_openings
    )

    def advance(running, inputs):
        decay_product, accumulated = running
        span_state, span_gate = inputs
        advanced = (span_gate * decay_product, span_gate[:, None, None] * accumulated + span_state)
        return (advanced, running)

    start_carry = (
        jnp.ones((heads_local,), jnp.float32),
        jnp.zeros((heads_local, HEAD_DIM, STATE), jnp.float32),
    )
    summary, prefixes = lax.scan(advance, start_carry, (local_states, span_gates))

    def combine(earlier_part, later_part):
        return (
            earlier_part[0] * later_part[0],
            later_part[0][:, None, None] * earlier_part[1] + later_part[1],
        )

    incoming = carried_in(summary, "ctx", combine, start_carry)
    entering = prefixes[0][:, :, None, None] * incoming[1][None] + prefixes[1]
    entering, inflows = (entering, inflows)
    inter = jax.vmap(span_inflow)(query_rows, entering, inflows)
    mixed_rows = intra + inter + skip_gain[None, None, :, None] * value_rows.astype(jnp.float32)
    mixed_rows = mixed_rows.reshape(token_count, heads_local * HEAD_DIM)
    normed = gated_norm(mixed_rows, own_gates, norm_gain, groups_local)
    return lax.psum_scatter(
        jnp.dot(normed, out_weight, preferred_element_type=jnp.float32).astype(jnp.bfloat16),
        "tp",
        scatter_dimension=0,
        tiled=True,
    )


CHUNK = 128
LANES = 128


def tapped(current, previous, taps, since):
    row_count = current.shape[0]
    extended = jnp.concatenate([previous, current], axis=0)
    total = None
    for tap_index in range(CONV):
        steps = CONV - 1 - tap_index
        weight = taps[tap_index : tap_index + 1, :]
        if steps == 0:
            term = current * weight
        else:
            shifted = pltpu.roll(extended, steps, 0)[8 : 8 + row_count]
            term = jnp.where(since >= steps, shifted * weight, 0.0)
        total = term if total is None else total + term
    return silu(total)


def silu(x):
    half = 0.5 * x
    return half + half * jnp.tanh(half)


def mixing_kernel(
    heads,
    group_heads,
    per_dev,
    chunks_step,
    piece_count,
    me_ref,
    order_ref,
    lengths_ref,
    bias_ref,
    log_ref,
    key_taps_ref,
    query_taps_ref,
    *refs,
):
    piece_refs, refs = refs[:piece_count], refs[piece_count:]
    mix_ref, query_ref, key_ref, tail_ref, inflow_ref, gate_ref, since_ref = refs[:7]
    sequence, previous, raw_steps, step_rows, row_stack = refs[7:]
    groups = piece_refs[0].shape[0]
    me = me_ref[0]
    step_id = pl.program_id(0)
    token_rows = per_dev * BLK
    chunks = raw_steps.shape[0]

    @pl.when(step_id == 0)
    def _():
        previous[...] = jnp.zeros_like(previous)
        lane = lax.broadcasted_iota(jnp.int32, (8, LANES), 1)
        row8 = lax.broadcasted_iota(jnp.int32, (8, LANES), 0)
        own = lax.rem(me * heads, group_heads)
        for g in range(groups):
            for turn, piece_ref in enumerate(piece_refs):
                loader = jnp.bitwise_xor(me, g * piece_count + turn)
                for b in range(per_dev):
                    place = order_ref[loader * per_dev + b]
                    rows = pl.ds(pl.multiple_of(place * BLK, BLK), BLK)
                    sequence[rows, :] = piece_ref[g, b * BLK : (b + 1) * BLK, :]
                    at = (b // 2) * LANES
                    steps_in = piece_ref[
                        g, token_rows : token_rows + group_heads, at : at + LANES
                    ].astype(jnp.float32)
                    parity = lax.rem(place, 2)
                    steps_in = pltpu.roll(
                        steps_in, lax.rem(group_heads - own, group_heads), 0
                    )[:8]
                    steps_in = pltpu.roll(steps_in, BLK * jnp.bitwise_xor(parity, b % 2), 1)
                    chunk = lax.div(place, 2)
                    raw_steps[chunk] = jnp.where(
                        lane // BLK == parity, steps_in, raw_steps[chunk]
                    )
        bias = jnp.zeros((8, LANES), jnp.float32)
        decay = jnp.zeros((8, LANES), jnp.float32)
        for h in range(heads):
            bias = jnp.where(row8 == h, bias_ref[me * heads + h], bias)
            decay = jnp.where(row8 == h, log_ref[me * heads + h], decay)
        decay = -jnp.exp(decay)
        raw = jnp.where(row8[None] < heads, raw_steps[...] + bias[None], 0.0)
        step = jnp.maximum(raw, 0.0) + jnp.log(1.0 + jnp.exp(-jnp.abs(raw)))
        step_rows[...] = step
        sums = decay[None] * step
        lanes = lax.broadcasted_iota(jnp.int32, (chunks, 8, LANES), 2)
        width = 1
        while width < CHUNK:
            sums = sums + jnp.where(lanes >= width, pltpu.roll(sums, width, 2), 0.0)
            width *= 2
        first = lax.broadcasted_iota(jnp.int32, (chunks, 8, LANES), 0) * CHUNK
        position = first + lanes
        begun = jnp.zeros_like(position)
        offset = jnp.int32(0)
        for k in range(lengths_ref.shape[0]):
            begun = jnp.where(position >= offset, offset, begun)
            offset = offset + lengths_ref[k]
        last_sum = jnp.sum(jnp.where(lanes == CHUNK - 1, sums, 0.0), axis=2, keepdims=True)
        last_begun = jnp.max(begun, axis=2, keepdims=True)
        row_stack[:, 0:8] = sums
        row_stack[:, 8:16] = jnp.where(
            position >= last_begun, jnp.exp(last_sum - sums) * step, 0.0
        )
        row_stack[:, 16:24] = jnp.where(begun < first, jnp.exp(sums), 0.0)
        row_stack[:, 24:32] = (position - begun).astype(jnp.float32)
        row_stack[:, 32:40] = jnp.where(
            last_begun < first, jnp.exp(last_sum), jnp.zeros_like(sums)
        )

    causal = lax.broadcasted_iota(jnp.int32, (CHUNK, CHUNK), 0) >= lax.broadcasted_iota(
        jnp.int32, (CHUNK, CHUNK), 1
    )
    column = lax.broadcasted_iota(jnp.int32, (CHUNK, CHUNK), 1).astype(jnp.float32)
    row_of = lax.broadcasted_iota(jnp.int32, (CHUNK, CHUNK), 0).astype(jnp.float32)
    low_half = lax.broadcasted_iota(jnp.int32, (CHUNK, LANES), 1) < HEAD_DIM
    taps = jnp.concatenate([key_taps_ref[...], query_taps_ref[...]], axis=1)

    def one_chunk(local, carry):
        chunk = step_id * chunks_step + local
        turned = jnp.concatenate(
            [row_stack[chunk, :32], jnp.zeros((CHUNK - 32, LANES), jnp.float32)], axis=0
        ).T

        def spread(at):
            return jnp.broadcast_to(turned[:, at : at + 1], (CHUNK, LANES))

        since_rows = spread(24)
        since_ref[local] = since_rows
        rows = pl.ds(pl.multiple_of(chunk * CHUNK, CHUNK), CHUNK)
        current = sequence[rows, :].astype(jnp.float32)
        wide_since = jnp.concatenate([since_rows, since_rows], axis=1)
        conv = tapped(current, previous[...], taps, wide_since)
        previous[...] = current[CHUNK - 8 :]
        keys, queries = conv[:, :STATE].astype(jnp.bfloat16), conv[:, STATE:].astype(jnp.bfloat16)
        query_ref[local] = queries
        key_ref[local] = conv[:, :STATE].T.astype(jnp.bfloat16)
        inner_products = lax.dot_general(
            queries, keys, (((1,), (1,)), ((), ())), preferred_element_type=jnp.float32
        )
        allowed = jnp.where(causal & (column >= row_of - since_rows), 0.0, -1e30)
        for h in range(heads):
            exponent = (spread(h) + allowed) - row_stack[chunk, h : h + 1, :]
            weights = jnp.exp(exponent) * (inner_products * step_rows[chunk, h : h + 1, :])
            mix_ref[local, :, h * CHUNK : (h + 1) * CHUNK] = weights.astype(jnp.bfloat16)
        gate = row_stack[chunk, 32:40]
        for pair in range(heads // 2):
            at = slice(pair * LANES, (pair + 1) * LANES)
            tail_ref[local, :, at] = jnp.where(
                low_half, spread(8 + 2 * pair), spread(9 + 2 * pair)
            )
            inflow_ref[local, :, at] = jnp.where(
                low_half, spread(16 + 2 * pair), spread(17 + 2 * pair)
            )
            gate_ref[local, :, at] = jnp.where(
                low_half[:8],
                jnp.broadcast_to(gate[2 * pair : 2 * pair + 1], (8, LANES)),
                jnp.broadcast_to(gate[2 * pair + 1 : 2 * pair + 2], (8, LANES)),
            )
        return carry

    lax.fori_loop(0, chunks_step, one_chunk, 0, unroll=2)


def scan_kernel(
    heads, per_dev, chunks_step, turns, me_ref, order_ref, skip_ref, taps_ref, *refs
):
    piece_refs, refs = refs[: len(turns)], refs[len(turns) :]
    mix_ref, query_ref, key_ref, tail_ref, inflow_ref, gate_ref, since_ref, out_ref = refs[:8]
    sequence, previous, state = refs[8:]
    me = me_ref[0]
    step_id = pl.program_id(0)

    @pl.when(step_id == 0)
    def _():
        previous[...] = jnp.zeros_like(previous)
        state[...] = jnp.zeros_like(state)
        for turn, piece_ref in zip(turns, piece_refs):
            loader = jnp.bitwise_xor(me, turn)
            for b in range(per_dev):
                place = order_ref[loader * per_dev + b]
                rows = pl.ds(pl.multiple_of(place * BLK, BLK), BLK)
                sequence[rows, :] = piece_ref[b * BLK : (b + 1) * BLK, :]

    width = heads * HEAD_DIM
    lane = lax.broadcasted_iota(jnp.int32, (1, width), 1)
    skip = jnp.zeros((1, width), jnp.float32)
    for h in range(heads):
        skip = jnp.where(lane >= h * HEAD_DIM, skip_ref[me * heads + h], skip)
    low_half = lax.broadcasted_iota(jnp.int32, (CHUNK, LANES), 1) < HEAD_DIM
    taps = taps_ref[...]

    def one_chunk(local, carry):
        chunk = step_id * chunks_step + local
        rows = pl.ds(pl.multiple_of(chunk * CHUNK, CHUNK), CHUNK)
        current = sequence[rows, :].astype(jnp.float32)
        wide_since = jnp.concatenate([since_ref[local]] * (width // LANES), axis=1)
        values = tapped(current, previous[...], taps, wide_since).astype(jnp.bfloat16)
        previous[...] = current[CHUNK - 8 :]
        values_wide = values.astype(jnp.float32)
        entering = state[...]
        carried = jnp.dot(
            query_ref[local], entering.astype(jnp.bfloat16), preferred_element_type=jnp.float32
        )
        total = carried * inflow_ref[local] + skip * values_wide
        tail_values = (values_wide * tail_ref[local]).astype(jnp.bfloat16)
        state[...] = gate_ref[local, :1, :] * entering + jnp.dot(
            key_ref[local], tail_values, preferred_element_type=jnp.float32
        )
        zero = jnp.zeros((CHUNK, LANES), jnp.bfloat16)
        for pair in range(heads // 2):
            at = slice(pair * LANES, (pair + 1) * LANES)
            both = values[:, at]
            block = jnp.concatenate(
                [jnp.where(low_half, both, zero), jnp.where(low_half, zero, both)], axis=0
            )
            intra = jnp.dot(
                mix_ref[local, :, 2 * pair * CHUNK : 2 * (pair + 1) * CHUNK],
                block,
                preferred_element_type=jnp.float32,
            )
            out_ref[local, :, at] = total[:, at] + intra
        return carry

    lax.fori_loop(0, chunks_step, one_chunk, 0, unroll=2)


def gating_kernel(per_dev, turns, place_ref, order_ref, mixed_ref, *refs):
    piece_refs, out_refs, laid = refs[: len(turns)], refs[len(turns) : -1], refs[-1]
    me, mine = place_ref[0], place_ref[1]
    for turn, piece_ref in zip(turns, piece_refs):
        loader = jnp.bitwise_xor(me, turn)
        for b in range(per_dev):
            place = order_ref[loader * per_dev + b]
            gates = piece_ref[b * BLK : (b + 1) * BLK, :].astype(jnp.float32)
            mixed = mixed_ref[pl.ds(pl.multiple_of(place * BLK, BLK), BLK), :]
            gated = (mixed * silu(gates)).astype(jnp.bfloat16)
            owner_turn = jnp.bitwise_xor(lax.div(place, per_dev), me)
            away = jnp.bitwise_xor(lax.rem(place, per_dev), mine)
            slot = 2 * (1 - lax.rem(away, 2)) + (1 - lax.div(away, 2))
            laid[owner_turn, pl.ds(pl.multiple_of(slot * BLK, BLK), BLK), :] = gated
    for turn, out_ref in enumerate(out_refs):
        out_ref[...] = laid[turn]


def normed_into(normed, gated_refs, gain_ref, me, first_turn):
    count = len(gated_refs)
    rows, width = gated_refs[0].shape
    wide = [ref[...].astype(jnp.float32) for ref in gated_refs]
    squares = wide[0] * wide[0]
    for piece in wide[1:]:
        squares = squares + piece * piece
    mean = jnp.sum(squares, axis=1, keepdims=True) * (1.0 / (count * width))
    inverse_rms = lax.rsqrt(mean + 1e-05)
    for turn, piece in enumerate(wide):
        source = jnp.bitwise_xor(me, first_turn + turn)
        at = pl.multiple_of(lax.rem(source, count) * width, width)
        gain = gain_ref[pl.ds(source, 1), :]
        normed[:, pl.ds(at, width)] = (piece * inverse_rms * gain).astype(jnp.bfloat16)


def weight_tiles(weight_ref, group, buffer, sems, count):
    tile = buffer.shape[1] // count
    tiles = [slice(i * tile, (i + 1) * tile) for i in range(count)]
    return tiles, [
        pltpu.make_async_copy(weight_ref.at[group, :, at], buffer.at[:, at], sems.at[i])
        for i, at in enumerate(tiles)
    ]


def near_kernel(place_ref, gain_ref, weight_ref, *refs):
    gated_refs, (partial_ref, next_ref, normed, buffer, sems) = refs[:-5], refs[-5:]
    count = sems.shape[0] - 1
    group = lax.div(place_ref[0], len(gated_refs))
    tiles, copies = weight_tiles(weight_ref, group, buffer, sems, count)
    onward = pltpu.make_async_copy(weight_ref.at[1 - group], next_ref, sems.at[count])
    for copy in copies + [onward]:
        copy.start()
    normed_into(normed, gated_refs, gain_ref, place_ref[0], 0)
    for at, copy in zip(tiles, copies):
        copy.wait()
        partial_ref[:, at] = jnp.dot(
            normed[...], buffer[:, at], preferred_element_type=jnp.float32
        )
    onward.wait()


def far_kernel(parts, place_ref, gain_ref, weight_ref, near_ref, *refs):
    gated_refs, refs = refs[: -2 * parts - 1], refs[-2 * parts - 1 :]
    away_refs, stay_refs, normed = refs[:parts], refs[parts:-1], refs[-1]
    normed_into(normed, gated_refs, gain_ref, place_ref[0], len(gated_refs))
    rows, columns = away_refs[0].shape
    tile = 1024
    for part in range(parts):
        for first in range(0, columns, tile):
            at = slice(part * columns + first, part * columns + first + tile)
            partial = near_ref[:, at] + jnp.dot(
                normed[...], weight_ref[:, at], preferred_element_type=jnp.float32
            )
            partial = partial.astype(jnp.bfloat16)
            away_refs[part][:, first : first + tile] = partial[:rows]
            stay_refs[part][:, first : first + tile] = partial[rows:]


def head_split(
    values_in,
    gate_in,
    keys_in,
    queries_in,
    step_in,
    block_order,
    doc_lengths,
    conv_values,
    conv_keys,
    conv_queries,
    decay_log,
    step_bias,
    skip_gain,
    norm_gain,
    out_weight,
):
    ctx_count = lax.axis_size("ctx")
    tp_count = lax.axis_size("tp")
    me = lax.axis_index("ctx")
    tp_index = lax.axis_index("tp")
    token_count, channels = values_in.shape
    per_dev = token_count // BLK
    total_tokens = token_count * ctx_count
    heads_local = step_in.shape[1]
    heads = heads_local // ctx_count
    width = heads * HEAD_DIM
    groups = keys_in.shape[1] // STATE
    group_heads = heads_local // groups
    near = ctx_count // groups
    chunks = total_tokens // CHUNK
    my_group = me // near
    place = jnp.stack([me, tp_index]).astype(jnp.int32)

    def turned(value, turn):
        return lax.ppermute(value, "ctx", [(i, i ^ turn) for i in range(ctx_count)])

    def for_group(group):
        keys = lax.dynamic_slice_in_dim(keys_in, group * STATE, STATE, 1)
        queries = lax.dynamic_slice_in_dim(queries_in, group * STATE, STATE, 1)
        steps = lax.dynamic_slice_in_dim(step_in, group * group_heads, group_heads, 1)
        return jnp.concatenate([jnp.concatenate([keys, queries], axis=1), steps.T], axis=0)

    def for_heads(turn):
        at = (me ^ turn) * width
        return jnp.stack(
            [lax.dynamic_slice_in_dim(rows, at, width, 1) for rows in (values_in, gate_in)]
        )

    held = jnp.stack([for_group(my_group), turned(for_group(my_group ^ 1), near)])
    group_rows = [held] + [turned(held, turn) for turn in range(1, near)]
    turns = (0, 6, 7, 4, 3, 2, 5, 1)
    head_rows = [turned(for_heads(turn), turn) if turn else for_heads(turn) for turn in turns]

    key_taps = lax.dynamic_slice_in_dim(conv_keys, my_group * STATE, STATE, 1)
    query_taps = lax.dynamic_slice_in_dim(conv_queries, my_group * STATE, STATE, 1)
    value_taps = lax.dynamic_slice_in_dim(conv_values, me * width, width, 1)

    smem = pl.BlockSpec(memory_space=pltpu.SMEM)
    vmem = pl.BlockSpec(memory_space=pltpu.VMEM)
    params = pltpu.CompilerParams(vmem_limit_bytes=28 * 1024 * 1024)

    def whole(array):
        return pl.BlockSpec(array.shape, lambda *ids: (0,) * array.ndim)

    grid_steps = 4
    chunks_step = chunks // grid_steps

    def per_step(rows, columns):
        return pl.BlockSpec((chunks_step, rows, columns), lambda i: (i, 0, 0))

    mix_shapes = [
        ((CHUNK, heads * CHUNK), jnp.bfloat16),
        ((CHUNK, STATE), jnp.bfloat16),
        ((STATE, CHUNK), jnp.bfloat16),
        ((CHUNK, width), jnp.float32),
        ((CHUNK, width), jnp.float32),
        ((8, width), jnp.float32),
        ((CHUNK, LANES), jnp.float32),
    ]
    mixing = pl.pallas_call(
        functools.partial(mixing_kernel, heads, group_heads, per_dev, chunks_step, near),
        grid=(grid_steps,),
        in_specs=[smem] * 5 + [whole(key_taps), whole(query_taps)] + [whole(held)] * near,
        out_specs=[per_step(*shape) for shape, _ in mix_shapes],
        out_shape=[jax.ShapeDtypeStruct((chunks,) + shape, kind) for shape, kind in mix_shapes],
        scratch_shapes=[
            pltpu.VMEM((total_tokens, 2 * STATE), jnp.bfloat16),
            pltpu.VMEM((8, 2 * STATE), jnp.float32),
            pltpu.VMEM((chunks, 8, LANES), jnp.float32),
            pltpu.VMEM((chunks, 8, LANES), jnp.float32),
            pltpu.VMEM((chunks, 40, LANES), jnp.float32),
        ],
        compiler_params=params,
        cost_estimate=pl.CostEstimate(
            flops=20_000_000, bytes_accessed=20_000_000, transcendentals=2_000_000
        ),
        name="mixing",
    )(place, block_order, doc_lengths, step_bias, decay_log, key_taps, query_taps, *group_rows)

    mixed = pl.pallas_call(
        functools.partial(scan_kernel, heads, per_dev, chunks_step, turns),
        grid=(grid_steps,),
        in_specs=[smem] * 3
        + [whole(value_taps)]
        + [pl.BlockSpec((None, token_count, width), lambda i: (0, 0, 0))] * ctx_count
        + [per_step(*shape) for shape, _ in mix_shapes],
        out_specs=per_step(CHUNK, width),
        out_shape=jax.ShapeDtypeStruct((chunks, CHUNK, width), jnp.float32),
        scratch_shapes=[
            pltpu.VMEM((total_tokens, width), jnp.bfloat16),
            pltpu.VMEM((8, width), jnp.float32),
            pltpu.VMEM((STATE, width), jnp.float32),
        ],
        compiler_params=params,
        cost_estimate=pl.CostEstimate(
            flops=600_000_000, bytes_accessed=14_000_000, transcendentals=600_000
        ),
        name="scan",
    )(place, block_order, skip_gain, value_taps, *head_rows, *mixing)

    gated = pl.pallas_call(
        functools.partial(gating_kernel, per_dev, turns),
        grid=(1,),
        in_specs=[smem, smem, pl.BlockSpec((total_tokens, width), lambda i: (0, 0))]
        + [pl.BlockSpec((None, token_count, width), lambda i: (1, 0, 0))] * ctx_count,
        out_specs=[pl.BlockSpec((token_count, width), lambda i: (0, 0))] * ctx_count,
        out_shape=[jax.ShapeDtypeStruct((token_count, width), jnp.bfloat16)] * ctx_count,
        scratch_shapes=[pltpu.VMEM((ctx_count, token_count, width), jnp.bfloat16)],
        compiler_params=params,
        cost_estimate=pl.CostEstimate(
            flops=5_000_000, bytes_accessed=4_000_000, transcendentals=600_000
        ),
        name="gating",
    )(place, block_order, mixed.reshape(total_tokens, width), *head_rows)

    pieces = [gated[0]] + [turned(gated[turn], turn) for turn in range(1, ctx_count)]

    columns = out_weight.shape[1]
    group_width = near * width
    gain = norm_gain.reshape(ctx_count, width)
    weight = out_weight.reshape(groups, group_width, columns)

    def project(kernel, weight, weight_space, operands, out_shape, scratch, limit, name):
        return pl.pallas_call(
            kernel,
            in_specs=[smem, vmem, pl.BlockSpec(memory_space=weight_space)] + [vmem] * len(operands),
            out_specs=[vmem] * len(out_shape),
            out_shape=out_shape,
            scratch_shapes=[pltpu.VMEM((token_count, group_width), jnp.bfloat16)] + scratch,
            compiler_params=pltpu.CompilerParams(vmem_limit_bytes=limit * 1024 * 1024),
            cost_estimate=pl.CostEstimate(
                flops=2 * token_count * group_width * columns,
                bytes_accessed=2 * group_width * columns,
                transcendentals=0,
            ),
            name=name,
        )(place, gain, weight, *operands)

    near_partial, far_weight = project(
        near_kernel,
        weight,
        pl.ANY,
        pieces[:near],
        [
            jax.ShapeDtypeStruct((token_count, columns), jnp.float32),
            jax.ShapeDtypeStruct((group_width, columns), jnp.bfloat16),
        ],
        [pltpu.VMEM((group_width, columns), jnp.bfloat16), pltpu.SemaphoreType.DMA((5,))],
        28,
        "near_projection",
    )
    parts = 2
    rows = token_count // 2
    part_shape = jax.ShapeDtypeStruct((rows, columns // parts), jnp.bfloat16)
    split = project(
        functools.partial(far_kernel, parts),
        far_weight,
        pltpu.VMEM,
        [near_partial] + pieces[near:],
        [part_shape] * (2 * parts),
        [],
        8,
        "far_projection",
    )

    def joined(kept, sent, turn):
        came = lax.ppermute(sent, "tp", [(i, i ^ turn) for i in range(tp_count)])
        return (kept.astype(jnp.float32) + came.astype(jnp.float32)).astype(jnp.bfloat16)

    results = []
    for away, stay in zip(split[:parts], split[parts:]):
        across = joined(stay, away, 1)
        results.append(joined(across[rows // 2 :], across[: rows // 2], 2))
    return jnp.concatenate(results, axis=1)


def on_mesh(*arrays):
    ctx_count, tp_count = lax.axis_size("ctx"), lax.axis_size("tp")
    groups = arrays[2].shape[1] // STATE
    heads_local = arrays[4].shape[1]
    fits = (
        groups == 2
        and tp_count == 4
        and ctx_count & (ctx_count - 1) == 0
        and heads_local % (2 * ctx_count) == 0
        and heads_local // ctx_count <= 8
        and arrays[0].shape[0] == 2 * STATE
    )
    return (head_split if fits else on_device)(*arrays)


def solution(mesh):
    in_specs = (
        P("ctx", "tp"),
        P("ctx", "tp"),
        P("ctx", "tp"),
        P("ctx", "tp"),
        P("ctx", "tp"),
        P(),
        P(),
        P(None, "tp"),
        P(None, "tp"),
        P(None, "tp"),
        P("tp"),
        P("tp"),
        P("tp"),
        P("tp"),
        P("tp", None),
    )
    out_specs = P(("ctx", "tp"), None)
    return jax.shard_map(
        on_mesh, mesh=mesh, in_specs=in_specs, out_specs=out_specs, check_vma=False
    )
```

```python
import functools

import jax
import jax.numpy as jnp
from jax import lax
from jax.experimental import pallas as pl
from jax.experimental.pallas import tpu as pltpu
from jax.sharding import PartitionSpec as P

HEAD_DIM = 64
STATE = 128
CONV = 4
SPAN = 256
BLK = 64


def shifted_2(value, axis, steps):
    count = lax.axis_size(axis)
    leading, last = (max(0, -steps), min(count, count - steps))
    return lax.ppermute(value, axis, [(source, source + steps) for source in range(leading, last)])


def carried_in(shard, axis, join, neutral):
    place = lax.axis_index(axis)
    gathered = jax.tree.map(
        lambda a, kind: lax.all_gather(a.astype(kind), axis),
        shard,
        jax.tree.map(lambda a: jnp.bfloat16 if a.dtype == jnp.float32 else a.dtype, shard),
    )
    state = jax.tree.map(lambda a, e: jnp.zeros_like(a) + jnp.asarray(e, a.dtype), shard, neutral)

    def one(turn, state):
        return join(
            state,
            jax.tree.map(
                lambda a, own: lax.dynamic_index_in_dim(a, turn, 0, False).astype(own.dtype),
                gathered,
                shard,
            ),
        )

    return lax.fori_loop(0, place, one, state)


def document_index(positions, doc_lengths):
    offsets = jnp.cumsum(doc_lengths) - doc_lengths
    below_start = offsets[None, :] <= positions[:, None]
    documents = jnp.sum(below_start.astype(jnp.int32), axis=1, dtype=jnp.int32) - 1
    openings = jnp.any(offsets[None, :] == positions[:, None], axis=1).astype(jnp.int32)
    return (documents, openings)


def causal_conv(extended, weight, doc_ext):
    tap_count = weight.shape[0]
    row_count = extended.shape[0] - tap_count + 1
    current = doc_ext[tap_count - 1 :]
    accumulated = jnp.zeros((row_count, extended.shape[1]), jnp.float32)
    for tap_index in range(tap_count):
        keep_rows = (doc_ext[tap_index : tap_index + row_count] == current)[:, None]
        shifted = (
            extended[tap_index : tap_index + row_count].astype(jnp.float32) * weight[tap_index]
        )
        accumulated = accumulated + jnp.where(keep_rows, shifted, 0.0)
    return lax.optimization_barrier(jax.nn.silu(accumulated).astype(jnp.bfloat16))


def span_outputs(value_rows, step_rows, key_rows, query_rows, decay_sums, documents):
    row_count = value_rows.shape[0]
    per_group = value_rows.shape[1] // key_rows.shape[1]
    row_ids = jnp.arange(row_count, dtype=jnp.int32)
    keep_mask = (documents[:, None] == documents[None, :]) & (row_ids[None, :] <= row_ids[:, None])
    differences = decay_sums[:, :, None] - decay_sums[:, None, :]
    decays = jnp.where(keep_mask[None], jnp.exp(jnp.minimum(differences, 0.0)), 0.0)
    inner_products = jnp.einsum(
        "ign,jgn->gij", query_rows, key_rows, preferred_element_type=jnp.float32
    )
    weighted = (
        decays * jnp.repeat(inner_products, per_group, axis=0) * step_rows.T[:, None, :]
    ).astype(jnp.bfloat16)
    return jnp.einsum("hij,jhp->ihp", weighted, value_rows, preferred_element_type=jnp.float32)


def span_states(value_rows, step_rows, key_rows, decay_sums, documents, openings):
    per_group = value_rows.shape[1] // key_rows.shape[1]
    tail_decay = jnp.where(
        (documents == documents[-1])[None, :], jnp.exp(decay_sums[:, -1:] - decay_sums), 0.0
    )
    tail_weight = tail_decay.T * step_rows
    head_keys = jnp.repeat(key_rows, per_group, axis=1)
    tail_keys = (tail_weight[:, :, None] * head_keys.astype(jnp.float32)).astype(jnp.bfloat16)
    local_state = jnp.einsum(
        "jhp,jhn->hpn", value_rows, tail_keys, preferred_element_type=jnp.float32
    )
    opened = jnp.cumsum(openings)
    span_gate = jnp.where(opened[-1] == 0, jnp.exp(decay_sums[:, -1]), 0.0)
    inflow = jnp.where((opened == 0)[None, :], jnp.exp(decay_sums), 0.0)
    return (local_state, span_gate, inflow)


def span_inflow(query_rows, entering, inflow):
    per_group = entering.shape[0] // query_rows.shape[1]
    head_queries = jnp.repeat(query_rows.astype(jnp.float32), per_group, axis=1)
    carried = jnp.einsum("ihn,hpn->ihp", head_queries, entering, precision=lax.Precision.HIGHEST)
    return carried * inflow.T[:, :, None]


def gated_norm(mixed_rows, gate_rows, norm_gain, groups_local):
    gated_rows = mixed_rows * jax.nn.silu(gate_rows.astype(jnp.float32))
    grouped = gated_rows.reshape(gated_rows.shape[0], groups_local, -1)
    inverse_rms = lax.rsqrt(jnp.mean(grouped * grouped, axis=2, keepdims=True) + 1e-05)
    return ((grouped * inverse_rms).reshape(gated_rows.shape) * norm_gain).astype(jnp.bfloat16)


def on_device(
    values_in,
    gate_in,
    keys_in,
    queries_in,
    step_in,
    block_order,
    doc_lengths,
    conv_values,
    conv_keys,
    conv_queries,
    decay_log,
    step_bias,
    skip_gain,
    norm_gain,
    out_weight,
):
    ctx_count = lax.axis_size("ctx")
    ctx_index = lax.axis_index("ctx")
    token_count = values_in.shape[0]
    per_dev = token_count // BLK
    capacity = (per_dev + ctx_count - 1) // ctx_count
    rim_rows = CONV - 1
    pos_table = block_order.reshape(ctx_count, per_dev)
    owner_of = pos_table // per_dev
    local_ids = jnp.arange(per_dev, dtype=jnp.int32)
    earlier = local_ids[None, :] < local_ids[:, None]
    same_owner = owner_of[:, :, None] == owner_of[:, None, :]
    slot_rank = jnp.sum((same_owner & earlier[None]).astype(jnp.int32), axis=2, dtype=jnp.int32)
    my_owner = lax.dynamic_index_in_dim(owner_of, ctx_index, 0, keepdims=False)
    my_rank = lax.dynamic_index_in_dim(slot_rank, ctx_index, 0, keepdims=False)
    slot_ids = jnp.arange(ctx_count * capacity, dtype=jnp.int32)
    slot_hit = (my_owner * capacity + my_rank)[None, :] == slot_ids[:, None]
    source = jnp.sum(jnp.where(slot_hit, local_ids[None, :], 0), axis=1, dtype=jnp.int32)
    filled = jnp.any(slot_hit, axis=1)

    def pack_slots(local_rows):
        blocks = local_rows.reshape(per_dev, BLK, local_rows.shape[1])
        picked = jnp.where(filled[:, None, None], blocks[source], jnp.zeros((), local_rows.dtype))
        return picked

    all_slots = (jnp.arange(ctx_count, dtype=jnp.int32)[:, None] * capacity + slot_rank).reshape(-1)
    wanted = ctx_index * per_dev + local_ids
    owner_hit = block_order[None, :] == wanted[:, None]
    pick_slot = jnp.sum(jnp.where(owner_hit, all_slots[None, :], 0), axis=1, dtype=jnp.int32)

    def unpack_slots(received):
        return received[pick_slot].reshape(token_count, received.shape[2])

    packed_values = pack_slots(values_in)
    packed_gates = pack_slots(gate_in)
    packed_keys = pack_slots(keys_in)
    packed_queries = pack_slots(queries_in)
    packed_steps = pack_slots(step_in)
    received = (
        lax.all_to_all(packed_values, "ctx", split_axis=0, concat_axis=0, tiled=True),
        lax.all_to_all(packed_gates, "ctx", split_axis=0, concat_axis=0, tiled=True),
        lax.all_to_all(packed_keys, "ctx", split_axis=0, concat_axis=0, tiled=True),
        lax.all_to_all(packed_queries, "ctx", split_axis=0, concat_axis=0, tiled=True),
        lax.all_to_all(packed_steps, "ctx", split_axis=0, concat_axis=0, tiled=True),
    )
    own_values = unpack_slots(received[0])
    own_gates = unpack_slots(received[1])
    own_keys = unpack_slots(received[2])
    own_queries = unpack_slots(received[3])
    own_steps = unpack_slots(received[4])
    rim_values, rim_keys, rim_queries = shifted_2(
        (
            own_values[token_count - rim_rows :],
            own_keys[token_count - rim_rows :],
            own_queries[token_count - rim_rows :],
        ),
        "ctx",
        1,
    )
    positions = (
        ctx_index * token_count - rim_rows + jnp.arange(token_count + rim_rows, dtype=jnp.int32)
    )
    doc_ext, open_ext = document_index(positions, doc_lengths)
    documents = doc_ext[rim_rows:]
    openings = open_ext[rim_rows:]
    conv_value = causal_conv(
        jnp.concatenate([rim_values, own_values], axis=0), conv_values, doc_ext
    )
    conv_key = causal_conv(jnp.concatenate([rim_keys, own_keys], axis=0), conv_keys, doc_ext)
    conv_query = causal_conv(
        jnp.concatenate([rim_queries, own_queries], axis=0), conv_queries, doc_ext
    )
    heads_local = own_steps.shape[1]
    groups_local = own_keys.shape[1] // STATE
    span_count = token_count // SPAN
    step_size = jax.nn.softplus(own_steps.astype(jnp.float32) + step_bias)
    rates = -jnp.exp(decay_log) * step_size
    value_rows = conv_value.reshape(span_count, SPAN, heads_local, HEAD_DIM)
    key_rows = conv_key.reshape(span_count, SPAN, groups_local, STATE)
    query_rows = conv_query.reshape(span_count, SPAN, groups_local, STATE)
    step_spans = step_size.reshape(span_count, SPAN, heads_local)
    decay_sums = jnp.cumsum(rates.reshape(span_count, SPAN, heads_local).transpose(0, 2, 1), axis=2)
    span_docs = documents.reshape(span_count, SPAN)
    span_openings = openings.reshape(span_count, SPAN)
    intra = jax.vmap(span_outputs)(
        value_rows, step_spans, key_rows, query_rows, decay_sums, span_docs
    )
    local_states, span_gates, inflows = jax.vmap(span_states)(
        value_rows, step_spans, key_rows, decay_sums, span_docs, span_openings
    )

    def advance(running, inputs):
        decay_product, accumulated = running
        span_state, span_gate = inputs
        advanced = (span_gate * decay_product, span_gate[:, None, None] * accumulated + span_state)
        return (advanced, running)

    start_carry = (
        jnp.ones((heads_local,), jnp.float32),
        jnp.zeros((heads_local, HEAD_DIM, STATE), jnp.float32),
    )
    summary, prefixes = lax.scan(advance, start_carry, (local_states, span_gates))

    def combine(earlier_part, later_part):
        return (
            earlier_part[0] * later_part[0],
            later_part[0][:, None, None] * earlier_part[1] + later_part[1],
        )

    incoming = carried_in(summary, "ctx", combine, start_carry)
    entering = prefixes[0][:, :, None, None] * incoming[1][None] + prefixes[1]
    entering, inflows = (entering, inflows)
    inter = jax.vmap(span_inflow)(query_rows, entering, inflows)
    mixed_rows = intra + inter + skip_gain[None, None, :, None] * value_rows.astype(jnp.float32)
    mixed_rows = mixed_rows.reshape(token_count, heads_local * HEAD_DIM)
    normed = gated_norm(mixed_rows, own_gates, norm_gain, groups_local)
    return lax.psum_scatter(
        jnp.dot(normed, out_weight, preferred_element_type=jnp.float32).astype(jnp.bfloat16),
        "tp",
        scatter_dimension=0,
        tiled=True,
    )


CHUNK = 128
LANES = 128


def tapped(current, previous, taps, since):
    row_count = current.shape[0]
    extended = jnp.concatenate([previous, current], axis=0)
    total = None
    for tap_index in range(CONV):
        steps = CONV - 1 - tap_index
        weight = taps[tap_index : tap_index + 1, :]
        if steps == 0:
            term = current * weight
        else:
            shifted = pltpu.roll(extended, steps, 0)[8 : 8 + row_count]
            term = jnp.where(since >= steps, shifted * weight, 0.0)
        total = term if total is None else total + term
    return silu(total)


def silu(x):
    half = 0.5 * x
    return half + half * jnp.tanh(half)


def mixing_kernel(
    heads,
    group_heads,
    per_dev,
    chunks_step,
    piece_count,
    me_ref,
    order_ref,
    lengths_ref,
    bias_ref,
    log_ref,
    key_taps_ref,
    query_taps_ref,
    *refs,
):
    piece_refs, refs = refs[:piece_count], refs[piece_count:]
    mix_ref, query_ref, key_ref, tail_ref, inflow_ref, gate_ref, since_ref = refs[:7]
    sequence, previous, raw_steps, step_rows, row_stack = refs[7:]
    groups = piece_refs[0].shape[0]
    me = me_ref[0]
    step_id = pl.program_id(0)
    token_rows = per_dev * BLK
    chunks = raw_steps.shape[0]

    @pl.when(step_id == 0)
    def _():
        previous[...] = jnp.zeros_like(previous)
        lane = lax.broadcasted_iota(jnp.int32, (8, LANES), 1)
        row8 = lax.broadcasted_iota(jnp.int32, (8, LANES), 0)
        own = lax.rem(me * heads, group_heads)
        for g in range(groups):
            for turn, piece_ref in enumerate(piece_refs):
                loader = jnp.bitwise_xor(me, g * piece_count + turn)
                for b in range(per_dev):
                    place = order_ref[loader * per_dev + b]
                    rows = pl.ds(pl.multiple_of(place * BLK, BLK), BLK)
                    sequence[rows, :] = piece_ref[g, b * BLK : (b + 1) * BLK, :]
                    at = (b // 2) * LANES
                    steps_in = piece_ref[
                        g, token_rows : token_rows + group_heads, at : at + LANES
                    ].astype(jnp.float32)
                    parity = lax.rem(place, 2)
                    steps_in = pltpu.roll(
                        steps_in, lax.rem(group_heads - own, group_heads), 0
                    )[:8]
                    steps_in = pltpu.roll(steps_in, BLK * jnp.bitwise_xor(parity, b % 2), 1)
                    chunk = lax.div(place, 2)
                    raw_steps[chunk] = jnp.where(
                        lane // BLK == parity, steps_in, raw_steps[chunk]
                    )
        bias = jnp.zeros((8, LANES), jnp.float32)
        decay = jnp.zeros((8, LANES), jnp.float32)
        for h in range(heads):
            bias = jnp.where(row8 == h, bias_ref[me * heads + h], bias)
            decay = jnp.where(row8 == h, log_ref[me * heads + h], decay)
        decay = -jnp.exp(decay)
        raw = jnp.where(row8[None] < heads, raw_steps[...] + bias[None], 0.0)
        step = jnp.maximum(raw, 0.0) + jnp.log(1.0 + jnp.exp(-jnp.abs(raw)))
        step_rows[...] = step
        sums = decay[None] * step
        lanes = lax.broadcasted_iota(jnp.int32, (chunks, 8, LANES), 2)
        width = 1
        while width < CHUNK:
            sums = sums + jnp.where(lanes >= width, pltpu.roll(sums, width, 2), 0.0)
            width *= 2
        first = lax.broadcasted_iota(jnp.int32, (chunks, 8, LANES), 0) * CHUNK
        position = first + lanes
        begun = jnp.zeros_like(position)
        offset = jnp.int32(0)
        for k in range(lengths_ref.shape[0]):
            begun = jnp.where(position >= offset, offset, begun)
            offset = offset + lengths_ref[k]
        last_sum = jnp.sum(jnp.where(lanes == CHUNK - 1, sums, 0.0), axis=2, keepdims=True)
        last_begun = jnp.max(begun, axis=2, keepdims=True)
        row_stack[:, 0:8] = sums
        row_stack[:, 8:16] = jnp.where(
            position >= last_begun, jnp.exp(last_sum - sums) * step, 0.0
        )
        row_stack[:, 16:24] = jnp.where(begun < first, jnp.exp(sums), 0.0)
        row_stack[:, 24:32] = (position - begun).astype(jnp.float32)
        row_stack[:, 32:40] = jnp.where(
            last_begun < first, jnp.exp(last_sum), jnp.zeros_like(sums)
        )

    causal = lax.broadcasted_iota(jnp.int32, (CHUNK, CHUNK), 0) >= lax.broadcasted_iota(
        jnp.int32, (CHUNK, CHUNK), 1
    )
    column = lax.broadcasted_iota(jnp.int32, (CHUNK, CHUNK), 1).astype(jnp.float32)
    row_of = lax.broadcasted_iota(jnp.int32, (CHUNK, CHUNK), 0).astype(jnp.float32)
    low_half = lax.broadcasted_iota(jnp.int32, (CHUNK, LANES), 1) < HEAD_DIM
    taps = jnp.concatenate([key_taps_ref[...], query_taps_ref[...]], axis=1)

    def one_chunk(local, carry):
        chunk = step_id * chunks_step + local
        turned = jnp.concatenate(
            [row_stack[chunk, :32], jnp.zeros((CHUNK - 32, LANES), jnp.float32)], axis=0
        ).T

        def spread(at):
            return jnp.broadcast_to(turned[:, at : at + 1], (CHUNK, LANES))

        since_rows = spread(24)
        since_ref[local] = since_rows
        rows = pl.ds(pl.multiple_of(chunk * CHUNK, CHUNK), CHUNK)
        current = sequence[rows, :].astype(jnp.float32)
        wide_since = jnp.concatenate([since_rows, since_rows], axis=1)
        conv = tapped(current, previous[...], taps, wide_since)
        previous[...] = current[CHUNK - 8 :]
        keys, queries = conv[:, :STATE].astype(jnp.bfloat16), conv[:, STATE:].astype(jnp.bfloat16)
        query_ref[local] = queries
        key_ref[local] = conv[:, :STATE].T.astype(jnp.bfloat16)
        inner_products = lax.dot_general(
            queries, keys, (((1,), (1,)), ((), ())), preferred_element_type=jnp.float32
        )
        allowed = jnp.where(causal & (column >= row_of - since_rows), 0.0, -1e30)
        for h in range(heads):
            exponent = (spread(h) + allowed) - row_stack[chunk, h : h + 1, :]
            weights = jnp.exp(exponent) * (inner_products * step_rows[chunk, h : h + 1, :])
            mix_ref[local, :, h * CHUNK : (h + 1) * CHUNK] = weights.astype(jnp.bfloat16)
        gate = row_stack[chunk, 32:40]
        for pair in range(heads // 2):
            at = slice(pair * LANES, (pair + 1) * LANES)
            tail_ref[local, :, at] = jnp.where(
                low_half, spread(8 + 2 * pair), spread(9 + 2 * pair)
            )
            inflow_ref[local, :, at] = jnp.where(
                low_half, spread(16 + 2 * pair), spread(17 + 2 * pair)
            )
            gate_ref[local, :, at] = jnp.where(
                low_half[:8],
                jnp.broadcast_to(gate[2 * pair : 2 * pair + 1], (8, LANES)),
                jnp.broadcast_to(gate[2 * pair + 1 : 2 * pair + 2], (8, LANES)),
            )
        return carry

    lax.fori_loop(0, chunks_step, one_chunk, 0, unroll=2)


def scan_kernel(heads, per_dev, turns, place_ref, order_ref, skip_ref, taps_ref, *refs):
    piece_refs, refs = refs[: len(turns)], refs[len(turns) :]
    mix_ref, query_ref, key_ref, tail_ref, inflow_ref, gate_ref, since_ref = refs[:7]
    out_refs, (sequence, gates, laid, previous, state) = refs[7:-5], refs[-5:]
    me, mine = place_ref[0], place_ref[1]
    previous[...] = jnp.zeros_like(previous)
    state[...] = jnp.zeros_like(state)
    for turn, piece_ref in zip(turns, piece_refs):
        loader = jnp.bitwise_xor(me, turn)
        for b in range(per_dev):
            place = order_ref[loader * per_dev + b]
            rows = pl.ds(pl.multiple_of(place * BLK, BLK), BLK)
            sequence[rows, :] = piece_ref[0, b * BLK : (b + 1) * BLK, :]
            gates[rows, :] = piece_ref[1, b * BLK : (b + 1) * BLK, :]
    width = heads * HEAD_DIM
    lane = lax.broadcasted_iota(jnp.int32, (1, width), 1)
    skip = jnp.zeros((1, width), jnp.float32)
    for h in range(heads):
        skip = jnp.where(lane >= h * HEAD_DIM, skip_ref[me * heads + h], skip)
    low_half = lax.broadcasted_iota(jnp.int32, (CHUNK, LANES), 1) < HEAD_DIM
    taps = taps_ref[...]
    blocks = CHUNK // BLK

    def one_chunk(chunk, carry):
        rows = pl.ds(pl.multiple_of(chunk * CHUNK, CHUNK), CHUNK)
        current = sequence[rows, :].astype(jnp.float32)
        wide_since = jnp.concatenate([since_ref[chunk]] * (width // LANES), axis=1)
        values = tapped(current, previous[...], taps, wide_since).astype(jnp.bfloat16)
        previous[...] = current[CHUNK - 8 :]
        values_wide = values.astype(jnp.float32)
        entering = state[...]
        carried = jnp.dot(
            query_ref[chunk], entering.astype(jnp.bfloat16), preferred_element_type=jnp.float32
        )
        total = carried * inflow_ref[chunk] + skip * values_wide
        tail_values = (values_wide * tail_ref[chunk]).astype(jnp.bfloat16)
        state[...] = gate_ref[chunk, :1, :] * entering + jnp.dot(
            key_ref[chunk], tail_values, preferred_element_type=jnp.float32
        )
        zero = jnp.zeros((CHUNK, LANES), jnp.bfloat16)
        intra = []
        for pair in range(heads // 2):
            both = values[:, pair * LANES : (pair + 1) * LANES]
            block = jnp.concatenate(
                [jnp.where(low_half, both, zero), jnp.where(low_half, zero, both)], axis=0
            )
            weights = mix_ref[chunk, :, 2 * pair * CHUNK : 2 * (pair + 1) * CHUNK]
            intra.append(jnp.dot(weights, block, preferred_element_type=jnp.float32))
        mixed = total + jnp.concatenate(intra, axis=1)
        gated = (mixed * silu(gates[rows, :].astype(jnp.float32))).astype(jnp.bfloat16)
        for block in range(blocks):
            place = chunk * blocks + block
            away = jnp.bitwise_xor(lax.rem(place, per_dev), mine)
            slot = 2 * (1 - lax.rem(away, 2)) + (1 - lax.div(away, 2))
            start = pl.multiple_of(slot * BLK, BLK)
            laid[lax.div(place, per_dev), pl.ds(start, BLK), :] = gated[
                block * BLK : (block + 1) * BLK
            ]
        return carry

    lax.fori_loop(0, mix_ref.shape[0], one_chunk, 0, unroll=2)
    for turn, out_ref in zip(turns, out_refs):
        out_ref[...] = laid[jnp.bitwise_xor(me, turn)]


def normed_into(normed, gated_refs, gain_ref, me, first_turn):
    count = len(gated_refs)
    rows, width = gated_refs[0].shape
    wide = [ref[...].astype(jnp.float32) for ref in gated_refs]
    squares = wide[0] * wide[0]
    for piece in wide[1:]:
        squares = squares + piece * piece
    mean = jnp.sum(squares, axis=1, keepdims=True) * (1.0 / (count * width))
    inverse_rms = lax.rsqrt(mean + 1e-05)
    for turn, piece in enumerate(wide):
        source = jnp.bitwise_xor(me, first_turn + turn)
        at = pl.multiple_of(lax.rem(source, count) * width, width)
        gain = gain_ref[pl.ds(source, 1), :]
        normed[:, pl.ds(at, width)] = (piece * inverse_rms * gain).astype(jnp.bfloat16)


def weight_tiles(weight_ref, group, buffer, sems, count):
    tile = buffer.shape[1] // count
    tiles = [slice(i * tile, (i + 1) * tile) for i in range(count)]
    return tiles, [
        pltpu.make_async_copy(weight_ref.at[group, :, at], buffer.at[:, at], sems.at[i])
        for i, at in enumerate(tiles)
    ]


def near_kernel(place_ref, gain_ref, weight_ref, *refs):
    gated_refs, (partial_ref, next_ref, normed, buffer, sems) = refs[:-5], refs[-5:]
    count = sems.shape[0] - 1
    group = lax.div(place_ref[0], len(gated_refs))
    tiles, copies = weight_tiles(weight_ref, group, buffer, sems, count)
    onward = pltpu.make_async_copy(weight_ref.at[1 - group], next_ref, sems.at[count])
    for copy in copies + [onward]:
        copy.start()
    normed_into(normed, gated_refs, gain_ref, place_ref[0], 0)
    for at, copy in zip(tiles, copies):
        copy.wait()
        partial_ref[:, at] = jnp.dot(
            normed[...], buffer[:, at], preferred_element_type=jnp.float32
        )
    onward.wait()


def project_far(normed, weight_ref, near_ref, at, away_ref, stay_ref):
    partial = near_ref[:, at] + jnp.dot(
        normed, weight_ref[:, at], preferred_element_type=jnp.float32
    )
    partial = partial.astype(jnp.bfloat16)
    rows = partial.shape[0] // 2
    away_ref[...] = partial[:rows]
    stay_ref[...] = partial[rows:]


def far_kernel(place_ref, gain_ref, weight_ref, near_ref, *refs):
    gated_refs, (away_ref, stay_ref, normed) = refs[:-3], refs[-3:]
    normed_into(normed, gated_refs, gain_ref, place_ref[0], len(gated_refs))
    at = slice(0, away_ref.shape[1])
    project_far(normed[...], weight_ref, near_ref, at, away_ref, stay_ref)


def rest_kernel(place_ref, normed_ref, weight_ref, near_ref, away_ref, stay_ref):
    at = slice(near_ref.shape[1] - away_ref.shape[1], near_ref.shape[1])
    project_far(normed_ref[...], weight_ref, near_ref, at, away_ref, stay_ref)


def head_split(
    values_in,
    gate_in,
    keys_in,
    queries_in,
    step_in,
    block_order,
    doc_lengths,
    conv_values,
    conv_keys,
    conv_queries,
    decay_log,
    step_bias,
    skip_gain,
    norm_gain,
    out_weight,
):
    ctx_count = lax.axis_size("ctx")
    tp_count = lax.axis_size("tp")
    me = lax.axis_index("ctx")
    tp_index = lax.axis_index("tp")
    token_count, channels = values_in.shape
    per_dev = token_count // BLK
    total_tokens = token_count * ctx_count
    heads_local = step_in.shape[1]
    heads = heads_local // ctx_count
    width = heads * HEAD_DIM
    groups = keys_in.shape[1] // STATE
    group_heads = heads_local // groups
    near = ctx_count // groups
    chunks = total_tokens // CHUNK
    my_group = me // near
    place = jnp.stack([me, tp_index]).astype(jnp.int32)

    def turned(value, turn):
        return lax.ppermute(value, "ctx", [(i, i ^ turn) for i in range(ctx_count)])

    def for_group(group):
        keys = lax.dynamic_slice_in_dim(keys_in, group * STATE, STATE, 1)
        queries = lax.dynamic_slice_in_dim(queries_in, group * STATE, STATE, 1)
        steps = lax.dynamic_slice_in_dim(step_in, group * group_heads, group_heads, 1)
        return jnp.concatenate([jnp.concatenate([keys, queries], axis=1), steps.T], axis=0)

    def for_heads(turn):
        at = (me ^ turn) * width
        return jnp.stack(
            [lax.dynamic_slice_in_dim(rows, at, width, 1) for rows in (values_in, gate_in)]
        )

    held = jnp.stack([for_group(my_group), turned(for_group(my_group ^ 1), near)])
    group_rows = [held] + [turned(held, turn) for turn in range(1, near)]
    turns = (0, 1, 2, 3, 4, 5, 6, 7)
    head_rows = [turned(for_heads(turn), turn) if turn else for_heads(turn) for turn in turns]

    key_taps = lax.dynamic_slice_in_dim(conv_keys, my_group * STATE, STATE, 1)
    query_taps = lax.dynamic_slice_in_dim(conv_queries, my_group * STATE, STATE, 1)
    value_taps = lax.dynamic_slice_in_dim(conv_values, me * width, width, 1)

    smem = pl.BlockSpec(memory_space=pltpu.SMEM)
    vmem = pl.BlockSpec(memory_space=pltpu.VMEM)
    params = pltpu.CompilerParams(vmem_limit_bytes=28 * 1024 * 1024)

    def whole(array):
        return pl.BlockSpec(array.shape, lambda *ids: (0,) * array.ndim)

    grid_steps = 4
    chunks_step = chunks // grid_steps

    def per_step(rows, columns):
        return pl.BlockSpec((chunks_step, rows, columns), lambda i: (i, 0, 0))

    mix_shapes = [
        ((CHUNK, heads * CHUNK), jnp.bfloat16),
        ((CHUNK, STATE), jnp.bfloat16),
        ((STATE, CHUNK), jnp.bfloat16),
        ((CHUNK, width), jnp.float32),
        ((CHUNK, width), jnp.float32),
        ((8, width), jnp.float32),
        ((CHUNK, LANES), jnp.float32),
    ]
    mixing = pl.pallas_call(
        functools.partial(mixing_kernel, heads, group_heads, per_dev, chunks_step, near),
        grid=(grid_steps,),
        in_specs=[smem] * 5 + [whole(key_taps), whole(query_taps)] + [whole(held)] * near,
        out_specs=[per_step(*shape) for shape, _ in mix_shapes],
        out_shape=[jax.ShapeDtypeStruct((chunks,) + shape, kind) for shape, kind in mix_shapes],
        scratch_shapes=[
            pltpu.VMEM((total_tokens, 2 * STATE), jnp.bfloat16),
            pltpu.VMEM((8, 2 * STATE), jnp.float32),
            pltpu.VMEM((chunks, 8, LANES), jnp.float32),
            pltpu.VMEM((chunks, 8, LANES), jnp.float32),
            pltpu.VMEM((chunks, 40, LANES), jnp.float32),
        ],
        compiler_params=params,
        cost_estimate=pl.CostEstimate(
            flops=20_000_000, bytes_accessed=20_000_000, transcendentals=2_000_000
        ),
        name="mixing",
    )(place, block_order, doc_lengths, step_bias, decay_log, key_taps, query_taps, *group_rows)

    gated = pl.pallas_call(
        functools.partial(scan_kernel, heads, per_dev, turns),
        in_specs=[smem] * 3 + [vmem] * (1 + ctx_count + len(mix_shapes)),
        out_specs=[vmem] * ctx_count,
        out_shape=[jax.ShapeDtypeStruct((token_count, width), jnp.bfloat16)] * ctx_count,
        scratch_shapes=[
            pltpu.VMEM((total_tokens, width), jnp.bfloat16),
            pltpu.VMEM((total_tokens, width), jnp.bfloat16),
            pltpu.VMEM((ctx_count, token_count, width), jnp.bfloat16),
            pltpu.VMEM((8, width), jnp.float32),
            pltpu.VMEM((STATE, width), jnp.float32),
        ],
        compiler_params=params,
        cost_estimate=pl.CostEstimate(
            flops=600_000_000, bytes_accessed=14_000_000, transcendentals=1_200_000
        ),
        name="scan",
    )(place, block_order, skip_gain, value_taps, *head_rows, *mixing)
    gated = dict(zip(turns, gated))

    pieces = [gated[0]] + [turned(gated[turn], turn) for turn in range(1, ctx_count)]

    columns = out_weight.shape[1]
    group_width = near * width
    gain = norm_gain.reshape(ctx_count, width)
    weight = out_weight.reshape(groups, group_width, columns)

    def project(kernel, first, weight, weight_space, operands, out_shape, scratch, limit, name):
        return pl.pallas_call(
            kernel,
            in_specs=[smem, vmem, pl.BlockSpec(memory_space=weight_space)] + [vmem] * len(operands),
            out_specs=[vmem] * len(out_shape),
            out_shape=out_shape,
            scratch_shapes=scratch,
            compiler_params=pltpu.CompilerParams(vmem_limit_bytes=limit * 1024 * 1024),
            cost_estimate=pl.CostEstimate(
                flops=2 * token_count * group_width * columns,
                bytes_accessed=2 * group_width * columns,
                transcendentals=0,
            ),
            name=name,
        )(place, first, weight, *operands)

    near_partial, far_weight = project(
        near_kernel,
        gain,
        weight,
        pl.ANY,
        pieces[:near],
        [
            jax.ShapeDtypeStruct((token_count, columns), jnp.float32),
            jax.ShapeDtypeStruct((group_width, columns), jnp.bfloat16),
        ],
        [
            pltpu.VMEM((token_count, group_width), jnp.bfloat16),
            pltpu.VMEM((group_width, columns), jnp.bfloat16),
            pltpu.SemaphoreType.DMA((5,)),
        ],
        28,
        "near_projection",
    )
    rows = token_count // 2
    normed_shape = jax.ShapeDtypeStruct((token_count, group_width), jnp.bfloat16)

    def part_shape(part_columns):
        return jax.ShapeDtypeStruct((rows, part_columns), jnp.bfloat16)

    first_columns = columns // 2
    away, stay, far_normed = project(
        far_kernel,
        gain,
        far_weight,
        pltpu.VMEM,
        [near_partial] + pieces[near:],
        [part_shape(first_columns)] * 2 + [normed_shape],
        [],
        8,
        "far_projection",
    )
    rest_away, rest_stay = project(
        rest_kernel,
        far_normed,
        far_weight,
        pltpu.VMEM,
        [near_partial],
        [part_shape(columns - first_columns)] * 2,
        [],
        8,
        "rest_projection",
    )

    def joined(kept, sent, turn):
        came = lax.ppermute(sent, "tp", [(i, i ^ turn) for i in range(tp_count)])
        return (kept.astype(jnp.float32) + came.astype(jnp.float32)).astype(jnp.bfloat16)

    results = []
    for away, stay in ((away, stay), (rest_away, rest_stay)):
        across = joined(stay, away, 1)
        results.append(joined(across[rows // 2 :], across[: rows // 2], 2))
    return jnp.concatenate(results, axis=1)


def on_mesh(*arrays):
    ctx_count, tp_count = lax.axis_size("ctx"), lax.axis_size("tp")
    groups = arrays[2].shape[1] // STATE
    heads_local = arrays[4].shape[1]
    fits = (
        groups == 2
        and tp_count == 4
        and ctx_count & (ctx_count - 1) == 0
        and heads_local % (2 * ctx_count) == 0
        and heads_local // ctx_count <= 8
        and arrays[0].shape[0] == 2 * STATE
    )
    return (head_split if fits else on_device)(*arrays)


def solution(mesh):
    in_specs = (
        P("ctx", "tp"),
        P("ctx", "tp"),
        P("ctx", "tp"),
        P("ctx", "tp"),
        P("ctx", "tp"),
        P(),
        P(),
        P(None, "tp"),
        P(None, "tp"),
        P(None, "tp"),
        P("tp"),
        P("tp"),
        P("tp"),
        P("tp"),
        P("tp", None),
    )
    out_specs = P(("ctx", "tp"), None)
    return jax.shard_map(
        on_mesh, mesh=mesh, in_specs=in_specs, out_specs=out_specs, check_vma=False
    )
```

```python
import functools

import jax
import jax.numpy as jnp
from jax import lax
from jax.experimental import pallas as pl
from jax.experimental.pallas import tpu as pltpu
from jax.sharding import PartitionSpec as P

HEAD_DIM = 64
STATE = 128
CONV = 4
SPAN = 256
BLK = 64


def shifted_2(value, axis, steps):
    count = lax.axis_size(axis)
    leading, last = (max(0, -steps), min(count, count - steps))
    return lax.ppermute(value, axis, [(source, source + steps) for source in range(leading, last)])


def carried_in(shard, axis, join, neutral):
    place = lax.axis_index(axis)
    gathered = jax.tree.map(
        lambda a, kind: lax.all_gather(a.astype(kind), axis),
        shard,
        jax.tree.map(lambda a: jnp.bfloat16 if a.dtype == jnp.float32 else a.dtype, shard),
    )
    state = jax.tree.map(lambda a, e: jnp.zeros_like(a) + jnp.asarray(e, a.dtype), shard, neutral)

    def one(turn, state):
        return join(
            state,
            jax.tree.map(
                lambda a, own: lax.dynamic_index_in_dim(a, turn, 0, False).astype(own.dtype),
                gathered,
                shard,
            ),
        )

    return lax.fori_loop(0, place, one, state)


def document_index(positions, doc_lengths):
    offsets = jnp.cumsum(doc_lengths) - doc_lengths
    below_start = offsets[None, :] <= positions[:, None]
    documents = jnp.sum(below_start.astype(jnp.int32), axis=1, dtype=jnp.int32) - 1
    openings = jnp.any(offsets[None, :] == positions[:, None], axis=1).astype(jnp.int32)
    return (documents, openings)


def causal_conv(extended, weight, doc_ext):
    tap_count = weight.shape[0]
    row_count = extended.shape[0] - tap_count + 1
    current = doc_ext[tap_count - 1 :]
    accumulated = jnp.zeros((row_count, extended.shape[1]), jnp.float32)
    for tap_index in range(tap_count):
        keep_rows = (doc_ext[tap_index : tap_index + row_count] == current)[:, None]
        shifted = (
            extended[tap_index : tap_index + row_count].astype(jnp.float32) * weight[tap_index]
        )
        accumulated = accumulated + jnp.where(keep_rows, shifted, 0.0)
    return lax.optimization_barrier(jax.nn.silu(accumulated).astype(jnp.bfloat16))


def span_outputs(value_rows, step_rows, key_rows, query_rows, decay_sums, documents):
    row_count = value_rows.shape[0]
    per_group = value_rows.shape[1] // key_rows.shape[1]
    row_ids = jnp.arange(row_count, dtype=jnp.int32)
    keep_mask = (documents[:, None] == documents[None, :]) & (row_ids[None, :] <= row_ids[:, None])
    differences = decay_sums[:, :, None] - decay_sums[:, None, :]
    decays = jnp.where(keep_mask[None], jnp.exp(jnp.minimum(differences, 0.0)), 0.0)
    inner_products = jnp.einsum(
        "ign,jgn->gij", query_rows, key_rows, preferred_element_type=jnp.float32
    )
    weighted = (
        decays * jnp.repeat(inner_products, per_group, axis=0) * step_rows.T[:, None, :]
    ).astype(jnp.bfloat16)
    return jnp.einsum("hij,jhp->ihp", weighted, value_rows, preferred_element_type=jnp.float32)


def span_states(value_rows, step_rows, key_rows, decay_sums, documents, openings):
    per_group = value_rows.shape[1] // key_rows.shape[1]
    tail_decay = jnp.where(
        (documents == documents[-1])[None, :], jnp.exp(decay_sums[:, -1:] - decay_sums), 0.0
    )
    tail_weight = tail_decay.T * step_rows
    head_keys = jnp.repeat(key_rows, per_group, axis=1)
    tail_keys = (tail_weight[:, :, None] * head_keys.astype(jnp.float32)).astype(jnp.bfloat16)
    local_state = jnp.einsum(
        "jhp,jhn->hpn", value_rows, tail_keys, preferred_element_type=jnp.float32
    )
    opened = jnp.cumsum(openings)
    span_gate = jnp.where(opened[-1] == 0, jnp.exp(decay_sums[:, -1]), 0.0)
    inflow = jnp.where((opened == 0)[None, :], jnp.exp(decay_sums), 0.0)
    return (local_state, span_gate, inflow)


def span_inflow(query_rows, entering, inflow):
    per_group = entering.shape[0] // query_rows.shape[1]
    head_queries = jnp.repeat(query_rows.astype(jnp.float32), per_group, axis=1)
    carried = jnp.einsum("ihn,hpn->ihp", head_queries, entering, precision=lax.Precision.HIGHEST)
    return carried * inflow.T[:, :, None]


def gated_norm(mixed_rows, gate_rows, norm_gain, groups_local):
    gated_rows = mixed_rows * jax.nn.silu(gate_rows.astype(jnp.float32))
    grouped = gated_rows.reshape(gated_rows.shape[0], groups_local, -1)
    inverse_rms = lax.rsqrt(jnp.mean(grouped * grouped, axis=2, keepdims=True) + 1e-05)
    return ((grouped * inverse_rms).reshape(gated_rows.shape) * norm_gain).astype(jnp.bfloat16)


def on_device(
    values_in,
    gate_in,
    keys_in,
    queries_in,
    step_in,
    block_order,
    doc_lengths,
    conv_values,
    conv_keys,
    conv_queries,
    decay_log,
    step_bias,
    skip_gain,
    norm_gain,
    out_weight,
):
    ctx_count = lax.axis_size("ctx")
    ctx_index = lax.axis_index("ctx")
    token_count = values_in.shape[0]
    per_dev = token_count // BLK
    capacity = (per_dev + ctx_count - 1) // ctx_count
    rim_rows = CONV - 1
    pos_table = block_order.reshape(ctx_count, per_dev)
    owner_of = pos_table // per_dev
    local_ids = jnp.arange(per_dev, dtype=jnp.int32)
    earlier = local_ids[None, :] < local_ids[:, None]
    same_owner = owner_of[:, :, None] == owner_of[:, None, :]
    slot_rank = jnp.sum((same_owner & earlier[None]).astype(jnp.int32), axis=2, dtype=jnp.int32)
    my_owner = lax.dynamic_index_in_dim(owner_of, ctx_index, 0, keepdims=False)
    my_rank = lax.dynamic_index_in_dim(slot_rank, ctx_index, 0, keepdims=False)
    slot_ids = jnp.arange(ctx_count * capacity, dtype=jnp.int32)
    slot_hit = (my_owner * capacity + my_rank)[None, :] == slot_ids[:, None]
    source = jnp.sum(jnp.where(slot_hit, local_ids[None, :], 0), axis=1, dtype=jnp.int32)
    filled = jnp.any(slot_hit, axis=1)

    def pack_slots(local_rows):
        blocks = local_rows.reshape(per_dev, BLK, local_rows.shape[1])
        picked = jnp.where(filled[:, None, None], blocks[source], jnp.zeros((), local_rows.dtype))
        return picked

    all_slots = (jnp.arange(ctx_count, dtype=jnp.int32)[:, None] * capacity + slot_rank).reshape(-1)
    wanted = ctx_index * per_dev + local_ids
    owner_hit = block_order[None, :] == wanted[:, None]
    pick_slot = jnp.sum(jnp.where(owner_hit, all_slots[None, :], 0), axis=1, dtype=jnp.int32)

    def unpack_slots(received):
        return received[pick_slot].reshape(token_count, received.shape[2])

    packed_values = pack_slots(values_in)
    packed_gates = pack_slots(gate_in)
    packed_keys = pack_slots(keys_in)
    packed_queries = pack_slots(queries_in)
    packed_steps = pack_slots(step_in)
    received = (
        lax.all_to_all(packed_values, "ctx", split_axis=0, concat_axis=0, tiled=True),
        lax.all_to_all(packed_gates, "ctx", split_axis=0, concat_axis=0, tiled=True),
        lax.all_to_all(packed_keys, "ctx", split_axis=0, concat_axis=0, tiled=True),
        lax.all_to_all(packed_queries, "ctx", split_axis=0, concat_axis=0, tiled=True),
        lax.all_to_all(packed_steps, "ctx", split_axis=0, concat_axis=0, tiled=True),
    )
    own_values = unpack_slots(received[0])
    own_gates = unpack_slots(received[1])
    own_keys = unpack_slots(received[2])
    own_queries = unpack_slots(received[3])
    own_steps = unpack_slots(received[4])
    rim_values, rim_keys, rim_queries = shifted_2(
        (
            own_values[token_count - rim_rows :],
            own_keys[token_count - rim_rows :],
            own_queries[token_count - rim_rows :],
        ),
        "ctx",
        1,
    )
    positions = (
        ctx_index * token_count - rim_rows + jnp.arange(token_count + rim_rows, dtype=jnp.int32)
    )
    doc_ext, open_ext = document_index(positions, doc_lengths)
    documents = doc_ext[rim_rows:]
    openings = open_ext[rim_rows:]
    conv_value = causal_conv(
        jnp.concatenate([rim_values, own_values], axis=0), conv_values, doc_ext
    )
    conv_key = causal_conv(jnp.concatenate([rim_keys, own_keys], axis=0), conv_keys, doc_ext)
    conv_query = causal_conv(
        jnp.concatenate([rim_queries, own_queries], axis=0), conv_queries, doc_ext
    )
    heads_local = own_steps.shape[1]
    groups_local = own_keys.shape[1] // STATE
    span_count = token_count // SPAN
    step_size = jax.nn.softplus(own_steps.astype(jnp.float32) + step_bias)
    rates = -jnp.exp(decay_log) * step_size
    value_rows = conv_value.reshape(span_count, SPAN, heads_local, HEAD_DIM)
    key_rows = conv_key.reshape(span_count, SPAN, groups_local, STATE)
    query_rows = conv_query.reshape(span_count, SPAN, groups_local, STATE)
    step_spans = step_size.reshape(span_count, SPAN, heads_local)
    decay_sums = jnp.cumsum(rates.reshape(span_count, SPAN, heads_local).transpose(0, 2, 1), axis=2)
    span_docs = documents.reshape(span_count, SPAN)
    span_openings = openings.reshape(span_count, SPAN)
    intra = jax.vmap(span_outputs)(
        value_rows, step_spans, key_rows, query_rows, decay_sums, span_docs
    )
    local_states, span_gates, inflows = jax.vmap(span_states)(
        value_rows, step_spans, key_rows, decay_sums, span_docs, span_openings
    )

    def advance(running, inputs):
        decay_product, accumulated = running
        span_state, span_gate = inputs
        advanced = (span_gate * decay_product, span_gate[:, None, None] * accumulated + span_state)
        return (advanced, running)

    start_carry = (
        jnp.ones((heads_local,), jnp.float32),
        jnp.zeros((heads_local, HEAD_DIM, STATE), jnp.float32),
    )
    summary, prefixes = lax.scan(advance, start_carry, (local_states, span_gates))

    def combine(earlier_part, later_part):
        return (
            earlier_part[0] * later_part[0],
            later_part[0][:, None, None] * earlier_part[1] + later_part[1],
        )

    incoming = carried_in(summary, "ctx", combine, start_carry)
    entering = prefixes[0][:, :, None, None] * incoming[1][None] + prefixes[1]
    entering, inflows = (entering, inflows)
    inter = jax.vmap(span_inflow)(query_rows, entering, inflows)
    mixed_rows = intra + inter + skip_gain[None, None, :, None] * value_rows.astype(jnp.float32)
    mixed_rows = mixed_rows.reshape(token_count, heads_local * HEAD_DIM)
    normed = gated_norm(mixed_rows, own_gates, norm_gain, groups_local)
    return lax.psum_scatter(
        jnp.dot(normed, out_weight, preferred_element_type=jnp.float32).astype(jnp.bfloat16),
        "tp",
        scatter_dimension=0,
        tiled=True,
    )


CHUNK = 128
LANES = 128


def tapped(current, previous, taps, since):
    row_count = current.shape[0]
    extended = jnp.concatenate([previous, current], axis=0)
    total = None
    for tap_index in range(CONV):
        steps = CONV - 1 - tap_index
        weight = taps[tap_index : tap_index + 1, :]
        if steps == 0:
            term = current * weight
        else:
            shifted = pltpu.roll(extended, steps, 0)[8 : 8 + row_count]
            term = jnp.where(since >= steps, shifted * weight, 0.0)
        total = term if total is None else total + term
    return silu(total)


def silu(x):
    half = 0.5 * x
    return half + half * jnp.tanh(half)


def mixing_kernel(
    heads,
    group_heads,
    per_dev,
    chunks_step,
    piece_count,
    me_ref,
    order_ref,
    lengths_ref,
    bias_ref,
    log_ref,
    key_taps_ref,
    query_taps_ref,
    *refs,
):
    piece_refs, refs = refs[:piece_count], refs[piece_count:]
    mix_ref, query_ref, key_ref, tail_ref, inflow_ref, gate_ref, since_ref = refs[:7]
    sequence, previous, raw_steps, step_rows, row_stack = refs[7:]
    groups = piece_refs[0].shape[0]
    me = me_ref[0]
    step_id = pl.program_id(0)
    token_rows = per_dev * BLK
    chunks = raw_steps.shape[0]

    @pl.when(step_id == 0)
    def _():
        previous[...] = jnp.zeros_like(previous)
        lane = lax.broadcasted_iota(jnp.int32, (8, LANES), 1)
        row8 = lax.broadcasted_iota(jnp.int32, (8, LANES), 0)
        own = lax.rem(me * heads, group_heads)
        for g in range(groups):
            for turn, piece_ref in enumerate(piece_refs):
                loader = jnp.bitwise_xor(me, g * piece_count + turn)
                for b in range(per_dev):
                    place = order_ref[loader * per_dev + b]
                    rows = pl.ds(pl.multiple_of(place * BLK, BLK), BLK)
                    sequence[rows, :] = piece_ref[g, b * BLK : (b + 1) * BLK, :]
                    at = (b // 2) * LANES
                    steps_in = piece_ref[
                        g, token_rows : token_rows + group_heads, at : at + LANES
                    ].astype(jnp.float32)
                    parity = lax.rem(place, 2)
                    steps_in = pltpu.roll(
                        steps_in, lax.rem(group_heads - own, group_heads), 0
                    )[:8]
                    steps_in = pltpu.roll(steps_in, BLK * jnp.bitwise_xor(parity, b % 2), 1)
                    chunk = lax.div(place, 2)
                    raw_steps[chunk] = jnp.where(
                        lane // BLK == parity, steps_in, raw_steps[chunk]
                    )
        bias = jnp.zeros((8, LANES), jnp.float32)
        decay = jnp.zeros((8, LANES), jnp.float32)
        for h in range(heads):
            bias = jnp.where(row8 == h, bias_ref[me * heads + h], bias)
            decay = jnp.where(row8 == h, log_ref[me * heads + h], decay)
        decay = -jnp.exp(decay)
        raw = jnp.where(row8[None] < heads, raw_steps[...] + bias[None], 0.0)
        step = jnp.maximum(raw, 0.0) + jnp.log(1.0 + jnp.exp(-jnp.abs(raw)))
        step_rows[...] = step
        sums = decay[None] * step
        lanes = lax.broadcasted_iota(jnp.int32, (chunks, 8, LANES), 2)
        width = 1
        while width < CHUNK:
            sums = sums + jnp.where(lanes >= width, pltpu.roll(sums, width, 2), 0.0)
            width *= 2
        first = lax.broadcasted_iota(jnp.int32, (chunks, 8, LANES), 0) * CHUNK
        position = first + lanes
        begun = jnp.zeros_like(position)
        offset = jnp.int32(0)
        for k in range(lengths_ref.shape[0]):
            begun = jnp.where(position >= offset, offset, begun)
            offset = offset + lengths_ref[k]
        last_sum = jnp.sum(jnp.where(lanes == CHUNK - 1, sums, 0.0), axis=2, keepdims=True)
        last_begun = jnp.max(begun, axis=2, keepdims=True)
        row_stack[:, 0:8] = sums
        row_stack[:, 8:16] = jnp.where(
            position >= last_begun, jnp.exp(last_sum - sums) * step, 0.0
        )
        row_stack[:, 16:24] = jnp.where(begun < first, jnp.exp(sums), 0.0)
        row_stack[:, 24:32] = (position - begun).astype(jnp.float32)
        row_stack[:, 32:40] = jnp.where(
            last_begun < first, jnp.exp(last_sum), jnp.zeros_like(sums)
        )

    causal = lax.broadcasted_iota(jnp.int32, (CHUNK, CHUNK), 0) >= lax.broadcasted_iota(
        jnp.int32, (CHUNK, CHUNK), 1
    )
    column = lax.broadcasted_iota(jnp.int32, (CHUNK, CHUNK), 1).astype(jnp.float32)
    row_of = lax.broadcasted_iota(jnp.int32, (CHUNK, CHUNK), 0).astype(jnp.float32)
    low_half = lax.broadcasted_iota(jnp.int32, (CHUNK, LANES), 1) < HEAD_DIM
    taps = jnp.concatenate([key_taps_ref[...], query_taps_ref[...]], axis=1)

    def one_chunk(local, carry):
        chunk = step_id * chunks_step + local
        turned = jnp.concatenate(
            [row_stack[chunk, :32], jnp.zeros((CHUNK - 32, LANES), jnp.float32)], axis=0
        ).T

        def spread(at):
            return jnp.broadcast_to(turned[:, at : at + 1], (CHUNK, LANES))

        since_rows = spread(24)
        since_ref[local] = since_rows
        rows = pl.ds(pl.multiple_of(chunk * CHUNK, CHUNK), CHUNK)
        current = sequence[rows, :].astype(jnp.float32)
        wide_since = jnp.concatenate([since_rows, since_rows], axis=1)
        conv = tapped(current, previous[...], taps, wide_since)
        previous[...] = current[CHUNK - 8 :]
        keys, queries = conv[:, :STATE].astype(jnp.bfloat16), conv[:, STATE:].astype(jnp.bfloat16)
        query_ref[local] = queries
        key_ref[local] = conv[:, :STATE].T.astype(jnp.bfloat16)
        inner_products = lax.dot_general(
            queries, keys, (((1,), (1,)), ((), ())), preferred_element_type=jnp.float32
        )
        allowed = jnp.where(causal & (column >= row_of - since_rows), 0.0, -1e30)
        for h in range(heads):
            exponent = (spread(h) + allowed) - row_stack[chunk, h : h + 1, :]
            weights = jnp.exp(exponent) * (inner_products * step_rows[chunk, h : h + 1, :])
            mix_ref[local, :, h * CHUNK : (h + 1) * CHUNK] = weights.astype(jnp.bfloat16)
        gate = row_stack[chunk, 32:40]
        for pair in range(heads // 2):
            at = slice(pair * LANES, (pair + 1) * LANES)
            tail_ref[local, :, at] = jnp.where(
                low_half, spread(8 + 2 * pair), spread(9 + 2 * pair)
            )
            inflow_ref[local, :, at] = jnp.where(
                low_half, spread(16 + 2 * pair), spread(17 + 2 * pair)
            )
            gate_ref[local, :, at] = jnp.where(
                low_half[:8],
                jnp.broadcast_to(gate[2 * pair : 2 * pair + 1], (8, LANES)),
                jnp.broadcast_to(gate[2 * pair + 1 : 2 * pair + 2], (8, LANES)),
            )
        return carry

    lax.fori_loop(0, chunks_step, one_chunk, 0, unroll=2)


def scan_kernel(heads, per_dev, turns, place_ref, order_ref, skip_ref, taps_ref, *refs):
    piece_refs, refs = refs[: len(turns)], refs[len(turns) :]
    mix_ref, query_ref, key_ref, tail_ref, inflow_ref, gate_ref, since_ref = refs[:7]
    out_refs, (sequence, gates, laid, previous, state) = refs[7:-5], refs[-5:]
    me, mine = place_ref[0], place_ref[1]
    previous[...] = jnp.zeros_like(previous)
    state[...] = jnp.zeros_like(state)
    for turn, piece_ref in zip(turns, piece_refs):
        loader = jnp.bitwise_xor(me, turn)
        for b in range(per_dev):
            place = order_ref[loader * per_dev + b]
            rows = pl.ds(pl.multiple_of(place * BLK, BLK), BLK)
            sequence[rows, :] = piece_ref[0, b * BLK : (b + 1) * BLK, :]
            gates[rows, :] = piece_ref[1, b * BLK : (b + 1) * BLK, :]
    width = heads * HEAD_DIM
    lane = lax.broadcasted_iota(jnp.int32, (1, width), 1)
    skip = jnp.zeros((1, width), jnp.float32)
    for h in range(heads):
        skip = jnp.where(lane >= h * HEAD_DIM, skip_ref[me * heads + h], skip)
    low_half = lax.broadcasted_iota(jnp.int32, (CHUNK, LANES), 1) < HEAD_DIM
    taps = taps_ref[...]
    blocks = CHUNK // BLK

    def one_chunk(chunk, carry):
        rows = pl.ds(pl.multiple_of(chunk * CHUNK, CHUNK), CHUNK)
        current = sequence[rows, :].astype(jnp.float32)
        wide_since = jnp.concatenate([since_ref[chunk]] * (width // LANES), axis=1)
        values = tapped(current, previous[...], taps, wide_since).astype(jnp.bfloat16)
        previous[...] = current[CHUNK - 8 :]
        values_wide = values.astype(jnp.float32)
        entering = state[...]
        carried = jnp.dot(
            query_ref[chunk], entering.astype(jnp.bfloat16), preferred_element_type=jnp.float32
        )
        total = carried * inflow_ref[chunk] + skip * values_wide
        tail_values = (values_wide * tail_ref[chunk]).astype(jnp.bfloat16)
        state[...] = gate_ref[chunk, :1, :] * entering + jnp.dot(
            key_ref[chunk], tail_values, preferred_element_type=jnp.float32
        )
        zero = jnp.zeros((CHUNK, LANES), jnp.bfloat16)
        intra = []
        for pair in range(heads // 2):
            both = values[:, pair * LANES : (pair + 1) * LANES]
            block = jnp.concatenate(
                [jnp.where(low_half, both, zero), jnp.where(low_half, zero, both)], axis=0
            )
            weights = mix_ref[chunk, :, 2 * pair * CHUNK : 2 * (pair + 1) * CHUNK]
            intra.append(jnp.dot(weights, block, preferred_element_type=jnp.float32))
        mixed = total + jnp.concatenate(intra, axis=1)
        gated = (mixed * silu(gates[rows, :].astype(jnp.float32))).astype(jnp.bfloat16)
        for block in range(blocks):
            place = chunk * blocks + block
            away = jnp.bitwise_xor(lax.rem(place, per_dev), mine)
            slot = 2 * (1 - lax.rem(away, 2)) + (1 - lax.div(away, 2))
            start = pl.multiple_of(slot * BLK, BLK)
            laid[lax.div(place, per_dev), pl.ds(start, BLK), :] = gated[
                block * BLK : (block + 1) * BLK
            ]
        return carry

    lax.fori_loop(0, mix_ref.shape[0], one_chunk, 0, unroll=4)
    for turn, out_ref in zip(turns, out_refs):
        out_ref[...] = laid[jnp.bitwise_xor(me, turn)]


def normed_into(normed, gated_refs, gain_ref, me, first_turn):
    count = len(gated_refs)
    rows, width = gated_refs[0].shape
    wide = [ref[...].astype(jnp.float32) for ref in gated_refs]
    squares = wide[0] * wide[0]
    for piece in wide[1:]:
        squares = squares + piece * piece
    mean = jnp.sum(squares, axis=1, keepdims=True) * (1.0 / (count * width))
    inverse_rms = lax.rsqrt(mean + 1e-05)
    for turn, piece in enumerate(wide):
        source = jnp.bitwise_xor(me, first_turn + turn)
        at = pl.multiple_of(lax.rem(source, count) * width, width)
        gain = gain_ref[pl.ds(source, 1), :]
        normed[:, pl.ds(at, width)] = (piece * inverse_rms * gain).astype(jnp.bfloat16)


def weight_tiles(weight_ref, group, buffer, sems, count):
    tile = buffer.shape[1] // count
    tiles = [slice(i * tile, (i + 1) * tile) for i in range(count)]
    return tiles, [
        pltpu.make_async_copy(weight_ref.at[group, :, at], buffer.at[:, at], sems.at[i])
        for i, at in enumerate(tiles)
    ]


def near_kernel(place_ref, gain_ref, weight_ref, *refs):
    gated_refs, (partial_ref, next_ref, normed, buffer, sems) = refs[:-5], refs[-5:]
    count = sems.shape[0] - 1
    group = lax.div(place_ref[0], len(gated_refs))
    tiles, copies = weight_tiles(weight_ref, group, buffer, sems, count)
    onward = pltpu.make_async_copy(weight_ref.at[1 - group], next_ref, sems.at[count])
    for copy in copies + [onward]:
        copy.start()
    normed_into(normed, gated_refs, gain_ref, place_ref[0], 0)
    for at, copy in zip(tiles, copies):
        copy.wait()
        partial_ref[:, at] = jnp.dot(
            normed[...], buffer[:, at], preferred_element_type=jnp.float32
        )
    onward.wait()


def project_far(normed, weight_ref, near_ref, at, away_ref, stay_ref):
    partial = near_ref[:, at] + jnp.dot(
        normed, weight_ref[:, at], preferred_element_type=jnp.float32
    )
    partial = partial.astype(jnp.bfloat16)
    rows = partial.shape[0] // 2
    away_ref[...] = partial[:rows]
    stay_ref[...] = partial[rows:]


def far_kernel(place_ref, gain_ref, weight_ref, near_ref, *refs):
    gated_refs, (away_ref, stay_ref, normed) = refs[:-3], refs[-3:]
    normed_into(normed, gated_refs, gain_ref, place_ref[0], len(gated_refs))
    at = slice(0, away_ref.shape[1])
    project_far(normed[...], weight_ref, near_ref, at, away_ref, stay_ref)


def rest_kernel(place_ref, normed_ref, weight_ref, near_ref, away_ref, stay_ref):
    at = slice(near_ref.shape[1] - away_ref.shape[1], near_ref.shape[1])
    project_far(normed_ref[...], weight_ref, near_ref, at, away_ref, stay_ref)


def head_split(
    values_in,
    gate_in,
    keys_in,
    queries_in,
    step_in,
    block_order,
    doc_lengths,
    conv_values,
    conv_keys,
    conv_queries,
    decay_log,
    step_bias,
    skip_gain,
    norm_gain,
    out_weight,
):
    ctx_count = lax.axis_size("ctx")
    tp_count = lax.axis_size("tp")
    me = lax.axis_index("ctx")
    tp_index = lax.axis_index("tp")
    token_count, channels = values_in.shape
    per_dev = token_count // BLK
    total_tokens = token_count * ctx_count
    heads_local = step_in.shape[1]
    heads = heads_local // ctx_count
    width = heads * HEAD_DIM
    groups = keys_in.shape[1] // STATE
    group_heads = heads_local // groups
    near = ctx_count // groups
    chunks = total_tokens // CHUNK
    my_group = me // near
    place = jnp.stack([me, tp_index]).astype(jnp.int32)

    def turned(value, turn):
        return lax.ppermute(value, "ctx", [(i, i ^ turn) for i in range(ctx_count)])

    def for_group(group):
        keys = lax.dynamic_slice_in_dim(keys_in, group * STATE, STATE, 1)
        queries = lax.dynamic_slice_in_dim(queries_in, group * STATE, STATE, 1)
        steps = lax.dynamic_slice_in_dim(step_in, group * group_heads, group_heads, 1)
        return jnp.concatenate([jnp.concatenate([keys, queries], axis=1), steps.T], axis=0)

    def for_heads(turn):
        at = (me ^ turn) * width
        return jnp.stack(
            [lax.dynamic_slice_in_dim(rows, at, width, 1) for rows in (values_in, gate_in)]
        )

    held = jnp.stack([for_group(my_group), turned(for_group(my_group ^ 1), near)])
    group_rows = [held] + [turned(held, turn) for turn in range(1, near)]
    turns = (0, 3, 4, 7, 1, 2, 5, 6)
    head_rows = [turned(for_heads(turn), turn) if turn else for_heads(turn) for turn in turns]

    key_taps = lax.dynamic_slice_in_dim(conv_keys, my_group * STATE, STATE, 1)
    query_taps = lax.dynamic_slice_in_dim(conv_queries, my_group * STATE, STATE, 1)
    value_taps = lax.dynamic_slice_in_dim(conv_values, me * width, width, 1)

    smem = pl.BlockSpec(memory_space=pltpu.SMEM)
    vmem = pl.BlockSpec(memory_space=pltpu.VMEM)
    params = pltpu.CompilerParams(vmem_limit_bytes=28 * 1024 * 1024)

    def whole(array):
        return pl.BlockSpec(array.shape, lambda *ids: (0,) * array.ndim)

    grid_steps = 4
    chunks_step = chunks // grid_steps

    def per_step(rows, columns):
        return pl.BlockSpec((chunks_step, rows, columns), lambda i: (i, 0, 0))

    mix_shapes = [
        ((CHUNK, heads * CHUNK), jnp.bfloat16),
        ((CHUNK, STATE), jnp.bfloat16),
        ((STATE, CHUNK), jnp.bfloat16),
        ((CHUNK, width), jnp.float32),
        ((CHUNK, width), jnp.float32),
        ((8, width), jnp.float32),
        ((CHUNK, LANES), jnp.float32),
    ]
    mixing = pl.pallas_call(
        functools.partial(mixing_kernel, heads, group_heads, per_dev, chunks_step, near),
        grid=(grid_steps,),
        in_specs=[smem] * 5 + [whole(key_taps), whole(query_taps)] + [whole(held)] * near,
        out_specs=[per_step(*shape) for shape, _ in mix_shapes],
        out_shape=[jax.ShapeDtypeStruct((chunks,) + shape, kind) for shape, kind in mix_shapes],
        scratch_shapes=[
            pltpu.VMEM((total_tokens, 2 * STATE), jnp.bfloat16),
            pltpu.VMEM((8, 2 * STATE), jnp.float32),
            pltpu.VMEM((chunks, 8, LANES), jnp.float32),
            pltpu.VMEM((chunks, 8, LANES), jnp.float32),
            pltpu.VMEM((chunks, 40, LANES), jnp.float32),
        ],
        compiler_params=params,
        cost_estimate=pl.CostEstimate(
            flops=20_000_000, bytes_accessed=20_000_000, transcendentals=2_000_000
        ),
        name="mixing",
    )(place, block_order, doc_lengths, step_bias, decay_log, key_taps, query_taps, *group_rows)

    gated = pl.pallas_call(
        functools.partial(scan_kernel, heads, per_dev, turns),
        in_specs=[smem] * 3 + [vmem] * (1 + ctx_count + len(mix_shapes)),
        out_specs=[vmem] * ctx_count,
        out_shape=[jax.ShapeDtypeStruct((token_count, width), jnp.bfloat16)] * ctx_count,
        scratch_shapes=[
            pltpu.VMEM((total_tokens, width), jnp.bfloat16),
            pltpu.VMEM((total_tokens, width), jnp.bfloat16),
            pltpu.VMEM((ctx_count, token_count, width), jnp.bfloat16),
            pltpu.VMEM((8, width), jnp.float32),
            pltpu.VMEM((STATE, width), jnp.float32),
        ],
        compiler_params=params,
        cost_estimate=pl.CostEstimate(
            flops=600_000_000, bytes_accessed=14_000_000, transcendentals=1_200_000
        ),
        name="scan",
    )(place, block_order, skip_gain, value_taps, *head_rows, *mixing)
    gated = dict(zip(turns, gated))

    pieces = [gated[0]] + [turned(gated[turn], turn) for turn in range(1, ctx_count)]

    columns = out_weight.shape[1]
    group_width = near * width
    gain = norm_gain.reshape(ctx_count, width)
    weight = out_weight.reshape(groups, group_width, columns)

    def project(kernel, first, weight, weight_space, operands, out_shape, scratch, limit, name):
        return pl.pallas_call(
            kernel,
            in_specs=[smem, vmem, pl.BlockSpec(memory_space=weight_space)] + [vmem] * len(operands),
            out_specs=[vmem] * len(out_shape),
            out_shape=out_shape,
            scratch_shapes=scratch,
            compiler_params=pltpu.CompilerParams(vmem_limit_bytes=limit * 1024 * 1024),
            cost_estimate=pl.CostEstimate(
                flops=2 * token_count * group_width * columns,
                bytes_accessed=2 * group_width * columns,
                transcendentals=0,
            ),
            name=name,
        )(place, first, weight, *operands)

    near_partial, far_weight = project(
        near_kernel,
        gain,
        weight,
        pl.ANY,
        pieces[:near],
        [
            jax.ShapeDtypeStruct((token_count, columns), jnp.float32),
            jax.ShapeDtypeStruct((group_width, columns), jnp.bfloat16),
        ],
        [
            pltpu.VMEM((token_count, group_width), jnp.bfloat16),
            pltpu.VMEM((group_width, columns), jnp.bfloat16),
            pltpu.SemaphoreType.DMA((5,)),
        ],
        28,
        "near_projection",
    )
    rows = token_count // 2
    normed_shape = jax.ShapeDtypeStruct((token_count, group_width), jnp.bfloat16)

    def part_shape(part_columns):
        return jax.ShapeDtypeStruct((rows, part_columns), jnp.bfloat16)

    first_columns = columns // 2
    away, stay, far_normed = project(
        far_kernel,
        gain,
        far_weight,
        pltpu.VMEM,
        [near_partial] + pieces[near:],
        [part_shape(first_columns)] * 2 + [normed_shape],
        [],
        8,
        "far_projection",
    )
    rest_away, rest_stay = project(
        rest_kernel,
        far_normed,
        far_weight,
        pltpu.VMEM,
        [near_partial],
        [part_shape(columns - first_columns)] * 2,
        [],
        8,
        "rest_projection",
    )

    def joined(kept, sent, turn):
        came = lax.ppermute(sent, "tp", [(i, i ^ turn) for i in range(tp_count)])
        return (kept.astype(jnp.float32) + came.astype(jnp.float32)).astype(jnp.bfloat16)

    results = []
    for away, stay in ((away, stay), (rest_away, rest_stay)):
        across = joined(stay, away, 1)
        results.append(joined(across[rows // 2 :], across[: rows // 2], 2))
    return jnp.concatenate(results, axis=1)


def on_mesh(*arrays):
    ctx_count, tp_count = lax.axis_size("ctx"), lax.axis_size("tp")
    groups = arrays[2].shape[1] // STATE
    heads_local = arrays[4].shape[1]
    fits = (
        groups == 2
        and tp_count == 4
        and ctx_count & (ctx_count - 1) == 0
        and heads_local % (2 * ctx_count) == 0
        and heads_local // ctx_count <= 8
        and arrays[0].shape[0] == 2 * STATE
    )
    return (head_split if fits else on_device)(*arrays)


def solution(mesh):
    in_specs = (
        P("ctx", "tp"),
        P("ctx", "tp"),
        P("ctx", "tp"),
        P("ctx", "tp"),
        P("ctx", "tp"),
        P(),
        P(),
        P(None, "tp"),
        P(None, "tp"),
        P(None, "tp"),
        P("tp"),
        P("tp"),
        P("tp"),
        P("tp"),
        P("tp", None),
    )
    out_specs = P(("ctx", "tp"), None)
    return jax.shard_map(
        on_mesh, mesh=mesh, in_specs=in_specs, out_specs=out_specs, check_vma=False
    )
```

```python
import functools

import jax
import jax.numpy as jnp
from jax import lax
from jax.experimental import pallas as pl
from jax.experimental.pallas import tpu as pltpu
from jax.sharding import PartitionSpec as P

HEAD_DIM = 64
STATE = 128
CONV = 4
SPAN = 256
BLK = 64


def shifted_2(value, axis, steps):
    count = lax.axis_size(axis)
    leading, last = (max(0, -steps), min(count, count - steps))
    return lax.ppermute(value, axis, [(source, source + steps) for source in range(leading, last)])


def carried_in(shard, axis, join, neutral):
    place = lax.axis_index(axis)
    gathered = jax.tree.map(
        lambda a, kind: lax.all_gather(a.astype(kind), axis),
        shard,
        jax.tree.map(lambda a: jnp.bfloat16 if a.dtype == jnp.float32 else a.dtype, shard),
    )
    state = jax.tree.map(lambda a, e: jnp.zeros_like(a) + jnp.asarray(e, a.dtype), shard, neutral)

    def one(turn, state):
        return join(
            state,
            jax.tree.map(
                lambda a, own: lax.dynamic_index_in_dim(a, turn, 0, False).astype(own.dtype),
                gathered,
                shard,
            ),
        )

    return lax.fori_loop(0, place, one, state)


def document_index(positions, doc_lengths):
    offsets = jnp.cumsum(doc_lengths) - doc_lengths
    below_start = offsets[None, :] <= positions[:, None]
    documents = jnp.sum(below_start.astype(jnp.int32), axis=1, dtype=jnp.int32) - 1
    openings = jnp.any(offsets[None, :] == positions[:, None], axis=1).astype(jnp.int32)
    return (documents, openings)


def causal_conv(extended, weight, doc_ext):
    tap_count = weight.shape[0]
    row_count = extended.shape[0] - tap_count + 1
    current = doc_ext[tap_count - 1 :]
    accumulated = jnp.zeros((row_count, extended.shape[1]), jnp.float32)
    for tap_index in range(tap_count):
        keep_rows = (doc_ext[tap_index : tap_index + row_count] == current)[:, None]
        shifted = (
            extended[tap_index : tap_index + row_count].astype(jnp.float32) * weight[tap_index]
        )
        accumulated = accumulated + jnp.where(keep_rows, shifted, 0.0)
    return lax.optimization_barrier(jax.nn.silu(accumulated).astype(jnp.bfloat16))


def span_outputs(value_rows, step_rows, key_rows, query_rows, decay_sums, documents):
    row_count = value_rows.shape[0]
    per_group = value_rows.shape[1] // key_rows.shape[1]
    row_ids = jnp.arange(row_count, dtype=jnp.int32)
    keep_mask = (documents[:, None] == documents[None, :]) & (row_ids[None, :] <= row_ids[:, None])
    differences = decay_sums[:, :, None] - decay_sums[:, None, :]
    decays = jnp.where(keep_mask[None], jnp.exp(jnp.minimum(differences, 0.0)), 0.0)
    inner_products = jnp.einsum(
        "ign,jgn->gij", query_rows, key_rows, preferred_element_type=jnp.float32
    )
    weighted = (
        decays * jnp.repeat(inner_products, per_group, axis=0) * step_rows.T[:, None, :]
    ).astype(jnp.bfloat16)
    return jnp.einsum("hij,jhp->ihp", weighted, value_rows, preferred_element_type=jnp.float32)


def span_states(value_rows, step_rows, key_rows, decay_sums, documents, openings):
    per_group = value_rows.shape[1] // key_rows.shape[1]
    tail_decay = jnp.where(
        (documents == documents[-1])[None, :], jnp.exp(decay_sums[:, -1:] - decay_sums), 0.0
    )
    tail_weight = tail_decay.T * step_rows
    head_keys = jnp.repeat(key_rows, per_group, axis=1)
    tail_keys = (tail_weight[:, :, None] * head_keys.astype(jnp.float32)).astype(jnp.bfloat16)
    local_state = jnp.einsum(
        "jhp,jhn->hpn", value_rows, tail_keys, preferred_element_type=jnp.float32
    )
    opened = jnp.cumsum(openings)
    span_gate = jnp.where(opened[-1] == 0, jnp.exp(decay_sums[:, -1]), 0.0)
    inflow = jnp.where((opened == 0)[None, :], jnp.exp(decay_sums), 0.0)
    return (local_state, span_gate, inflow)


def span_inflow(query_rows, entering, inflow):
    per_group = entering.shape[0] // query_rows.shape[1]
    head_queries = jnp.repeat(query_rows.astype(jnp.float32), per_group, axis=1)
    carried = jnp.einsum("ihn,hpn->ihp", head_queries, entering, precision=lax.Precision.HIGHEST)
    return carried * inflow.T[:, :, None]


def gated_norm(mixed_rows, gate_rows, norm_gain, groups_local):
    gated_rows = mixed_rows * jax.nn.silu(gate_rows.astype(jnp.float32))
    grouped = gated_rows.reshape(gated_rows.shape[0], groups_local, -1)
    inverse_rms = lax.rsqrt(jnp.mean(grouped * grouped, axis=2, keepdims=True) + 1e-05)
    return ((grouped * inverse_rms).reshape(gated_rows.shape) * norm_gain).astype(jnp.bfloat16)


def on_device(
    values_in,
    gate_in,
    keys_in,
    queries_in,
    step_in,
    block_order,
    doc_lengths,
    conv_values,
    conv_keys,
    conv_queries,
    decay_log,
    step_bias,
    skip_gain,
    norm_gain,
    out_weight,
):
    ctx_count = lax.axis_size("ctx")
    ctx_index = lax.axis_index("ctx")
    token_count = values_in.shape[0]
    per_dev = token_count // BLK
    capacity = (per_dev + ctx_count - 1) // ctx_count
    rim_rows = CONV - 1
    pos_table = block_order.reshape(ctx_count, per_dev)
    owner_of = pos_table // per_dev
    local_ids = jnp.arange(per_dev, dtype=jnp.int32)
    earlier = local_ids[None, :] < local_ids[:, None]
    same_owner = owner_of[:, :, None] == owner_of[:, None, :]
    slot_rank = jnp.sum((same_owner & earlier[None]).astype(jnp.int32), axis=2, dtype=jnp.int32)
    my_owner = lax.dynamic_index_in_dim(owner_of, ctx_index, 0, keepdims=False)
    my_rank = lax.dynamic_index_in_dim(slot_rank, ctx_index, 0, keepdims=False)
    slot_ids = jnp.arange(ctx_count * capacity, dtype=jnp.int32)
    slot_hit = (my_owner * capacity + my_rank)[None, :] == slot_ids[:, None]
    source = jnp.sum(jnp.where(slot_hit, local_ids[None, :], 0), axis=1, dtype=jnp.int32)
    filled = jnp.any(slot_hit, axis=1)

    def pack_slots(local_rows):
        blocks = local_rows.reshape(per_dev, BLK, local_rows.shape[1])
        picked = jnp.where(filled[:, None, None], blocks[source], jnp.zeros((), local_rows.dtype))
        return picked

    all_slots = (jnp.arange(ctx_count, dtype=jnp.int32)[:, None] * capacity + slot_rank).reshape(-1)
    wanted = ctx_index * per_dev + local_ids
    owner_hit = block_order[None, :] == wanted[:, None]
    pick_slot = jnp.sum(jnp.where(owner_hit, all_slots[None, :], 0), axis=1, dtype=jnp.int32)

    def unpack_slots(received):
        return received[pick_slot].reshape(token_count, received.shape[2])

    packed_values = pack_slots(values_in)
    packed_gates = pack_slots(gate_in)
    packed_keys = pack_slots(keys_in)
    packed_queries = pack_slots(queries_in)
    packed_steps = pack_slots(step_in)
    received = (
        lax.all_to_all(packed_values, "ctx", split_axis=0, concat_axis=0, tiled=True),
        lax.all_to_all(packed_gates, "ctx", split_axis=0, concat_axis=0, tiled=True),
        lax.all_to_all(packed_keys, "ctx", split_axis=0, concat_axis=0, tiled=True),
        lax.all_to_all(packed_queries, "ctx", split_axis=0, concat_axis=0, tiled=True),
        lax.all_to_all(packed_steps, "ctx", split_axis=0, concat_axis=0, tiled=True),
    )
    own_values = unpack_slots(received[0])
    own_gates = unpack_slots(received[1])
    own_keys = unpack_slots(received[2])
    own_queries = unpack_slots(received[3])
    own_steps = unpack_slots(received[4])
    rim_values, rim_keys, rim_queries = shifted_2(
        (
            own_values[token_count - rim_rows :],
            own_keys[token_count - rim_rows :],
            own_queries[token_count - rim_rows :],
        ),
        "ctx",
        1,
    )
    positions = (
        ctx_index * token_count - rim_rows + jnp.arange(token_count + rim_rows, dtype=jnp.int32)
    )
    doc_ext, open_ext = document_index(positions, doc_lengths)
    documents = doc_ext[rim_rows:]
    openings = open_ext[rim_rows:]
    conv_value = causal_conv(
        jnp.concatenate([rim_values, own_values], axis=0), conv_values, doc_ext
    )
    conv_key = causal_conv(jnp.concatenate([rim_keys, own_keys], axis=0), conv_keys, doc_ext)
    conv_query = causal_conv(
        jnp.concatenate([rim_queries, own_queries], axis=0), conv_queries, doc_ext
    )
    heads_local = own_steps.shape[1]
    groups_local = own_keys.shape[1] // STATE
    span_count = token_count // SPAN
    step_size = jax.nn.softplus(own_steps.astype(jnp.float32) + step_bias)
    rates = -jnp.exp(decay_log) * step_size
    value_rows = conv_value.reshape(span_count, SPAN, heads_local, HEAD_DIM)
    key_rows = conv_key.reshape(span_count, SPAN, groups_local, STATE)
    query_rows = conv_query.reshape(span_count, SPAN, groups_local, STATE)
    step_spans = step_size.reshape(span_count, SPAN, heads_local)
    decay_sums = jnp.cumsum(rates.reshape(span_count, SPAN, heads_local).transpose(0, 2, 1), axis=2)
    span_docs = documents.reshape(span_count, SPAN)
    span_openings = openings.reshape(span_count, SPAN)
    intra = jax.vmap(span_outputs)(
        value_rows, step_spans, key_rows, query_rows, decay_sums, span_docs
    )
    local_states, span_gates, inflows = jax.vmap(span_states)(
        value_rows, step_spans, key_rows, decay_sums, span_docs, span_openings
    )

    def advance(running, inputs):
        decay_product, accumulated = running
        span_state, span_gate = inputs
        advanced = (span_gate * decay_product, span_gate[:, None, None] * accumulated + span_state)
        return (advanced, running)

    start_carry = (
        jnp.ones((heads_local,), jnp.float32),
        jnp.zeros((heads_local, HEAD_DIM, STATE), jnp.float32),
    )
    summary, prefixes = lax.scan(advance, start_carry, (local_states, span_gates))

    def combine(earlier_part, later_part):
        return (
            earlier_part[0] * later_part[0],
            later_part[0][:, None, None] * earlier_part[1] + later_part[1],
        )

    incoming = carried_in(summary, "ctx", combine, start_carry)
    entering = prefixes[0][:, :, None, None] * incoming[1][None] + prefixes[1]
    entering, inflows = (entering, inflows)
    inter = jax.vmap(span_inflow)(query_rows, entering, inflows)
    mixed_rows = intra + inter + skip_gain[None, None, :, None] * value_rows.astype(jnp.float32)
    mixed_rows = mixed_rows.reshape(token_count, heads_local * HEAD_DIM)
    normed = gated_norm(mixed_rows, own_gates, norm_gain, groups_local)
    return lax.psum_scatter(
        jnp.dot(normed, out_weight, preferred_element_type=jnp.float32).astype(jnp.bfloat16),
        "tp",
        scatter_dimension=0,
        tiled=True,
    )


CHUNK = 128
LANES = 128


def tapped(current, previous, taps, since):
    row_count = current.shape[0]
    extended = jnp.concatenate([previous, current], axis=0)
    total = None
    for tap_index in range(CONV):
        steps = CONV - 1 - tap_index
        weight = taps[tap_index : tap_index + 1, :]
        if steps == 0:
            term = current * weight
        else:
            shifted = pltpu.roll(extended, steps, 0)[8 : 8 + row_count]
            term = jnp.where(since >= steps, shifted * weight, 0.0)
        total = term if total is None else total + term
    return silu(total)


def silu(x):
    half = 0.5 * x
    return half + half * jnp.tanh(half)


def mixing_kernel(
    heads,
    group_heads,
    per_dev,
    chunks_step,
    piece_count,
    me_ref,
    order_ref,
    lengths_ref,
    bias_ref,
    log_ref,
    key_taps_ref,
    query_taps_ref,
    *refs,
):
    piece_refs, refs = refs[:piece_count], refs[piece_count:]
    mix_ref, query_ref, key_ref, tail_ref, inflow_ref, gate_ref, since_ref = refs[:7]
    sequence, previous, raw_steps, step_rows, row_stack = refs[7:]
    groups = piece_refs[0].shape[0]
    me = me_ref[0]
    step_id = pl.program_id(0)
    token_rows = per_dev * BLK
    chunks = raw_steps.shape[0]

    @pl.when(step_id == 0)
    def _():
        previous[...] = jnp.zeros_like(previous)
        lane = lax.broadcasted_iota(jnp.int32, (8, LANES), 1)
        row8 = lax.broadcasted_iota(jnp.int32, (8, LANES), 0)
        own = lax.rem(me * heads, group_heads)
        for g in range(groups):
            for turn, piece_ref in enumerate(piece_refs):
                loader = jnp.bitwise_xor(me, g * piece_count + turn)
                for b in range(per_dev):
                    place = order_ref[loader * per_dev + b]
                    rows = pl.ds(pl.multiple_of(place * BLK, BLK), BLK)
                    sequence[rows, :] = piece_ref[g, b * BLK : (b + 1) * BLK, :]
                    at = (b // 2) * LANES
                    steps_in = piece_ref[
                        g, token_rows : token_rows + group_heads, at : at + LANES
                    ].astype(jnp.float32)
                    parity = lax.rem(place, 2)
                    steps_in = pltpu.roll(
                        steps_in, lax.rem(group_heads - own, group_heads), 0
                    )[:8]
                    steps_in = pltpu.roll(steps_in, BLK * jnp.bitwise_xor(parity, b % 2), 1)
                    chunk = lax.div(place, 2)
                    raw_steps[chunk] = jnp.where(
                        lane // BLK == parity, steps_in, raw_steps[chunk]
                    )
        bias = jnp.zeros((8, LANES), jnp.float32)
        decay = jnp.zeros((8, LANES), jnp.float32)
        for h in range(heads):
            bias = jnp.where(row8 == h, bias_ref[me * heads + h], bias)
            decay = jnp.where(row8 == h, log_ref[me * heads + h], decay)
        decay = -jnp.exp(decay)
        raw = jnp.where(row8[None] < heads, raw_steps[...] + bias[None], 0.0)
        step = jnp.maximum(raw, 0.0) + jnp.log(1.0 + jnp.exp(-jnp.abs(raw)))
        step_rows[...] = step
        sums = decay[None] * step
        lanes = lax.broadcasted_iota(jnp.int32, (chunks, 8, LANES), 2)
        width = 1
        while width < CHUNK:
            sums = sums + jnp.where(lanes >= width, pltpu.roll(sums, width, 2), 0.0)
            width *= 2
        first = lax.broadcasted_iota(jnp.int32, (chunks, 8, LANES), 0) * CHUNK
        position = first + lanes
        begun = jnp.zeros_like(position)
        offset = jnp.int32(0)
        for k in range(lengths_ref.shape[0]):
            begun = jnp.where(position >= offset, offset, begun)
            offset = offset + lengths_ref[k]
        last_sum = jnp.sum(jnp.where(lanes == CHUNK - 1, sums, 0.0), axis=2, keepdims=True)
        last_begun = jnp.max(begun, axis=2, keepdims=True)
        row_stack[:, 0:8] = sums
        row_stack[:, 8:16] = jnp.where(
            position >= last_begun, jnp.exp(last_sum - sums) * step, 0.0
        )
        row_stack[:, 16:24] = jnp.where(begun < first, jnp.exp(sums), 0.0)
        row_stack[:, 24:32] = (position - begun).astype(jnp.float32)
        row_stack[:, 32:40] = jnp.where(
            last_begun < first, jnp.exp(last_sum), jnp.zeros_like(sums)
        )

    causal = lax.broadcasted_iota(jnp.int32, (CHUNK, CHUNK), 0) >= lax.broadcasted_iota(
        jnp.int32, (CHUNK, CHUNK), 1
    )
    column = lax.broadcasted_iota(jnp.int32, (CHUNK, CHUNK), 1).astype(jnp.float32)
    row_of = lax.broadcasted_iota(jnp.int32, (CHUNK, CHUNK), 0).astype(jnp.float32)
    low_half = lax.broadcasted_iota(jnp.int32, (CHUNK, LANES), 1) < HEAD_DIM
    taps = jnp.concatenate([key_taps_ref[...], query_taps_ref[...]], axis=1)

    def one_chunk(local, carry):
        chunk = step_id * chunks_step + local
        turned = jnp.concatenate(
            [row_stack[chunk, :32], jnp.zeros((CHUNK - 32, LANES), jnp.float32)], axis=0
        ).T

        def spread(at):
            return jnp.broadcast_to(turned[:, at : at + 1], (CHUNK, LANES))

        since_rows = spread(24)
        since_ref[local] = since_rows
        rows = pl.ds(pl.multiple_of(chunk * CHUNK, CHUNK), CHUNK)
        current = sequence[rows, :].astype(jnp.float32)
        wide_since = jnp.concatenate([since_rows, since_rows], axis=1)
        conv = tapped(current, previous[...], taps, wide_since)
        previous[...] = current[CHUNK - 8 :]
        keys, queries = conv[:, :STATE].astype(jnp.bfloat16), conv[:, STATE:].astype(jnp.bfloat16)
        query_ref[local] = queries
        key_ref[local] = conv[:, :STATE].T.astype(jnp.bfloat16)
        inner_products = lax.dot_general(
            queries, keys, (((1,), (1,)), ((), ())), preferred_element_type=jnp.float32
        )
        allowed = jnp.where(causal & (column >= row_of - since_rows), 0.0, -1e30)
        for h in range(heads):
            exponent = (spread(h) + allowed) - row_stack[chunk, h : h + 1, :]
            weights = jnp.exp(exponent) * (inner_products * step_rows[chunk, h : h + 1, :])
            mix_ref[local, :, h * CHUNK : (h + 1) * CHUNK] = weights.astype(jnp.bfloat16)
        gate = row_stack[chunk, 32:40]
        for pair in range(heads // 2):
            at = slice(pair * LANES, (pair + 1) * LANES)
            tail_ref[local, :, at] = jnp.where(
                low_half, spread(8 + 2 * pair), spread(9 + 2 * pair)
            )
            inflow_ref[local, :, at] = jnp.where(
                low_half, spread(16 + 2 * pair), spread(17 + 2 * pair)
            )
            gate_ref[local, :, at] = jnp.where(
                low_half[:8],
                jnp.broadcast_to(gate[2 * pair : 2 * pair + 1], (8, LANES)),
                jnp.broadcast_to(gate[2 * pair + 1 : 2 * pair + 2], (8, LANES)),
            )
        return carry

    lax.fori_loop(0, chunks_step, one_chunk, 0, unroll=2)


def scan_kernel(heads, per_dev, turns, place_ref, order_ref, skip_ref, taps_ref, *refs):
    piece_refs, refs = refs[: len(turns)], refs[len(turns) :]
    mix_ref, query_ref, key_ref, tail_ref, inflow_ref, gate_ref, since_ref = refs[:7]
    out_refs, (sequence, gates, laid, previous, state) = refs[7:-5], refs[-5:]
    me, mine = place_ref[0], place_ref[1]
    previous[...] = jnp.zeros_like(previous)
    state[...] = jnp.zeros_like(state)
    for turn, piece_ref in zip(turns, piece_refs):
        loader = jnp.bitwise_xor(me, turn)
        for b in range(per_dev):
            place = order_ref[loader * per_dev + b]
            rows = pl.ds(pl.multiple_of(place * BLK, BLK), BLK)
            sequence[rows, :] = piece_ref[0, b * BLK : (b + 1) * BLK, :]
            gates[rows, :] = piece_ref[1, b * BLK : (b + 1) * BLK, :]
    width = heads * HEAD_DIM
    lane = lax.broadcasted_iota(jnp.int32, (1, width), 1)
    skip = jnp.zeros((1, width), jnp.float32)
    for h in range(heads):
        skip = jnp.where(lane >= h * HEAD_DIM, skip_ref[me * heads + h], skip)
    low_half = lax.broadcasted_iota(jnp.int32, (CHUNK, LANES), 1) < HEAD_DIM
    taps = taps_ref[...]
    blocks = CHUNK // BLK

    def one_chunk(chunk, carry):
        rows = pl.ds(pl.multiple_of(chunk * CHUNK, CHUNK), CHUNK)
        current = sequence[rows, :].astype(jnp.float32)
        wide_since = jnp.concatenate([since_ref[chunk]] * (width // LANES), axis=1)
        values = tapped(current, previous[...], taps, wide_since).astype(jnp.bfloat16)
        previous[...] = current[CHUNK - 8 :]
        values_wide = values.astype(jnp.float32)
        entering = state[...]
        carried = jnp.dot(
            query_ref[chunk], entering.astype(jnp.bfloat16), preferred_element_type=jnp.float32
        )
        total = carried * inflow_ref[chunk] + skip * values_wide
        tail_values = (values_wide * tail_ref[chunk]).astype(jnp.bfloat16)
        state[...] = gate_ref[chunk, :1, :] * entering + jnp.dot(
            key_ref[chunk], tail_values, preferred_element_type=jnp.float32
        )
        zero = jnp.zeros((CHUNK, LANES), jnp.bfloat16)
        intra = []
        for pair in range(heads // 2):
            both = values[:, pair * LANES : (pair + 1) * LANES]
            block = jnp.concatenate(
                [jnp.where(low_half, both, zero), jnp.where(low_half, zero, both)], axis=0
            )
            weights = mix_ref[chunk, :, 2 * pair * CHUNK : 2 * (pair + 1) * CHUNK]
            intra.append(jnp.dot(weights, block, preferred_element_type=jnp.float32))
        mixed = total + jnp.concatenate(intra, axis=1)
        gated = (mixed * silu(gates[rows, :].astype(jnp.float32))).astype(jnp.bfloat16)
        for block in range(blocks):
            place = chunk * blocks + block
            away = jnp.bitwise_xor(lax.rem(place, per_dev), mine)
            slot = 2 * (1 - lax.rem(away, 2)) + (1 - lax.div(away, 2))
            start = pl.multiple_of(slot * BLK, BLK)
            laid[lax.div(place, per_dev), pl.ds(start, BLK), :] = gated[
                block * BLK : (block + 1) * BLK
            ]
        return carry

    lax.fori_loop(0, mix_ref.shape[0], one_chunk, 0, unroll=4)
    for turn, out_ref in zip(turns, out_refs):
        out_ref[...] = laid[jnp.bitwise_xor(me, turn)]


def normed_into(normed, gated_refs, gain_ref, me, first_turn):
    count = len(gated_refs)
    rows, width = gated_refs[0].shape
    wide = [ref[...].astype(jnp.float32) for ref in gated_refs]
    squares = wide[0] * wide[0]
    for piece in wide[1:]:
        squares = squares + piece * piece
    mean = jnp.sum(squares, axis=1, keepdims=True) * (1.0 / (count * width))
    inverse_rms = lax.rsqrt(mean + 1e-05)
    for turn, piece in enumerate(wide):
        source = jnp.bitwise_xor(me, first_turn + turn)
        at = pl.multiple_of(lax.rem(source, count) * width, width)
        gain = gain_ref[pl.ds(source, 1), :]
        normed[:, pl.ds(at, width)] = (piece * inverse_rms * gain).astype(jnp.bfloat16)


def weight_tiles(weight_ref, group, buffer, sems, count):
    tile = buffer.shape[1] // count
    tiles = [slice(i * tile, (i + 1) * tile) for i in range(count)]
    return tiles, [
        pltpu.make_async_copy(weight_ref.at[group, :, at], buffer.at[:, at], sems.at[i])
        for i, at in enumerate(tiles)
    ]


def near_kernel(place_ref, gain_ref, weight_ref, *refs):
    gated_refs, (partial_ref, next_ref, normed, buffer, sems) = refs[:-5], refs[-5:]
    count = sems.shape[0] - 1
    group = lax.div(place_ref[0], len(gated_refs))
    tiles, copies = weight_tiles(weight_ref, group, buffer, sems, count)
    onward = pltpu.make_async_copy(weight_ref.at[1 - group], next_ref, sems.at[count])
    for copy in copies + [onward]:
        copy.start()
    normed_into(normed, gated_refs, gain_ref, place_ref[0], 0)
    for at, copy in zip(tiles, copies):
        copy.wait()
        partial_ref[:, at] = jnp.dot(
            normed[...], buffer[:, at], preferred_element_type=jnp.float32
        )
    onward.wait()


def project_far(normed, weight_ref, near_ref, at, away_ref, stay_ref):
    partial = near_ref[:, at] + jnp.dot(
        normed, weight_ref[:, at], preferred_element_type=jnp.float32
    )
    partial = partial.astype(jnp.bfloat16)
    rows = partial.shape[0] // 2
    away_ref[...] = partial[:rows]
    stay_ref[...] = partial[rows:]


def far_kernel(place_ref, gain_ref, weight_ref, near_ref, *refs):
    gated_refs, (away_ref, stay_ref, normed) = refs[:-3], refs[-3:]
    normed_into(normed, gated_refs, gain_ref, place_ref[0], len(gated_refs))
    at = slice(0, away_ref.shape[1])
    project_far(normed[...], weight_ref, near_ref, at, away_ref, stay_ref)


def rest_kernel(place_ref, normed_ref, weight_ref, near_ref, away_ref, stay_ref):
    at = slice(near_ref.shape[1] - away_ref.shape[1], near_ref.shape[1])
    project_far(normed_ref[...], weight_ref, near_ref, at, away_ref, stay_ref)


def head_split(
    values_in,
    gate_in,
    keys_in,
    queries_in,
    step_in,
    block_order,
    doc_lengths,
    conv_values,
    conv_keys,
    conv_queries,
    decay_log,
    step_bias,
    skip_gain,
    norm_gain,
    out_weight,
):
    ctx_count = lax.axis_size("ctx")
    tp_count = lax.axis_size("tp")
    me = lax.axis_index("ctx")
    tp_index = lax.axis_index("tp")
    token_count, channels = values_in.shape
    per_dev = token_count // BLK
    total_tokens = token_count * ctx_count
    heads_local = step_in.shape[1]
    heads = heads_local // ctx_count
    width = heads * HEAD_DIM
    groups = keys_in.shape[1] // STATE
    group_heads = heads_local // groups
    near = ctx_count // groups
    chunks = total_tokens // CHUNK
    my_group = me // near
    place = jnp.stack([me, tp_index]).astype(jnp.int32)

    def turned(value, turn):
        return lax.ppermute(value, "ctx", [(i, i ^ turn) for i in range(ctx_count)])

    def for_group(group):
        keys = lax.dynamic_slice_in_dim(keys_in, group * STATE, STATE, 1)
        queries = lax.dynamic_slice_in_dim(queries_in, group * STATE, STATE, 1)
        steps = lax.dynamic_slice_in_dim(step_in, group * group_heads, group_heads, 1)
        return jnp.concatenate([jnp.concatenate([keys, queries], axis=1), steps.T], axis=0)

    def for_heads(turn):
        at = (me ^ turn) * width
        return jnp.stack(
            [lax.dynamic_slice_in_dim(rows, at, width, 1) for rows in (values_in, gate_in)]
        )

    held = jnp.stack([for_group(my_group), turned(for_group(my_group ^ 1), near)])
    group_rows = [held] + [turned(held, turn) for turn in range(1, near)]
    turns = (0, 1, 4, 7, 3, 2, 5, 6)
    head_rows = [turned(for_heads(turn), turn) if turn else for_heads(turn) for turn in turns]

    key_taps = lax.dynamic_slice_in_dim(conv_keys, my_group * STATE, STATE, 1)
    query_taps = lax.dynamic_slice_in_dim(conv_queries, my_group * STATE, STATE, 1)
    value_taps = lax.dynamic_slice_in_dim(conv_values, me * width, width, 1)

    smem = pl.BlockSpec(memory_space=pltpu.SMEM)
    vmem = pl.BlockSpec(memory_space=pltpu.VMEM)
    params = pltpu.CompilerParams(vmem_limit_bytes=28 * 1024 * 1024)

    def whole(array):
        return pl.BlockSpec(array.shape, lambda *ids: (0,) * array.ndim)

    grid_steps = 4
    chunks_step = chunks // grid_steps

    def per_step(rows, columns):
        return pl.BlockSpec((chunks_step, rows, columns), lambda i: (i, 0, 0))

    mix_shapes = [
        ((CHUNK, heads * CHUNK), jnp.bfloat16),
        ((CHUNK, STATE), jnp.bfloat16),
        ((STATE, CHUNK), jnp.bfloat16),
        ((CHUNK, width), jnp.float32),
        ((CHUNK, width), jnp.float32),
        ((8, width), jnp.float32),
        ((CHUNK, LANES), jnp.float32),
    ]
    mixing = pl.pallas_call(
        functools.partial(mixing_kernel, heads, group_heads, per_dev, chunks_step, near),
        grid=(grid_steps,),
        in_specs=[smem] * 5 + [whole(key_taps), whole(query_taps)] + [whole(held)] * near,
        out_specs=[per_step(*shape) for shape, _ in mix_shapes],
        out_shape=[jax.ShapeDtypeStruct((chunks,) + shape, kind) for shape, kind in mix_shapes],
        scratch_shapes=[
            pltpu.VMEM((total_tokens, 2 * STATE), jnp.bfloat16),
            pltpu.VMEM((8, 2 * STATE), jnp.float32),
            pltpu.VMEM((chunks, 8, LANES), jnp.float32),
            pltpu.VMEM((chunks, 8, LANES), jnp.float32),
            pltpu.VMEM((chunks, 40, LANES), jnp.float32),
        ],
        compiler_params=params,
        cost_estimate=pl.CostEstimate(
            flops=20_000_000, bytes_accessed=20_000_000, transcendentals=2_000_000
        ),
        name="mixing",
    )(place, block_order, doc_lengths, step_bias, decay_log, key_taps, query_taps, *group_rows)

    gated = pl.pallas_call(
        functools.partial(scan_kernel, heads, per_dev, turns),
        in_specs=[smem] * 3 + [vmem] * (1 + ctx_count + len(mix_shapes)),
        out_specs=[vmem] * ctx_count,
        out_shape=[jax.ShapeDtypeStruct((token_count, width), jnp.bfloat16)] * ctx_count,
        scratch_shapes=[
            pltpu.VMEM((total_tokens, width), jnp.bfloat16),
            pltpu.VMEM((total_tokens, width), jnp.bfloat16),
            pltpu.VMEM((ctx_count, token_count, width), jnp.bfloat16),
            pltpu.VMEM((8, width), jnp.float32),
            pltpu.VMEM((STATE, width), jnp.float32),
        ],
        compiler_params=params,
        cost_estimate=pl.CostEstimate(
            flops=600_000_000, bytes_accessed=14_000_000, transcendentals=1_200_000
        ),
        name="scan",
    )(place, block_order, skip_gain, value_taps, *head_rows, *mixing)
    gated = dict(zip(turns, gated))

    pieces = [gated[0]] + [turned(gated[turn], turn) for turn in range(1, ctx_count)]

    columns = out_weight.shape[1]
    group_width = near * width
    gain = norm_gain.reshape(ctx_count, width)
    weight = out_weight.reshape(groups, group_width, columns)

    def project(kernel, first, weight, weight_space, operands, out_shape, scratch, limit, name):
        return pl.pallas_call(
            kernel,
            in_specs=[smem, vmem, pl.BlockSpec(memory_space=weight_space)] + [vmem] * len(operands),
            out_specs=[vmem] * len(out_shape),
            out_shape=out_shape,
            scratch_shapes=scratch,
            compiler_params=pltpu.CompilerParams(vmem_limit_bytes=limit * 1024 * 1024),
            cost_estimate=pl.CostEstimate(
                flops=2 * token_count * group_width * columns,
                bytes_accessed=2 * group_width * columns,
                transcendentals=0,
            ),
            name=name,
        )(place, first, weight, *operands)

    near_partial, far_weight = project(
        near_kernel,
        gain,
        weight,
        pl.ANY,
        pieces[:near],
        [
            jax.ShapeDtypeStruct((token_count, columns), jnp.float32),
            jax.ShapeDtypeStruct((group_width, columns), jnp.bfloat16),
        ],
        [
            pltpu.VMEM((token_count, group_width), jnp.bfloat16),
            pltpu.VMEM((group_width, columns), jnp.bfloat16),
            pltpu.SemaphoreType.DMA((5,)),
        ],
        28,
        "near_projection",
    )
    rows = token_count // 2
    normed_shape = jax.ShapeDtypeStruct((token_count, group_width), jnp.bfloat16)

    def part_shape(part_columns):
        return jax.ShapeDtypeStruct((rows, part_columns), jnp.bfloat16)

    first_columns = columns // 2
    away, stay, far_normed = project(
        far_kernel,
        gain,
        far_weight,
        pltpu.VMEM,
        [near_partial] + pieces[near:],
        [part_shape(first_columns)] * 2 + [normed_shape],
        [],
        8,
        "far_projection",
    )
    rest_away, rest_stay = project(
        rest_kernel,
        far_normed,
        far_weight,
        pltpu.VMEM,
        [near_partial],
        [part_shape(columns - first_columns)] * 2,
        [],
        8,
        "rest_projection",
    )

    def joined(kept, sent, turn):
        came = lax.ppermute(sent, "tp", [(i, i ^ turn) for i in range(tp_count)])
        return (kept.astype(jnp.float32) + came.astype(jnp.float32)).astype(jnp.bfloat16)

    results = []
    for away, stay in ((away, stay), (rest_away, rest_stay)):
        across = joined(stay, away, 1)
        results.append(joined(across[rows // 2 :], across[: rows // 2], 2))
    return jnp.concatenate(results, axis=1)


def on_mesh(*arrays):
    ctx_count, tp_count = lax.axis_size("ctx"), lax.axis_size("tp")
    groups = arrays[2].shape[1] // STATE
    heads_local = arrays[4].shape[1]
    fits = (
        groups == 2
        and tp_count == 4
        and ctx_count & (ctx_count - 1) == 0
        and heads_local % (2 * ctx_count) == 0
        and heads_local // ctx_count <= 8
        and arrays[0].shape[0] == 2 * STATE
    )
    return (head_split if fits else on_device)(*arrays)


def solution(mesh):
    in_specs = (
        P("ctx", "tp"),
        P("ctx", "tp"),
        P("ctx", "tp"),
        P("ctx", "tp"),
        P("ctx", "tp"),
        P(),
        P(),
        P(None, "tp"),
        P(None, "tp"),
        P(None, "tp"),
        P("tp"),
        P("tp"),
        P("tp"),
        P("tp"),
        P("tp", None),
    )
    out_specs = P(("ctx", "tp"), None)
    return jax.shard_map(
        on_mesh, mesh=mesh, in_specs=in_specs, out_specs=out_specs, check_vma=False
    )
```

```python
import functools

import jax
import jax.numpy as jnp
from jax import lax
from jax.experimental import pallas as pl
from jax.experimental.pallas import tpu as pltpu
from jax.sharding import PartitionSpec as P

HEAD_DIM = 64
STATE = 128
CONV = 4
SPAN = 256
BLK = 64


def shifted_2(value, axis, steps):
    count = lax.axis_size(axis)
    leading, last = (max(0, -steps), min(count, count - steps))
    return lax.ppermute(value, axis, [(source, source + steps) for source in range(leading, last)])


def carried_in(shard, axis, join, neutral):
    place = lax.axis_index(axis)
    gathered = jax.tree.map(
        lambda a, kind: lax.all_gather(a.astype(kind), axis),
        shard,
        jax.tree.map(lambda a: jnp.bfloat16 if a.dtype == jnp.float32 else a.dtype, shard),
    )
    state = jax.tree.map(lambda a, e: jnp.zeros_like(a) + jnp.asarray(e, a.dtype), shard, neutral)

    def one(turn, state):
        return join(
            state,
            jax.tree.map(
                lambda a, own: lax.dynamic_index_in_dim(a, turn, 0, False).astype(own.dtype),
                gathered,
                shard,
            ),
        )

    return lax.fori_loop(0, place, one, state)


def document_index(positions, doc_lengths):
    offsets = jnp.cumsum(doc_lengths) - doc_lengths
    below_start = offsets[None, :] <= positions[:, None]
    documents = jnp.sum(below_start.astype(jnp.int32), axis=1, dtype=jnp.int32) - 1
    openings = jnp.any(offsets[None, :] == positions[:, None], axis=1).astype(jnp.int32)
    return (documents, openings)


def causal_conv(extended, weight, doc_ext):
    tap_count = weight.shape[0]
    row_count = extended.shape[0] - tap_count + 1
    current = doc_ext[tap_count - 1 :]
    accumulated = jnp.zeros((row_count, extended.shape[1]), jnp.float32)
    for tap_index in range(tap_count):
        keep_rows = (doc_ext[tap_index : tap_index + row_count] == current)[:, None]
        shifted = (
            extended[tap_index : tap_index + row_count].astype(jnp.float32) * weight[tap_index]
        )
        accumulated = accumulated + jnp.where(keep_rows, shifted, 0.0)
    return lax.optimization_barrier(jax.nn.silu(accumulated).astype(jnp.bfloat16))


def span_outputs(value_rows, step_rows, key_rows, query_rows, decay_sums, documents):
    row_count = value_rows.shape[0]
    per_group = value_rows.shape[1] // key_rows.shape[1]
    row_ids = jnp.arange(row_count, dtype=jnp.int32)
    keep_mask = (documents[:, None] == documents[None, :]) & (row_ids[None, :] <= row_ids[:, None])
    differences = decay_sums[:, :, None] - decay_sums[:, None, :]
    decays = jnp.where(keep_mask[None], jnp.exp(jnp.minimum(differences, 0.0)), 0.0)
    inner_products = jnp.einsum(
        "ign,jgn->gij", query_rows, key_rows, preferred_element_type=jnp.float32
    )
    weighted = (
        decays * jnp.repeat(inner_products, per_group, axis=0) * step_rows.T[:, None, :]
    ).astype(jnp.bfloat16)
    return jnp.einsum("hij,jhp->ihp", weighted, value_rows, preferred_element_type=jnp.float32)


def span_states(value_rows, step_rows, key_rows, decay_sums, documents, openings):
    per_group = value_rows.shape[1] // key_rows.shape[1]
    tail_decay = jnp.where(
        (documents == documents[-1])[None, :], jnp.exp(decay_sums[:, -1:] - decay_sums), 0.0
    )
    tail_weight = tail_decay.T * step_rows
    head_keys = jnp.repeat(key_rows, per_group, axis=1)
    tail_keys = (tail_weight[:, :, None] * head_keys.astype(jnp.float32)).astype(jnp.bfloat16)
    local_state = jnp.einsum(
        "jhp,jhn->hpn", value_rows, tail_keys, preferred_element_type=jnp.float32
    )
    opened = jnp.cumsum(openings)
    span_gate = jnp.where(opened[-1] == 0, jnp.exp(decay_sums[:, -1]), 0.0)
    inflow = jnp.where((opened == 0)[None, :], jnp.exp(decay_sums), 0.0)
    return (local_state, span_gate, inflow)


def span_inflow(query_rows, entering, inflow):
    per_group = entering.shape[0] // query_rows.shape[1]
    head_queries = jnp.repeat(query_rows.astype(jnp.float32), per_group, axis=1)
    carried = jnp.einsum("ihn,hpn->ihp", head_queries, entering, precision=lax.Precision.HIGHEST)
    return carried * inflow.T[:, :, None]


def gated_norm(mixed_rows, gate_rows, norm_gain, groups_local):
    gated_rows = mixed_rows * jax.nn.silu(gate_rows.astype(jnp.float32))
    grouped = gated_rows.reshape(gated_rows.shape[0], groups_local, -1)
    inverse_rms = lax.rsqrt(jnp.mean(grouped * grouped, axis=2, keepdims=True) + 1e-05)
    return ((grouped * inverse_rms).reshape(gated_rows.shape) * norm_gain).astype(jnp.bfloat16)


def on_device(
    values_in,
    gate_in,
    keys_in,
    queries_in,
    step_in,
    block_order,
    doc_lengths,
    conv_values,
    conv_keys,
    conv_queries,
    decay_log,
    step_bias,
    skip_gain,
    norm_gain,
    out_weight,
):
    ctx_count = lax.axis_size("ctx")
    ctx_index = lax.axis_index("ctx")
    token_count = values_in.shape[0]
    per_dev = token_count // BLK
    capacity = (per_dev + ctx_count - 1) // ctx_count
    rim_rows = CONV - 1
    pos_table = block_order.reshape(ctx_count, per_dev)
    owner_of = pos_table // per_dev
    local_ids = jnp.arange(per_dev, dtype=jnp.int32)
    earlier = local_ids[None, :] < local_ids[:, None]
    same_owner = owner_of[:, :, None] == owner_of[:, None, :]
    slot_rank = jnp.sum((same_owner & earlier[None]).astype(jnp.int32), axis=2, dtype=jnp.int32)
    my_owner = lax.dynamic_index_in_dim(owner_of, ctx_index, 0, keepdims=False)
    my_rank = lax.dynamic_index_in_dim(slot_rank, ctx_index, 0, keepdims=False)
    slot_ids = jnp.arange(ctx_count * capacity, dtype=jnp.int32)
    slot_hit = (my_owner * capacity + my_rank)[None, :] == slot_ids[:, None]
    source = jnp.sum(jnp.where(slot_hit, local_ids[None, :], 0), axis=1, dtype=jnp.int32)
    filled = jnp.any(slot_hit, axis=1)

    def pack_slots(local_rows):
        blocks = local_rows.reshape(per_dev, BLK, local_rows.shape[1])
        picked = jnp.where(filled[:, None, None], blocks[source], jnp.zeros((), local_rows.dtype))
        return picked

    all_slots = (jnp.arange(ctx_count, dtype=jnp.int32)[:, None] * capacity + slot_rank).reshape(-1)
    wanted = ctx_index * per_dev + local_ids
    owner_hit = block_order[None, :] == wanted[:, None]
    pick_slot = jnp.sum(jnp.where(owner_hit, all_slots[None, :], 0), axis=1, dtype=jnp.int32)

    def unpack_slots(received):
        return received[pick_slot].reshape(token_count, received.shape[2])

    packed_values = pack_slots(values_in)
    packed_gates = pack_slots(gate_in)
    packed_keys = pack_slots(keys_in)
    packed_queries = pack_slots(queries_in)
    packed_steps = pack_slots(step_in)
    received = (
        lax.all_to_all(packed_values, "ctx", split_axis=0, concat_axis=0, tiled=True),
        lax.all_to_all(packed_gates, "ctx", split_axis=0, concat_axis=0, tiled=True),
        lax.all_to_all(packed_keys, "ctx", split_axis=0, concat_axis=0, tiled=True),
        lax.all_to_all(packed_queries, "ctx", split_axis=0, concat_axis=0, tiled=True),
        lax.all_to_all(packed_steps, "ctx", split_axis=0, concat_axis=0, tiled=True),
    )
    own_values = unpack_slots(received[0])
    own_gates = unpack_slots(received[1])
    own_keys = unpack_slots(received[2])
    own_queries = unpack_slots(received[3])
    own_steps = unpack_slots(received[4])
    rim_values, rim_keys, rim_queries = shifted_2(
        (
            own_values[token_count - rim_rows :],
            own_keys[token_count - rim_rows :],
            own_queries[token_count - rim_rows :],
        ),
        "ctx",
        1,
    )
    positions = (
        ctx_index * token_count - rim_rows + jnp.arange(token_count + rim_rows, dtype=jnp.int32)
    )
    doc_ext, open_ext = document_index(positions, doc_lengths)
    documents = doc_ext[rim_rows:]
    openings = open_ext[rim_rows:]
    conv_value = causal_conv(
        jnp.concatenate([rim_values, own_values], axis=0), conv_values, doc_ext
    )
    conv_key = causal_conv(jnp.concatenate([rim_keys, own_keys], axis=0), conv_keys, doc_ext)
    conv_query = causal_conv(
        jnp.concatenate([rim_queries, own_queries], axis=0), conv_queries, doc_ext
    )
    heads_local = own_steps.shape[1]
    groups_local = own_keys.shape[1] // STATE
    span_count = token_count // SPAN
    step_size = jax.nn.softplus(own_steps.astype(jnp.float32) + step_bias)
    rates = -jnp.exp(decay_log) * step_size
    value_rows = conv_value.reshape(span_count, SPAN, heads_local, HEAD_DIM)
    key_rows = conv_key.reshape(span_count, SPAN, groups_local, STATE)
    query_rows = conv_query.reshape(span_count, SPAN, groups_local, STATE)
    step_spans = step_size.reshape(span_count, SPAN, heads_local)
    decay_sums = jnp.cumsum(rates.reshape(span_count, SPAN, heads_local).transpose(0, 2, 1), axis=2)
    span_docs = documents.reshape(span_count, SPAN)
    span_openings = openings.reshape(span_count, SPAN)
    intra = jax.vmap(span_outputs)(
        value_rows, step_spans, key_rows, query_rows, decay_sums, span_docs
    )
    local_states, span_gates, inflows = jax.vmap(span_states)(
        value_rows, step_spans, key_rows, decay_sums, span_docs, span_openings
    )

    def advance(running, inputs):
        decay_product, accumulated = running
        span_state, span_gate = inputs
        advanced = (span_gate * decay_product, span_gate[:, None, None] * accumulated + span_state)
        return (advanced, running)

    start_carry = (
        jnp.ones((heads_local,), jnp.float32),
        jnp.zeros((heads_local, HEAD_DIM, STATE), jnp.float32),
    )
    summary, prefixes = lax.scan(advance, start_carry, (local_states, span_gates))

    def combine(earlier_part, later_part):
        return (
            earlier_part[0] * later_part[0],
            later_part[0][:, None, None] * earlier_part[1] + later_part[1],
        )

    incoming = carried_in(summary, "ctx", combine, start_carry)
    entering = prefixes[0][:, :, None, None] * incoming[1][None] + prefixes[1]
    entering, inflows = (entering, inflows)
    inter = jax.vmap(span_inflow)(query_rows, entering, inflows)
    mixed_rows = intra + inter + skip_gain[None, None, :, None] * value_rows.astype(jnp.float32)
    mixed_rows = mixed_rows.reshape(token_count, heads_local * HEAD_DIM)
    normed = gated_norm(mixed_rows, own_gates, norm_gain, groups_local)
    return lax.psum_scatter(
        jnp.dot(normed, out_weight, preferred_element_type=jnp.float32).astype(jnp.bfloat16),
        "tp",
        scatter_dimension=0,
        tiled=True,
    )


CHUNK = 128
LANES = 128


def tapped(current, previous, taps, since):
    row_count = current.shape[0]
    extended = jnp.concatenate([previous, current], axis=0)
    total = None
    for tap_index in range(CONV):
        steps = CONV - 1 - tap_index
        weight = taps[tap_index : tap_index + 1, :]
        if steps == 0:
            term = current * weight
        else:
            shifted = pltpu.roll(extended, steps, 0)[8 : 8 + row_count]
            term = jnp.where(since >= steps, shifted * weight, 0.0)
        total = term if total is None else total + term
    return silu(total)


def silu(x):
    half = 0.5 * x
    return half + half * jnp.tanh(half)


def mixing_kernel(
    heads,
    group_heads,
    per_dev,
    chunks_step,
    piece_count,
    me_ref,
    order_ref,
    lengths_ref,
    bias_ref,
    log_ref,
    key_taps_ref,
    query_taps_ref,
    *refs,
):
    piece_refs, refs = refs[:piece_count], refs[piece_count:]
    mix_ref, query_ref, key_ref, tail_ref, inflow_ref, gate_ref, since_ref = refs[:7]
    sequence, previous, raw_steps, step_rows, row_stack = refs[7:]
    groups = piece_refs[0].shape[0]
    me = me_ref[0]
    step_id = pl.program_id(0)
    token_rows = per_dev * BLK
    chunks = raw_steps.shape[0]

    @pl.when(step_id == 0)
    def _():
        previous[...] = jnp.zeros_like(previous)
        lane = lax.broadcasted_iota(jnp.int32, (8, LANES), 1)
        row8 = lax.broadcasted_iota(jnp.int32, (8, LANES), 0)
        own = lax.rem(me * heads, group_heads)
        for g in range(groups):
            for turn, piece_ref in enumerate(piece_refs):
                loader = jnp.bitwise_xor(me, g * piece_count + turn)
                for b in range(per_dev):
                    place = order_ref[loader * per_dev + b]
                    rows = pl.ds(pl.multiple_of(place * BLK, BLK), BLK)
                    sequence[rows, :] = piece_ref[g, b * BLK : (b + 1) * BLK, :]
                    at = (b // 2) * LANES
                    steps_in = piece_ref[
                        g, token_rows : token_rows + group_heads, at : at + LANES
                    ].astype(jnp.float32)
                    parity = lax.rem(place, 2)
                    steps_in = pltpu.roll(
                        steps_in, lax.rem(group_heads - own, group_heads), 0
                    )[:8]
                    steps_in = pltpu.roll(steps_in, BLK * jnp.bitwise_xor(parity, b % 2), 1)
                    chunk = lax.div(place, 2)
                    raw_steps[chunk] = jnp.where(
                        lane // BLK == parity, steps_in, raw_steps[chunk]
                    )
        bias = jnp.zeros((8, LANES), jnp.float32)
        decay = jnp.zeros((8, LANES), jnp.float32)
        for h in range(heads):
            bias = jnp.where(row8 == h, bias_ref[me * heads + h], bias)
            decay = jnp.where(row8 == h, log_ref[me * heads + h], decay)
        decay = -jnp.exp(decay)
        raw = jnp.where(row8[None] < heads, raw_steps[...] + bias[None], 0.0)
        step = jnp.maximum(raw, 0.0) + jnp.log(1.0 + jnp.exp(-jnp.abs(raw)))
        step_rows[...] = step
        sums = decay[None] * step
        lanes = lax.broadcasted_iota(jnp.int32, (chunks, 8, LANES), 2)
        width = 1
        while width < CHUNK:
            sums = sums + jnp.where(lanes >= width, pltpu.roll(sums, width, 2), 0.0)
            width *= 2
        first = lax.broadcasted_iota(jnp.int32, (chunks, 8, LANES), 0) * CHUNK
        position = first + lanes
        begun = jnp.zeros_like(position)
        offset = jnp.int32(0)
        for k in range(lengths_ref.shape[0]):
            begun = jnp.where(position >= offset, offset, begun)
            offset = offset + lengths_ref[k]
        last_sum = jnp.sum(jnp.where(lanes == CHUNK - 1, sums, 0.0), axis=2, keepdims=True)
        last_begun = jnp.max(begun, axis=2, keepdims=True)
        row_stack[:, 0:8] = sums
        row_stack[:, 8:16] = jnp.where(
            position >= last_begun, jnp.exp(last_sum - sums) * step, 0.0
        )
        row_stack[:, 16:24] = jnp.where(begun < first, jnp.exp(sums), 0.0)
        row_stack[:, 24:32] = (position - begun).astype(jnp.float32)
        row_stack[:, 32:40] = jnp.where(
            last_begun < first, jnp.exp(last_sum), jnp.zeros_like(sums)
        )

    causal = lax.broadcasted_iota(jnp.int32, (CHUNK, CHUNK), 0) >= lax.broadcasted_iota(
        jnp.int32, (CHUNK, CHUNK), 1
    )
    column = lax.broadcasted_iota(jnp.int32, (CHUNK, CHUNK), 1).astype(jnp.float32)
    row_of = lax.broadcasted_iota(jnp.int32, (CHUNK, CHUNK), 0).astype(jnp.float32)
    low_half = lax.broadcasted_iota(jnp.int32, (CHUNK, LANES), 1) < HEAD_DIM
    taps = jnp.concatenate([key_taps_ref[...], query_taps_ref[...]], axis=1)

    def one_chunk(local, carry):
        chunk = step_id * chunks_step + local
        turned = jnp.concatenate(
            [row_stack[chunk, :32], jnp.zeros((CHUNK - 32, LANES), jnp.float32)], axis=0
        ).T

        def spread(at):
            return jnp.broadcast_to(turned[:, at : at + 1], (CHUNK, LANES))

        since_rows = spread(24)
        since_ref[local] = since_rows
        rows = pl.ds(pl.multiple_of(chunk * CHUNK, CHUNK), CHUNK)
        current = sequence[rows, :].astype(jnp.float32)
        wide_since = jnp.concatenate([since_rows, since_rows], axis=1)
        conv = tapped(current, previous[...], taps, wide_since)
        previous[...] = current[CHUNK - 8 :]
        keys, queries = conv[:, :STATE].astype(jnp.bfloat16), conv[:, STATE:].astype(jnp.bfloat16)
        query_ref[local] = queries
        key_ref[local] = conv[:, :STATE].T.astype(jnp.bfloat16)
        inner_products = lax.dot_general(
            queries, keys, (((1,), (1,)), ((), ())), preferred_element_type=jnp.float32
        )
        allowed = jnp.where(causal & (column >= row_of - since_rows), 0.0, -1e30)
        for h in range(heads):
            exponent = (spread(h) + allowed) - row_stack[chunk, h : h + 1, :]
            weights = jnp.exp(exponent) * (inner_products * step_rows[chunk, h : h + 1, :])
            mix_ref[local, :, h * CHUNK : (h + 1) * CHUNK] = weights.astype(jnp.bfloat16)
        gate = row_stack[chunk, 32:40]
        for pair in range(heads // 2):
            at = slice(pair * LANES, (pair + 1) * LANES)
            tail_ref[local, :, at] = jnp.where(
                low_half, spread(8 + 2 * pair), spread(9 + 2 * pair)
            )
            inflow_ref[local, :, at] = jnp.where(
                low_half, spread(16 + 2 * pair), spread(17 + 2 * pair)
            )
            gate_ref[local, :, at] = jnp.where(
                low_half[:8],
                jnp.broadcast_to(gate[2 * pair : 2 * pair + 1], (8, LANES)),
                jnp.broadcast_to(gate[2 * pair + 1 : 2 * pair + 2], (8, LANES)),
            )
        return carry

    lax.fori_loop(0, chunks_step, one_chunk, 0, unroll=2)


def scan_kernel(heads, per_dev, turns, place_ref, order_ref, skip_ref, taps_ref, *refs):
    piece_refs, refs = refs[: len(turns)], refs[len(turns) :]
    mix_ref, query_ref, key_ref, tail_ref, inflow_ref, gate_ref, since_ref = refs[:7]
    out_refs, (sequence, gates, laid, previous, state) = refs[7:-5], refs[-5:]
    me, mine = place_ref[0], place_ref[1]
    previous[...] = jnp.zeros_like(previous)
    state[...] = jnp.zeros_like(state)
    for turn, piece_ref in zip(turns, piece_refs):
        loader = jnp.bitwise_xor(me, turn)
        for b in range(per_dev):
            place = order_ref[loader * per_dev + b]
            rows = pl.ds(pl.multiple_of(place * BLK, BLK), BLK)
            sequence[rows, :] = piece_ref[0, b * BLK : (b + 1) * BLK, :]
            gates[rows, :] = piece_ref[1, b * BLK : (b + 1) * BLK, :]
    width = heads * HEAD_DIM
    lane = lax.broadcasted_iota(jnp.int32, (1, width), 1)
    skip = jnp.zeros((1, width), jnp.float32)
    for h in range(heads):
        skip = jnp.where(lane >= h * HEAD_DIM, skip_ref[me * heads + h], skip)
    low_half = lax.broadcasted_iota(jnp.int32, (CHUNK, LANES), 1) < HEAD_DIM
    taps = taps_ref[...]
    blocks = CHUNK // BLK

    def one_chunk(chunk, carry):
        rows = pl.ds(pl.multiple_of(chunk * CHUNK, CHUNK), CHUNK)
        current = sequence[rows, :].astype(jnp.float32)
        wide_since = jnp.concatenate([since_ref[chunk]] * (width // LANES), axis=1)
        values = tapped(current, previous[...], taps, wide_since).astype(jnp.bfloat16)
        previous[...] = current[CHUNK - 8 :]
        values_wide = values.astype(jnp.float32)
        entering = state[...]
        carried = jnp.dot(
            query_ref[chunk], entering.astype(jnp.bfloat16), preferred_element_type=jnp.float32
        )
        total = carried * inflow_ref[chunk] + skip * values_wide
        tail_values = (values_wide * tail_ref[chunk]).astype(jnp.bfloat16)
        state[...] = gate_ref[chunk, :1, :] * entering + jnp.dot(
            key_ref[chunk], tail_values, preferred_element_type=jnp.float32
        )
        zero = jnp.zeros((CHUNK, LANES), jnp.bfloat16)
        intra = []
        for pair in range(heads // 2):
            both = values[:, pair * LANES : (pair + 1) * LANES]
            block = jnp.concatenate(
                [jnp.where(low_half, both, zero), jnp.where(low_half, zero, both)], axis=0
            )
            weights = mix_ref[chunk, :, 2 * pair * CHUNK : 2 * (pair + 1) * CHUNK]
            intra.append(jnp.dot(weights, block, preferred_element_type=jnp.float32))
        mixed = total + jnp.concatenate(intra, axis=1)
        gated = (mixed * silu(gates[rows, :].astype(jnp.float32))).astype(jnp.bfloat16)
        for block in range(blocks):
            place = chunk * blocks + block
            away = jnp.bitwise_xor(lax.rem(place, per_dev), mine)
            slot = 2 * (1 - lax.rem(away, 2)) + (1 - lax.div(away, 2))
            start = pl.multiple_of(slot * BLK, BLK)
            laid[lax.div(place, per_dev), pl.ds(start, BLK), :] = gated[
                block * BLK : (block + 1) * BLK
            ]
        return carry

    lax.fori_loop(0, mix_ref.shape[0], one_chunk, 0, unroll=4)
    for turn, out_ref in zip(turns, out_refs):
        out_ref[...] = laid[jnp.bitwise_xor(me, turn)]


def squares_of(pieces):
    squares = pieces[0] * pieces[0]
    for piece in pieces[1:]:
        squares = squares + piece * piece
    return jnp.sum(squares, axis=1, keepdims=True)


def weight_tiles(weight_ref, group, buffer, sems, count):
    tile = buffer.shape[1] // count
    tiles = [slice(i * tile, (i + 1) * tile) for i in range(count)]
    return tiles, [
        pltpu.make_async_copy(weight_ref.at[group, :, at], buffer.at[:, at], sems.at[i])
        for i, at in enumerate(tiles)
    ]


def near_kernel(place_ref, gain_ref, weight_ref, *refs):
    gated_refs, refs = refs[:-6], refs[-6:]
    partial_ref, squares_ref, next_ref, gained, buffer, sems = refs
    me = place_ref[0]
    near = len(gated_refs) + 1
    width = gated_refs[0].shape[1]
    depth = near * width
    count = sems.shape[0] - 2
    group = lax.div(me, near)
    last = pl.multiple_of(lax.rem(jnp.bitwise_xor(me, near - 1), near) * width, width)
    tiles, copies = weight_tiles(weight_ref, group, buffer, sems, count)
    onward = [
        pltpu.make_async_copy(weight_ref.at[1 - group], next_ref.at[:depth], sems.at[count]),
        pltpu.make_async_copy(
            weight_ref.at[group, pl.ds(last, width)], next_ref.at[depth:], sems.at[count + 1]
        ),
    ]
    for copy in copies + onward:
        copy.start()
    wide = [ref[...].astype(jnp.float32) for ref in gated_refs]
    squares_ref[...] = jnp.broadcast_to(squares_of(wide), squares_ref.shape)
    for turn, piece in enumerate(wide):
        source = jnp.bitwise_xor(me, turn)
        at = pl.multiple_of(lax.rem(source, near) * width, width)
        gained[:, pl.ds(at, width)] = (piece * gain_ref[pl.ds(source, 1), :]).astype(jnp.bfloat16)
    gained[:, pl.ds(last, width)] = jnp.zeros((gained.shape[0], width), jnp.bfloat16)
    for at, copy in zip(tiles, copies):
        copy.wait()
        partial_ref[:, at] = jnp.dot(
            gained[...], buffer[:, at], preferred_element_type=jnp.float32
        )
    for copy in onward:
        copy.wait()


def project_far(normed, scale, weight_ref, near_ref, at, away_ref, stay_ref):
    wide_scale = jnp.concatenate([scale] * (away_ref.shape[1] // LANES), axis=1)
    partial = near_ref[:, at] * wide_scale + jnp.dot(
        normed, weight_ref[:, at], preferred_element_type=jnp.float32
    )
    partial = partial.astype(jnp.bfloat16)
    rows = partial.shape[0] // 2
    away_ref[...] = partial[:rows]
    stay_ref[...] = partial[rows:]


def far_kernel(place_ref, gain_ref, weight_ref, near_ref, squares_ref, *refs):
    gated_refs, (away_ref, stay_ref, normed, scale_ref) = refs[:-4], refs[-4:]
    me = place_ref[0]
    near = len(gated_refs) - 1
    rows, width = gated_refs[0].shape
    share = 1.0 / (near * width)
    wide = [ref[...].astype(jnp.float32) for ref in gated_refs]
    far_scale = lax.rsqrt(squares_of(wide[:near]) * share + 1e-05)
    for turn, piece in enumerate(wide[:near]):
        source = jnp.bitwise_xor(me, near + turn)
        at = pl.multiple_of(lax.rem(source, near) * width, width)
        gain = gain_ref[pl.ds(source, 1), :]
        normed[:, pl.ds(at, width)] = (piece * far_scale * gain).astype(jnp.bfloat16)
    near_scale = lax.rsqrt((squares_ref[:, :1] + squares_of(wide[near:])) * share + 1e-05)
    gain = gain_ref[pl.ds(jnp.bitwise_xor(me, near - 1), 1), :]
    normed[:, near * width :] = (wide[near] * near_scale * gain).astype(jnp.bfloat16)
    scale = jnp.broadcast_to(near_scale, scale_ref.shape)
    scale_ref[...] = scale
    at = slice(0, away_ref.shape[1])
    project_far(normed[...], scale, weight_ref, near_ref, at, away_ref, stay_ref)


def rest_kernel(place_ref, normed_ref, weight_ref, near_ref, scale_ref, away_ref, stay_ref):
    at = slice(near_ref.shape[1] - away_ref.shape[1], near_ref.shape[1])
    project_far(normed_ref[...], scale_ref[...], weight_ref, near_ref, at, away_ref, stay_ref)


def head_split(
    values_in,
    gate_in,
    keys_in,
    queries_in,
    step_in,
    block_order,
    doc_lengths,
    conv_values,
    conv_keys,
    conv_queries,
    decay_log,
    step_bias,
    skip_gain,
    norm_gain,
    out_weight,
):
    ctx_count = lax.axis_size("ctx")
    tp_count = lax.axis_size("tp")
    me = lax.axis_index("ctx")
    tp_index = lax.axis_index("tp")
    token_count, channels = values_in.shape
    per_dev = token_count // BLK
    total_tokens = token_count * ctx_count
    heads_local = step_in.shape[1]
    heads = heads_local // ctx_count
    width = heads * HEAD_DIM
    groups = keys_in.shape[1] // STATE
    group_heads = heads_local // groups
    near = ctx_count // groups
    chunks = total_tokens // CHUNK
    my_group = me // near
    place = jnp.stack([me, tp_index]).astype(jnp.int32)

    def turned(value, turn):
        return lax.ppermute(value, "ctx", [(i, i ^ turn) for i in range(ctx_count)])

    def for_group(group):
        keys = lax.dynamic_slice_in_dim(keys_in, group * STATE, STATE, 1)
        queries = lax.dynamic_slice_in_dim(queries_in, group * STATE, STATE, 1)
        steps = lax.dynamic_slice_in_dim(step_in, group * group_heads, group_heads, 1)
        return jnp.concatenate([jnp.concatenate([keys, queries], axis=1), steps.T], axis=0)

    def for_heads(turn):
        at = (me ^ turn) * width
        return jnp.stack(
            [lax.dynamic_slice_in_dim(rows, at, width, 1) for rows in (values_in, gate_in)]
        )

    held = jnp.stack([for_group(my_group), turned(for_group(my_group ^ 1), near)])
    group_rows = [held] + [turned(held, turn) for turn in range(1, near)]
    turns = (0, 1, 4, 7, 3, 2, 5, 6)
    head_rows = [turned(for_heads(turn), turn) if turn else for_heads(turn) for turn in turns]

    key_taps = lax.dynamic_slice_in_dim(conv_keys, my_group * STATE, STATE, 1)
    query_taps = lax.dynamic_slice_in_dim(conv_queries, my_group * STATE, STATE, 1)
    value_taps = lax.dynamic_slice_in_dim(conv_values, me * width, width, 1)

    smem = pl.BlockSpec(memory_space=pltpu.SMEM)
    vmem = pl.BlockSpec(memory_space=pltpu.VMEM)
    params = pltpu.CompilerParams(vmem_limit_bytes=28 * 1024 * 1024)

    def whole(array):
        return pl.BlockSpec(array.shape, lambda *ids: (0,) * array.ndim)

    grid_steps = 4
    chunks_step = chunks // grid_steps

    def per_step(rows, columns):
        return pl.BlockSpec((chunks_step, rows, columns), lambda i: (i, 0, 0))

    mix_shapes = [
        ((CHUNK, heads * CHUNK), jnp.bfloat16),
        ((CHUNK, STATE), jnp.bfloat16),
        ((STATE, CHUNK), jnp.bfloat16),
        ((CHUNK, width), jnp.float32),
        ((CHUNK, width), jnp.float32),
        ((8, width), jnp.float32),
        ((CHUNK, LANES), jnp.float32),
    ]
    mixing = pl.pallas_call(
        functools.partial(mixing_kernel, heads, group_heads, per_dev, chunks_step, near),
        grid=(grid_steps,),
        in_specs=[smem] * 5 + [whole(key_taps), whole(query_taps)] + [whole(held)] * near,
        out_specs=[per_step(*shape) for shape, _ in mix_shapes],
        out_shape=[jax.ShapeDtypeStruct((chunks,) + shape, kind) for shape, kind in mix_shapes],
        scratch_shapes=[
            pltpu.VMEM((total_tokens, 2 * STATE), jnp.bfloat16),
            pltpu.VMEM((8, 2 * STATE), jnp.float32),
            pltpu.VMEM((chunks, 8, LANES), jnp.float32),
            pltpu.VMEM((chunks, 8, LANES), jnp.float32),
            pltpu.VMEM((chunks, 40, LANES), jnp.float32),
        ],
        compiler_params=params,
        cost_estimate=pl.CostEstimate(
            flops=20_000_000, bytes_accessed=20_000_000, transcendentals=2_000_000
        ),
        name="mixing",
    )(place, block_order, doc_lengths, step_bias, decay_log, key_taps, query_taps, *group_rows)

    gated = pl.pallas_call(
        functools.partial(scan_kernel, heads, per_dev, turns),
        in_specs=[smem] * 3 + [vmem] * (1 + ctx_count + len(mix_shapes)),
        out_specs=[vmem] * ctx_count,
        out_shape=[jax.ShapeDtypeStruct((token_count, width), jnp.bfloat16)] * ctx_count,
        scratch_shapes=[
            pltpu.VMEM((total_tokens, width), jnp.bfloat16),
            pltpu.VMEM((total_tokens, width), jnp.bfloat16),
            pltpu.VMEM((ctx_count, token_count, width), jnp.bfloat16),
            pltpu.VMEM((8, width), jnp.float32),
            pltpu.VMEM((STATE, width), jnp.float32),
        ],
        compiler_params=params,
        cost_estimate=pl.CostEstimate(
            flops=600_000_000, bytes_accessed=14_000_000, transcendentals=1_200_000
        ),
        name="scan",
    )(place, block_order, skip_gain, value_taps, *head_rows, *mixing)
    gated = dict(zip(turns, gated))

    pieces = [gated[0]] + [turned(gated[turn], turn) for turn in range(1, ctx_count)]

    columns = out_weight.shape[1]
    group_width = near * width
    gain = norm_gain.reshape(ctx_count, width)
    weight = out_weight.reshape(groups, group_width, columns)

    def project(kernel, first, weight, weight_space, operands, out_shape, scratch, limit, name):
        return pl.pallas_call(
            kernel,
            in_specs=[smem, vmem, pl.BlockSpec(memory_space=weight_space)] + [vmem] * len(operands),
            out_specs=[vmem] * len(out_shape),
            out_shape=out_shape,
            scratch_shapes=scratch,
            compiler_params=pltpu.CompilerParams(vmem_limit_bytes=limit * 1024 * 1024),
            cost_estimate=pl.CostEstimate(
                flops=2 * token_count * group_width * columns,
                bytes_accessed=2 * group_width * columns,
                transcendentals=0,
            ),
            name=name,
        )(place, first, weight, *operands)

    far_width = group_width + width
    row_shape = jax.ShapeDtypeStruct((token_count, LANES), jnp.float32)
    near_partial, near_squares, far_weight = project(
        near_kernel,
        gain,
        weight,
        pl.ANY,
        pieces[: near - 1],
        [
            jax.ShapeDtypeStruct((token_count, columns), jnp.float32),
            row_shape,
            jax.ShapeDtypeStruct((far_width, columns), jnp.bfloat16),
        ],
        [
            pltpu.VMEM((token_count, group_width), jnp.bfloat16),
            pltpu.VMEM((group_width, columns), jnp.bfloat16),
            pltpu.SemaphoreType.DMA((6,)),
        ],
        28,
        "near_projection",
    )
    rows = token_count // 2
    normed_shape = jax.ShapeDtypeStruct((token_count, far_width), jnp.bfloat16)

    def part_shape(part_columns):
        return jax.ShapeDtypeStruct((rows, part_columns), jnp.bfloat16)

    first_columns = columns // 2
    away, stay, far_normed, near_scale = project(
        far_kernel,
        gain,
        far_weight,
        pltpu.VMEM,
        [near_partial, near_squares] + pieces[near:] + pieces[near - 1 : near],
        [part_shape(first_columns)] * 2 + [normed_shape, row_shape],
        [],
        8,
        "far_projection",
    )
    rest_away, rest_stay = project(
        rest_kernel,
        far_normed,
        far_weight,
        pltpu.VMEM,
        [near_partial, near_scale],
        [part_shape(columns - first_columns)] * 2,
        [],
        8,
        "rest_projection",
    )

    def joined(kept, sent, turn):
        came = lax.ppermute(sent, "tp", [(i, i ^ turn) for i in range(tp_count)])
        return (kept.astype(jnp.float32) + came.astype(jnp.float32)).astype(jnp.bfloat16)

    results = []
    for away, stay in ((away, stay), (rest_away, rest_stay)):
        across = joined(stay, away, 1)
        results.append(joined(across[rows // 2 :], across[: rows // 2], 2))
    return jnp.concatenate(results, axis=1)


def on_mesh(*arrays):
    ctx_count, tp_count = lax.axis_size("ctx"), lax.axis_size("tp")
    groups = arrays[2].shape[1] // STATE
    heads_local = arrays[4].shape[1]
    fits = (
        groups == 2
        and tp_count == 4
        and ctx_count & (ctx_count - 1) == 0
        and heads_local % (2 * ctx_count) == 0
        and heads_local // ctx_count <= 8
        and arrays[0].shape[0] == 2 * STATE
    )
    return (head_split if fits else on_device)(*arrays)


def solution(mesh):
    in_specs = (
        P("ctx", "tp"),
        P("ctx", "tp"),
        P("ctx", "tp"),
        P("ctx", "tp"),
        P("ctx", "tp"),
        P(),
        P(),
        P(None, "tp"),
        P(None, "tp"),
        P(None, "tp"),
        P("tp"),
        P("tp"),
        P("tp"),
        P("tp"),
        P("tp", None),
    )
    out_specs = P(("ctx", "tp"), None)
    return jax.shard_map(
        on_mesh, mesh=mesh, in_specs=in_specs, out_specs=out_specs, check_vma=False
    )
```
